256 devices in a mesh: blk: 64 (over y_lo, x, z), grid: 4 (over y_hi, core).
Axes of the slice: x: 4, y: 4 (y_hi: 2, y_lo: 2; y = y_hi * 2 + y_lo), z: 8, core: 2. Of those that a mesh axis runs over, the one named last changes fastest.
Arguments:
- patches: bfloat16 [4, 8192, 1024], P('grid', 'blk'), may hold values from -6 to 6
- stem_weight: bfloat16 [2, 1024, 768], replicated, may hold values from -0.125 to 0.125
- norm_gain: bfloat16 [768], replicated, may hold values from 0.25 to 1.75
- w_qkv: bfloat16 [768, 1280], replicated, may hold values from -0.21875 to 0.21875
- w_out: bfloat16 [768, 768], replicated, may hold values from -0.21875 to 0.21875
- per_head_scale: float32 [12], replicated, may hold values from 0.05 to 1, as said below
- positions: int32 [8192], replicated, may hold values from 0 to 8191, each once
- d_out: bfloat16 [4, 8192, 768], P('grid', 'blk'), may hold values from -48 to 48
Outputs:
- d_stem_weight: float32 [2, 1024, 768], P(None, None, ('blk', 'grid'))
- d_norm_gain: float32 [768], P(('blk', 'grid'))
- d_w_qkv: float32 [768, 1280], P(('blk', 'grid'))
- d_w_out: float32 [768, 768], P(None, ('blk', 'grid'))
The draws below stay inside these ranges and needn't reach their ends.
Inputs may be any that keep to these rules, and one draw needn't show every extreme that they name: A permutation of the 8192 positions of a band. `per_head_scale`: positive.
All inputs are finite; a program needn't handle non-finite values.
Results may differ from the reference program's by a relative error of at most 0.015.
The reference program's roundings to bfloat16 on the way count: a program that leaves them out, or rounds other values in their place, can miss the bound.
Values may be sent and summed in bfloat16 or wider, within the bound.
No kernel may reach another device: no remote copies, remote signals or barrier semaphores. Data moves between devices by JAX's collectives and lax.ppermute only.
A program may use at most 128 MiB of HBM per device.

```python
from functools import partial
import jax
import jax.numpy as jnp
from jax import lax

D = 768
QUERY_HEADS = 12
KEY_VALUE_HEADS = 4
HEAD_SIZE = 64
TR = 8
TC = 16
TOK_DEV = 128
BAND_TOKENS = 8192
PIN = 1024
QD = 768
KD = 256
N_BLK = 64
N_GRID = 4


def draw_per_head_scale(key, part):
    lowest, highest = (0.05, 0.4)
    uniform_draw = jax.random.uniform(key, (QUERY_HEADS,), jnp.float32)
    return jnp.exp(jnp.log(lowest) + uniform_draw * (jnp.log(highest) - jnp.log(lowest)))


def draw_d_out(key, part):
    noise_key = jax.random.fold_in(key, 11)
    order_key = jax.random.fold_in(key, 23)
    owners = N_BLK * N_GRID
    noise = jnp.clip(jax.random.normal(noise_key, (N_GRID, BAND_TOKENS, D), jnp.float32), -6.0, 6.0)
    factor = 8.0
    pairing = jax.random.permutation(order_key, owners).astype(jnp.int32)
    band_index = jnp.arange(N_GRID, dtype=jnp.int32)[:, None]
    block_index = (jnp.arange(BAND_TOKENS, dtype=jnp.int32) // TOK_DEV)[None, :]
    owner = block_index * N_GRID + band_index
    target = jnp.take(pairing, owner.reshape(-1)).reshape(N_GRID, BAND_TOKENS, 1)
    column_block = (jnp.arange(D, dtype=jnp.int32) // (D // owners))[None, None, :]
    heavy = jnp.where(target == column_block, factor, 1.0)
    return jnp.clip(noise * heavy, -48.0, 48.0).astype(jnp.bfloat16)


def block_scale(key, extent, cuts, least, high):
    factor_of, own = 1.0, jax.random.fold_in(key, 6)
    for position, blocks in cuts:
        draws = jnp.exp(jax.random.uniform(jax.random.fold_in(own, position), (blocks,), jnp.float32, least / len(cuts), high / len(cuts)))
        factor_of = factor_of * jnp.repeat(draws, extent[position] // blocks).reshape([-1 if axis == position else 1 for axis in range(len(extent))])
    return factor_of


def scatter_about(own_key, extent, deviation, most, cuts=(), kind=jnp.bfloat16):
    result = jax.random.normal(own_key, extent, jnp.float32) * deviation
    if len(cuts) > 0:
        result = block_scale(own_key, extent, cuts, -0.22, 0.18) * result
    return jnp.clip(result, min=-most, max=most).astype(kind)


def setup_inputs(seed: int = 0) -> dict:
    seeds = jax.random.split(jax.random.key(seed), 9)
    patches = scatter_about(seeds[0], (N_GRID, BAND_TOKENS, PIN), 1.0, 6.0, ((0, 4), (1, 64)))
    stem_weight = scatter_about(seeds[1], (2, PIN, D), (2 * PIN) ** -0.5, 0.125)
    norm_gain = jnp.clip(1.0 + 0.15 * jax.random.normal(seeds[2], (D,), jnp.float32), 0.25, 1.75).astype(jnp.bfloat16)
    w_qkv = scatter_about(seeds[3], (D, QD + 2 * KD), D ** -0.5, 0.21875)
    w_out = scatter_about(seeds[4], (QD, D), QD ** -0.5, 0.21875)
    per_head_scale = draw_per_head_scale(jax.random.fold_in(seeds[8], 71), 0)
    positions = jax.random.permutation(seeds[6], BAND_TOKENS).astype(jnp.int32)
    d_out = draw_d_out(jax.random.fold_in(seeds[8], 71), 0)
    return dict(patches=patches, stem_weight=stem_weight, norm_gain=norm_gain, w_qkv=w_qkv, w_out=w_out, per_head_scale=per_head_scale, positions=positions, d_out=d_out)


def lower(values):
    return lax.optimization_barrier(values.astype(jnp.bfloat16))

def row_norm(values):
    return values * lax.rsqrt(lax.optimization_barrier(jnp.mean(values * values, axis=-1, keepdims=True)) + 1e-05)

def head_norm(values):
    return values * lax.rsqrt(lax.optimization_barrier(jnp.mean(values * values, axis=-1, keepdims=True)) + 1e-06)

def window_blocks(array):
    blocks = array.reshape((N_BLK, TOK_DEV) + array.shape[1:])
    return jnp.concatenate([jnp.roll(blocks, offset, axis=0) for offset in range(4)], axis=1)

def attend_block(per_head_scale, inputs):
    query_tile_block, gradient_block, key_band_window, value_band_window, query_pos, key_pos = inputs
    group_factor = QUERY_HEADS // KEY_VALUE_HEADS
    token_row_count = query_tile_block.shape[0]
    every_key = key_band_window.shape[0]
    visible = (key_pos[None, :] <= query_pos[:, None])[None, None]
    query_wide = query_tile_block.astype(jnp.float32).reshape(token_row_count, KEY_VALUE_HEADS, group_factor, HEAD_SIZE)
    gradient_wide = gradient_block.astype(jnp.float32).reshape(token_row_count, KEY_VALUE_HEADS, group_factor, HEAD_SIZE)
    key_wide = key_band_window.astype(jnp.float32).reshape(every_key, KEY_VALUE_HEADS, HEAD_SIZE)
    value_wide = value_band_window.astype(jnp.float32).reshape(every_key, KEY_VALUE_HEADS, HEAD_SIZE)
    score_scale = per_head_scale.astype(jnp.float32).reshape(KEY_VALUE_HEADS, group_factor)[:, :, None, None]
    attention_scores = jnp.einsum('phiv,chv->hipc', query_wide, key_wide) * score_scale
    attention_scores = jnp.where(visible, attention_scores, -1e+30)
    top = lax.optimization_barrier(jnp.max(attention_scores, axis=-1, keepdims=True))
    weights = jnp.where(visible, jnp.exp(attention_scores - top), 0.0)
    probs = weights / lax.optimization_barrier(jnp.sum(weights, axis=-1, keepdims=True))
    probability_narrow = lower(probs).astype(jnp.float32)
    attention_output = jnp.einsum('ychp,pyu->hycu', probability_narrow, value_wide)
    softmax_delta = jnp.einsum('pyui,pyui->yup', gradient_wide, attention_output)
    probability_gradient = jnp.einsum('phiv,chv->hipc', gradient_wide, value_wide)
    score_gradient = lower(score_scale * probs * (probability_gradient - softmax_delta[..., None])).astype(jnp.float32)
    query_gradient = jnp.einsum('ychp,pyu->hycu', score_gradient, key_wide).reshape(token_row_count, QUERY_HEADS * HEAD_SIZE)
    key_gradient = jnp.einsum('lpma,mlpx->alx', score_gradient, query_wide).reshape(every_key, KEY_VALUE_HEADS * HEAD_SIZE)
    value_gradient = jnp.einsum('lpma,mlpx->alx', probability_narrow, gradient_wide).reshape(every_key, KEY_VALUE_HEADS * HEAD_SIZE)
    return (attention_output.reshape(token_row_count, QUERY_HEADS * HEAD_SIZE), query_gradient, jnp.concatenate([key_gradient, value_gradient], axis=1))

def band_terms(patches, below, stem_weight, norm_gain, w_qkv, w_out, per_head_scale, positions, d_out):
    query_span_width = QUERY_HEADS * HEAD_SIZE
    key_span_width = KEY_VALUE_HEADS * HEAD_SIZE
    stem = jnp.dot(patches, stem_weight[0], preferred_element_type=jnp.float32)
    stem = stem + jnp.dot(below, stem_weight[1], preferred_element_type=jnp.float32)
    token_f = lower(stem).astype(jnp.float32)
    gain_f = norm_gain.astype(jnp.float32)
    normed = row_norm(token_f)
    hidden = lower(normed * gain_f)
    query_key_value = jnp.dot(hidden, w_qkv, preferred_element_type=jnp.float32)
    query = query_key_value[:, :query_span_width].reshape(BAND_TOKENS, QUERY_HEADS, HEAD_SIZE)
    key = query_key_value[:, query_span_width:query_span_width + key_span_width].reshape(BAND_TOKENS, KEY_VALUE_HEADS, HEAD_SIZE)
    query_normalized = lower(head_norm(query)).reshape(BAND_TOKENS, query_span_width)
    key_n = lower(head_norm(key)).reshape(BAND_TOKENS, key_span_width)
    value = lower(query_key_value[:, query_span_width + key_span_width:])
    attention_gradient = lower(jnp.dot(d_out, w_out.T, preferred_element_type=jnp.float32))
    attn_f, query_gradient, dkv = lax.map(partial(attend_block, per_head_scale), (query_normalized.reshape(N_BLK, TOK_DEV, query_span_width), attention_gradient.reshape(N_BLK, TOK_DEV, query_span_width), window_blocks(key_n), window_blocks(value), positions.reshape(N_BLK, TOK_DEV), window_blocks(positions)))
    attention_output = lower(attn_f.reshape(BAND_TOKENS, query_span_width))
    key_value_gradient_sum = jnp.zeros((N_BLK, TOK_DEV, 2 * key_span_width), jnp.float32)
    for offset in range(4):
        key_value_gradient_sum = key_value_gradient_sum + jnp.roll(dkv[:, offset * TOK_DEV:(offset + 1) * TOK_DEV], -offset, axis=0)
    key_value_gradient_sum = key_value_gradient_sum.reshape(BAND_TOKENS, 2 * key_span_width)
    pull_query = jax.vjp(head_norm, query)[1]
    gather_key = jax.vjp(head_norm, key)[1]
    dq_full = pull_query(query_gradient.reshape(BAND_TOKENS, QUERY_HEADS, HEAD_SIZE))[0].reshape(BAND_TOKENS, query_span_width)
    key_gradient_whole = gather_key(key_value_gradient_sum[:, :key_span_width].reshape(BAND_TOKENS, KEY_VALUE_HEADS, HEAD_SIZE))[0].reshape(BAND_TOKENS, key_span_width)
    d_qkv = lower(jnp.concatenate([dq_full, key_gradient_whole, key_value_gradient_sum[:, key_span_width:]], axis=1))
    d_w_qkv = jnp.dot(hidden.T, d_qkv, preferred_element_type=jnp.float32)
    d_w_out = jnp.dot(attention_output.T, d_out, preferred_element_type=jnp.float32)
    d_hidden = jnp.dot(d_qkv, w_qkv.T, preferred_element_type=jnp.float32)
    d_gain = lax.optimization_barrier(jnp.sum(d_hidden * normed, axis=0))
    pull_tokens = jax.vjp(row_norm, token_f)[1]
    d_tokens = lower(d_out.astype(jnp.float32) + pull_tokens(d_hidden * gain_f)[0])
    d_stem = jnp.stack([jnp.dot(patches.T, d_tokens, preferred_element_type=jnp.float32), jnp.dot(below.T, d_tokens, preferred_element_type=jnp.float32)])
    return (d_stem, d_gain, d_w_qkv, d_w_out)

def reference(patches, stem_weight, norm_gain, w_qkv, w_out, per_head_scale, positions, d_out):
    image = patches.reshape(N_GRID, N_BLK, TR, TC, PIN).transpose(0, 2, 1, 3, 4).reshape(N_GRID * TR, N_BLK, TC, PIN)
    shifted = jnp.concatenate([image[1:], jnp.zeros_like(image[:1])], axis=0)
    below = shifted.reshape(N_GRID, TR, N_BLK, TC, PIN).transpose(0, 2, 1, 3, 4).reshape(N_GRID, BAND_TOKENS, PIN)
    totals = band_terms(patches[0], below[0], stem_weight, norm_gain, w_qkv, w_out, per_head_scale, positions, d_out[0])
    for band in range(1, N_GRID):
        terms = band_terms(patches[band], below[band], stem_weight, norm_gain, w_qkv, w_out, per_head_scale, positions, d_out[band])
        totals = jax.tree.map(lambda first, second: first + second, totals, terms)
    return (totals[0], totals[1], totals[2], totals[3])
```

```python
import jax
import jax.numpy as jnp
from jax import lax
from jax.sharding import Mesh, PartitionSpec as P

QUERY_HEADS = 12
KEY_VALUE_HEADS = 4
HEAD_SIZE = 64
TC = 16
BLK = ("yl", "x", "z")
BAND = ("yh", "c")
RING = ("yl", "yh", "c")
REST = ("x", "z")


def passed_along(x, by):
    peers = lax.axis_size(BLK)
    return lax.ppermute(x, BLK, [(i, (i + by) % peers) for i in range(peers)])


def row_norm(values):
    return values * lax.rsqrt(jnp.mean(values * values, axis=-1, keepdims=True) + 1e-05)


def head_norm(values):
    return values * lax.rsqrt(jnp.mean(values * values, axis=-1, keepdims=True) + 1e-06)


def one_hot(sources, size):
    rows = lax.broadcasted_iota(jnp.int32, (sources.shape[0], size, sources.shape[1]), 1)
    return (rows == sources[:, None, :]).astype(jnp.bfloat16)


def spread(x, sources):
    pick = one_hot(sources, x.shape[1])
    return jnp.einsum("tc,qcj->qtj", x, pick, preferred_element_type=jnp.float32).astype(
        jnp.bfloat16
    )


def exchange(x, axes):
    return lax.all_to_all(x, axes, split_axis=0, concat_axis=0, tiled=True)


def shards(patches, stem_weight, norm_gain, w_qkv, w_out, per_head_scale, positions, d_out):
    tiles = patches[0]
    grad_out = d_out[0]
    token_rows = tiles.shape[0]
    group_factor = QUERY_HEADS // KEY_VALUE_HEADS
    query_span_width = QUERY_HEADS * HEAD_SIZE
    key_span_width = KEY_VALUE_HEADS * HEAD_SIZE
    bands = lax.axis_size(BAND)
    arrived = lax.ppermute(tiles[:TC], BAND, [(i, i - 1) for i in range(1, bands)])
    dout_ring = lax.all_gather(grad_out, RING, axis=0, tiled=True)
    tiles_ring = lax.all_gather(tiles, RING, axis=0, tiled=True)
    below = jnp.concatenate([tiles[TC:], arrived], axis=0)
    stem = jnp.dot(tiles, stem_weight[0], preferred_element_type=jnp.float32)
    stem = stem + jnp.dot(below, stem_weight[1], preferred_element_type=jnp.float32)
    token_f = lax.optimization_barrier(stem.astype(jnp.bfloat16)).astype(jnp.float32)
    gain_f = norm_gain.astype(jnp.float32)
    normed = row_norm(token_f)
    hidden = (normed * gain_f).astype(jnp.bfloat16)
    hidden_ring = lax.all_gather(hidden, RING, axis=0, tiled=True)
    query_key_value = jnp.dot(hidden, w_qkv, preferred_element_type=jnp.float32)
    query = query_key_value[:, :query_span_width].reshape(token_rows, QUERY_HEADS, HEAD_SIZE)
    key = query_key_value[:, query_span_width : query_span_width + key_span_width].reshape(
        token_rows, KEY_VALUE_HEADS, HEAD_SIZE
    )
    query_normalized = head_norm(query).astype(jnp.bfloat16)
    key_n = head_norm(key).astype(jnp.bfloat16).reshape(token_rows, key_span_width)
    value = query_key_value[:, query_span_width + key_span_width :].astype(jnp.bfloat16)
    kv_own = jnp.concatenate([key_n, value], axis=1)
    blk_count = lax.axis_size(BLK)
    own_index = lax.axis_index(BLK)
    blocks = [kv_own] + [passed_along(kv_own, offset) for offset in range(1, 4)]
    attention_gradient = jnp.dot(grad_out, w_out.T, preferred_element_type=jnp.float32).astype(
        jnp.bfloat16
    )
    causal_window = jnp.concatenate(blocks, axis=0)
    key_pos = jnp.concatenate(
        [
            lax.dynamic_slice_in_dim(
                positions, (own_index - offset) % blk_count * token_rows, token_rows
            )
            for offset in range(4)
        ]
    )
    query_pos = lax.dynamic_slice_in_dim(positions, own_index * token_rows, token_rows)
    visible = (key_pos[None, :] <= query_pos[:, None])[None]
    every_key = causal_window.shape[0]
    query_cube = query_normalized.reshape(token_rows, KEY_VALUE_HEADS, group_factor, HEAD_SIZE)
    gradient_cube = attention_gradient.reshape(token_rows, KEY_VALUE_HEADS, group_factor, HEAD_SIZE)
    key_cube = causal_window[:, :key_span_width].reshape(every_key, KEY_VALUE_HEADS, HEAD_SIZE)
    value_cube = causal_window[:, key_span_width:].reshape(every_key, KEY_VALUE_HEADS, HEAD_SIZE)
    score_scales = per_head_scale.reshape(KEY_VALUE_HEADS, group_factor)
    attn_list = []
    dquery_list = []
    dkey_list = []
    dvalue_list = []
    f32 = jnp.float32
    for group in range(KEY_VALUE_HEADS):
        scale_col = score_scales[group][:, None, None]
        q_group = query_cube[:, group]
        grad_group = gradient_cube[:, group]
        k_group = key_cube[:, group]
        v_group = value_cube[:, group]
        scores = jnp.einsum("trd,sd->rts", q_group, k_group, preferred_element_type=f32) * scale_col
        scores = jnp.where(visible, scores, -1e30)
        top = jnp.max(scores, axis=-1, keepdims=True)
        weights = jnp.where(visible, jnp.exp(scores - top), 0.0)
        probs = weights / jnp.sum(weights, axis=-1, keepdims=True)
        narrow = probs.astype(jnp.bfloat16)
        attn = jnp.einsum("rts,sd->trd", narrow, v_group, preferred_element_type=f32)
        attn_list.append(attn)
        delta = jnp.sum(grad_group.astype(f32) * attn, axis=-1)
        dprobs = jnp.einsum("trd,sd->rts", grad_group, v_group, preferred_element_type=f32)
        dscores = (scale_col * probs * (dprobs - delta.T[:, :, None])).astype(jnp.bfloat16)
        dquery_list.append(jnp.einsum("rts,sd->trd", dscores, k_group, preferred_element_type=f32))
        dkey_list.append(jnp.einsum("rts,trd->sd", dscores, q_group, preferred_element_type=f32))
        dvalue_list.append(
            jnp.einsum("rts,trd->sd", narrow, grad_group, preferred_element_type=f32)
        )
    attention_output = (
        jnp.stack(attn_list, axis=1).reshape(token_rows, query_span_width).astype(jnp.bfloat16)
    )
    query_gradient = jnp.stack(dquery_list, axis=1).reshape(token_rows, QUERY_HEADS, HEAD_SIZE)
    dkey_all = jnp.stack(dkey_list, axis=1).reshape(every_key, key_span_width)
    dvalue_all = jnp.stack(dvalue_list, axis=1).reshape(every_key, key_span_width)
    partial_terms = jnp.concatenate([dkey_all, dvalue_all], axis=1)
    pieces = [partial_terms[offset * token_rows : (offset + 1) * token_rows] for offset in range(4)]
    returned = [
        passed_along(pieces[offset].astype(jnp.bfloat16), -offset) for offset in (1, 2, 3)
    ]
    pull_query = jax.vjp(head_norm, query)[1]
    pull_key = jax.vjp(head_norm, key)[1]
    d_q = pull_query(query_gradient)[0].reshape(token_rows, query_span_width).astype(jnp.bfloat16)
    members = jnp.arange(8, dtype=jnp.int32)[:, None]
    lane = jnp.arange(192, dtype=jnp.int32)[None, :]
    early = spread(
        jnp.concatenate([attention_output, d_q], axis=1),
        members * 96 + lane % 96 + lane // 96 * query_span_width,
    )
    early_ring = exchange(early, RING).reshape(8 * token_rows, 192)
    carried = pieces[0] + sum(piece.astype(f32) for piece in returned)
    d_key = pull_key(
        carried[:, :key_span_width].reshape(token_rows, KEY_VALUE_HEADS, HEAD_SIZE)
    )[0].reshape(token_rows, key_span_width)
    d_kv = jnp.concatenate([d_key, carried[:, key_span_width:]], axis=1).astype(jnp.bfloat16)
    d_hidden = jnp.dot(
        jnp.concatenate([d_q, d_kv], axis=1), w_qkv.T, preferred_element_type=f32
    )
    gain_term = jnp.sum(d_hidden * normed, axis=0)
    pull_tokens = jax.vjp(row_norm, token_f)[1]
    d_tokens = (grad_out.astype(f32) + pull_tokens(d_hidden * gain_f)[0]).astype(jnp.bfloat16)
    extra = TC
    width = d_tokens.shape[1]
    late_rows = jnp.concatenate(
        [
            jnp.concatenate([d_tokens, d_kv], axis=1),
            jnp.pad(gain_term.astype(jnp.bfloat16)[None], ((0, extra - 1), (0, 2 * key_span_width))),
        ],
        axis=0,
    )
    lane = jnp.arange(160, dtype=jnp.int32)[None, :]
    token_source = members // 4 * 384 + lane // 3 * 12 + members % 4 * 3 + lane % 3
    kv_lane = lane - 96
    kv_source = width + kv_lane // 32 * key_span_width + members * 32 + kv_lane % 32
    late = spread(late_rows, jnp.where(lane < 96, token_source, kv_source))
    late_ring = exchange(late, RING)
    gain_ring = jnp.sum(late_ring[:, token_rows, :96].astype(f32), axis=0)
    late_ring = late_ring[:, :token_rows]
    own_tokens = late_ring[:, :, :96].reshape(2, 4 * token_rows, 96)
    above = jnp.pad(own_tokens, ((0, 0), (TC, 0), (0, 0)))[:, : 4 * token_rows]
    both = jnp.concatenate([own_tokens, above], axis=2).reshape(8 * token_rows, 192)
    stem_part = jnp.dot(both.T, tiles_ring, preferred_element_type=f32).astype(jnp.bfloat16)
    stem_part = stem_part.reshape(2, 32, 3, 1024).transpose(1, 0, 2, 3).reshape(32, 48, 128)
    qkv_columns = jnp.concatenate(
        [early_ring[:, 96:], late_ring[:, :, 96:].reshape(8 * token_rows, 64)], axis=1
    )
    qkv_part = jnp.dot(hidden_ring.T, qkv_columns, preferred_element_type=f32)
    out_part = jnp.dot(dout_ring.T, early_ring[:, :96], preferred_element_type=f32)
    rows_part = jnp.concatenate([qkv_part, out_part], axis=1).astype(jnp.bfloat16)
    rows_part = rows_part.reshape(2, 32, 12, 256).transpose(1, 0, 2, 3).reshape(32, 48, 128)
    gain_part = jnp.pad(
        gain_ring.reshape(32, 1, 3).astype(jnp.bfloat16), ((0, 0), (0, 15), (0, 125))
    )
    terms = exchange(jnp.concatenate([stem_part, rows_part, gain_part], axis=1), REST)
    total = jnp.sum(terms.astype(f32), axis=0)
    d_stem_weight = total[:48].reshape(2, 3, 1024).transpose(0, 2, 1)
    d_norm_gain = total[96, :3]
    rows = exchange(total[48:96].reshape(8, 3, 256), RING)
    d_w_qkv = jnp.concatenate(
        [
            rows[:, :, first:last].transpose(1, 0, 2).reshape(3, -1)
            for first, last in ((0, 96), (96, 128), (128, 160))
        ],
        axis=1,
    )
    d_w_out = rows[:, :, 160:].transpose(0, 2, 1).reshape(query_span_width, 3)
    return (d_stem_weight, d_norm_gain, d_w_qkv, d_w_out)


def solution(mesh):
    fine = Mesh(mesh.devices.reshape(2, 4, 8, 2, 2), BLK + BAND)
    placed = (P(BAND, BLK, None), P(), P(), P(), P(), P(), P(), P(BAND, BLK, None))
    every = BLK + BAND
    return jax.shard_map(
        shards,
        mesh=fine,
        in_specs=placed,
        out_specs=(P(None, None, every), P(every), P(every, None), P(None, every)),
        check_vma=False,
    )
```

```python
import jax
import jax.numpy as jnp
import numpy as np
from jax import lax
from jax.experimental import pallas as pl
from jax.experimental.pallas import tpu as pltpu
from jax.sharding import Mesh, PartitionSpec as P

QUERY_HEADS = 12
KEY_VALUE_HEADS = 4
HEAD_SIZE = 64
TC = 16
D = 768
KV = 512
TOK = 128
BLK = ("yl", "x", "z")
BAND = ("yh", "c")
RING = ("yl", "yh", "c")
REST = ("x", "z")
F32 = jnp.float32
B16 = jnp.bfloat16
NN = (((1,), (0,)), ((), ()))
NT = (((1,), (1,)), ((), ()))
TN = (((0,), (0,)), ((), ()))


def dot(a, b, dims=NN):
    return lax.dot_general(a, b, dims, preferred_element_type=F32)


def passed_along(x, by):
    peers = lax.axis_size(BLK)
    return lax.ppermute(x, BLK, [(i, (i + by) % peers) for i in range(peers)])


def exchange(x, axes):
    return lax.all_to_all(x, axes, split_axis=0, concat_axis=0, tiled=True)


def orders():
    column = np.arange(D).reshape(2, 32, 4, 3)
    by_rest = column.transpose(1, 0, 2, 3).reshape(-1)
    by_member = column.transpose(0, 2, 1, 3).reshape(-1)
    eye = np.eye(D, dtype=np.float32)
    place = np.zeros((256, 192), np.float32)
    for j in range(2):
        for r in range(32):
            for k in range(3):
                place[r * 8 + j * 3 + k, j * 96 + r * 3 + k] = 1
    return jnp.asarray(eye[by_rest], B16), jnp.asarray(eye[by_member], B16), jnp.asarray(place, B16)


def call(body, outs, scratch=(), smem=(), count=0, limit=32, flops=10**9):
    specs = [
        pl.BlockSpec(memory_space=pltpu.SMEM if i in smem else pltpu.VMEM) for i in range(count)
    ]
    shapes = [jax.ShapeDtypeStruct(shape, kind) for shape, kind in outs]
    return pl.pallas_call(
        body,
        out_shape=shapes,
        in_specs=specs,
        out_specs=[pl.BlockSpec(memory_space=pltpu.VMEM)] * len(shapes),
        scratch_shapes=list(scratch),
        compiler_params=pltpu.CompilerParams(vmem_limit_bytes=limit * 2**20),
        cost_estimate=pl.CostEstimate(flops=flops, bytes_accessed=4 * 2**20, transcendentals=0),
    )


def stem_body(tiles, arrived, stem_w, gain, w_qkv, tokens_o, hidden_o, key_o, kv_o):
    own = tiles[...]
    below = jnp.concatenate([tiles[TC:, :], arrived[...]], axis=0)
    stem = dot(own, stem_w[0]) + dot(below, stem_w[1])
    low = stem.astype(B16)
    tokens_o[...] = low
    tok = low.astype(F32)
    factor = lax.rsqrt(jnp.mean(tok * tok, axis=1, keepdims=True) + 1e-05)
    hidden = (tok * factor * gain[...].astype(F32)).astype(B16)
    hidden_o[...] = hidden
    kv = dot(hidden, w_qkv[:, D:]).T
    key_o[...] = kv[:256]
    for h in range(KEY_VALUE_HEADS):
        k = kv[h * 64 : h * 64 + 64]
        scale = lax.rsqrt(jnp.mean(k * k, axis=0, keepdims=True) + 1e-06)
        kv_o[h * 64 : h * 64 + 64, :] = (k * scale).astype(B16)
    kv_o[256:, :] = kv[256:].astype(B16)


def query_body(hidden, d_out, w_qkv, w_out, by_rest, query_o, query_n_o, do_o, ring_o):
    h = hidden[...]
    q = dot(h, w_qkv[:, :D]).T
    query_o[...] = q
    for i in range(QUERY_HEADS):
        part = q[i * 64 : i * 64 + 64]
        scale = lax.rsqrt(jnp.mean(part * part, axis=0, keepdims=True) + 1e-06)
        query_n_o[i * 64 : i * 64 + 64, :] = (part * scale).astype(B16)
    g = d_out[...]
    do_o[...] = dot(w_out[...], g, NT).astype(B16)
    ring_o[:, :TOK] = dot(by_rest[...], h, NT).astype(B16)
    ring_o[:, TOK:] = dot(by_rest[...], g, NT).astype(B16)


def attend_body(
    own_block, scales, query, query_n, do, kv0, kv1, kv2, kv3, positions,
    early_o, dq_o, own_o, back1_o, back2_o, back3_o, attn_s,
):
    own = own_block[0]
    blocks = (kv0, kv1, kv2, kv3)
    q_pos = positions[pl.ds(own, 1), :]
    columns = []
    for j in range(4):
        row = positions[pl.ds(lax.rem(own - j + 64, 64), 1), :].astype(F32)
        columns.append(jnp.broadcast_to(row, (TOK, TOK)).T)
    key_pos = jnp.concatenate(columns, axis=0)
    bias = jnp.where(key_pos <= q_pos.astype(F32), 0.0, -1e30)
    bias = jnp.concatenate([bias] * 3, axis=1)
    for g in range(KEY_VALUE_HEADS):
        k = jnp.concatenate([b[g * 64 : g * 64 + 64, :] for b in blocks], axis=1)
        v = jnp.concatenate([b[256 + g * 64 : 320 + g * 64, :] for b in blocks], axis=1)
        heads = [3 * g + i for i in range(3)]
        q = jnp.concatenate([query_n[h * 64 : h * 64 + 64, :] for h in heads], axis=1)
        dy = jnp.concatenate([do[h * 64 : h * 64 + 64, :] for h in heads], axis=1)
        scale = jnp.concatenate([jnp.full((1, TOK), scales[h], F32) for h in heads], axis=1)
        scores = dot(k, q, TN) * scale
        scores = jnp.where(bias < 0.0, -1e30, scores)
        top = jnp.max(scores, axis=0, keepdims=True)
        weights = jnp.exp(scores - top)
        probs = weights * (1.0 / jnp.sum(weights, axis=0, keepdims=True))
        low = probs.astype(B16)
        attn = dot(v, low)
        delta = jnp.sum(dy.astype(F32) * attn, axis=0, keepdims=True)
        dprobs = dot(v, dy, TN)
        dscores = (scale * probs * (dprobs - delta)).astype(B16)
        dq = dot(k, dscores)
        dk = dot(q, dscores, NT)
        dv = dot(dy, low, NT)
        for i, h in enumerate(heads):
            rows = slice(h * 64, h * 64 + 64)
            lanes = slice(i * TOK, i * TOK + TOK)
            attn_s[rows, :] = attn[:, lanes].astype(B16)
            x = query[rows, :]
            dx = dq[:, lanes]
            r = lax.rsqrt(jnp.mean(x * x, axis=0, keepdims=True) + 1e-06)
            inner = jnp.mean(x * dx, axis=0, keepdims=True)
            dq_o[rows, :] = (r * dx - x * (r * r * r * inner)).astype(B16)
        own_o[g * 64 : g * 64 + 64, :] = dk[:, :TOK]
        own_o[256 + g * 64 : 320 + g * 64, :] = dv[:, :TOK]
        for j, back in enumerate((back1_o, back2_o, back3_o)):
            lanes = slice((j + 1) * TOK, (j + 2) * TOK)
            back[g * 64 : g * 64 + 64, :] = dk[:, lanes].astype(B16)
            back[256 + g * 64 : 320 + g * 64, :] = dv[:, lanes].astype(B16)
    for m in range(8):
        early_o[m, :96, :] = attn_s[m * 96 : m * 96 + 96, :]
        early_o[m, 96:, :] = dq_o[m * 96 : m * 96 + 96, :]


def tokens_body(
    own, back1, back2, back3, key, dq, w_qkv, tokens, gain, d_out, by_member, late_o, dkv_s
):
    total = own[...] + back1[...].astype(F32) + back2[...].astype(F32) + back3[...].astype(F32)
    for h in range(KEY_VALUE_HEADS):
        rows = slice(h * 64, h * 64 + 64)
        x = key[rows, :]
        dx = total[rows]
        r = lax.rsqrt(jnp.mean(x * x, axis=0, keepdims=True) + 1e-06)
        inner = jnp.mean(x * dx, axis=0, keepdims=True)
        dkv_s[rows, :] = (r * dx - x * (r * r * r * inner)).astype(B16)
    dkv_s[256:, :] = total[256:].astype(B16)
    d_hidden = (dot(w_qkv[:, :D], dq[...]) + dot(w_qkv[:, D:], dkv_s[...])).T
    tok = tokens[...].astype(F32)
    r = lax.rsqrt(jnp.mean(tok * tok, axis=1, keepdims=True) + 1e-05)
    gain_term = jnp.sum(d_hidden * (tok * r), axis=0, keepdims=True)
    dx = d_hidden * gain[...].astype(F32)
    inner = jnp.mean(tok * dx, axis=1, keepdims=True)
    d_tokens = (d_out[...].astype(F32) + (r * dx - tok * (r * r * r * inner))).astype(B16)
    spread = dot(by_member[...], d_tokens, NT).astype(B16)
    gains = jnp.concatenate(
        [gain_term[:, i * TOK : i * TOK + TOK] for i in range(6)] + [jnp.zeros((10, TOK), F32)],
        axis=0,
    ).astype(B16)
    for m in range(8):
        late_o[m, :96, :] = spread[m * 96 : m * 96 + 96]
        late_o[m, 96:128, :] = dkv_s[m * 32 : m * 32 + 32, :]
        late_o[m, 128:160, :] = dkv_s[256 + m * 32 : 288 + m * 32, :]
        late_o[m, 160:, :] = gains


def terms_body(
    core, early, late, tiles0, tiles1, ring0, ring1, place, stem_o, rows_o, pair_s, rhs_s, both_s
):
    lane = lax.broadcasted_iota(jnp.int32, (96, TOK), 1)
    gain = jnp.zeros((16, TOK), F32)
    zero = jnp.zeros((TOK, TOK), B16)
    for yl in range(2):
        before = jnp.zeros((96, TOK), F32)
        for band in range(4):
            m = yl * 4 + band
            block = late[m, :96, :]
            gain = gain + late[m, 160:, :].astype(F32)
            moved = pltpu.roll(block.astype(F32), TC, 1)
            pair_s[m, :96, :] = block
            pair_s[m, 96:, :] = jnp.where(lane < TC, before, moved).astype(B16)
            before = moved
            rhs_s[m, :96, :TOK] = early[m, 96:, :]
            rhs_s[m, 96:128, :TOK] = late[m, 96:128, :]
            rhs_s[m, :128, TOK:] = zero
            rhs_s[m, 128:224, :TOK] = zero[:96]
            rhs_s[m, 128:224, TOK:] = early[m, :96, :]
            rhs_s[m, 224:, :TOK] = late[m, 128:160, :]
            rhs_s[m, 224:, TOK:] = zero[:32]
    rows = jnp.zeros((D, 256), F32)
    for s, ring in enumerate((ring0, ring1)):
        side = lax.rem(core[0] + s, 2)
        for j in range(4):
            m = (j % 2) * 4 + (j // 2) * 2 + side
            at = s * 4 + j
            both_s[:, at * TOK : at * TOK + TOK] = dot(place[...], pair_s[m]).astype(B16)
            rows = rows + dot(ring[j], rhs_s[m], NT)
    rows_o[...] = rows.astype(B16)
    stem = dot(both_s[:, :512], tiles0[...]) + dot(both_s[:, 512:], tiles1[...])
    gain_row = jnp.concatenate(
        [gain[i : i + 1, :] for i in range(6)] + [jnp.zeros((1, 256), F32)], axis=1
    )
    slot = lax.rem(lax.broadcasted_iota(jnp.int32, (256, 1024), 0), 8)
    stem_o[...] = jnp.where(slot == 6, jnp.broadcast_to(gain_row, (256, 1024)), stem).astype(B16)


def shards(patches, stem_weight, norm_gain, w_qkv, w_out, per_head_scale, positions, d_out):
    tiles = patches[0]
    grad_out = d_out[0]
    by_rest, by_member, place = orders()
    bands = lax.axis_size(BAND)
    arrived = lax.ppermute(tiles[:TC], BAND, [(i, i - 1) for i in range(1, bands)])
    tiles_mine = lax.all_gather(tiles, ("yh", "yl"), axis=0, tiled=True)
    tiles_other = lax.ppermute(tiles_mine, "c", [(0, 1), (1, 0)])
    gain = norm_gain.reshape(1, D)
    tokens, hidden, key, kv_own = call(
        stem_body,
        [((TOK, D), B16), ((TOK, D), B16), ((256, TOK), F32), ((KV, TOK), B16)],
        count=5,
    )(tiles, arrived, stem_weight, gain, w_qkv)
    moved = [passed_along(kv_own, offset) for offset in range(1, 4)]
    query, query_n, do, ring_own = call(
        query_body,
        [((D, TOK), F32), ((D, TOK), B16), ((D, TOK), B16), ((D, 2 * TOK), B16)],
        count=5,
    )(hidden, grad_out, w_qkv, w_out, by_rest)
    ring_mine = lax.all_gather(ring_own, ("yh", "yl"), axis=0, tiled=False)
    ring_other = lax.ppermute(ring_mine, "c", [(0, 1), (1, 0)])
    own_block = lax.axis_index(BLK).astype(jnp.int32).reshape(1)
    early, d_q, own, back1, back2, back3 = call(
        attend_body,
        [((8, 192, TOK), B16), ((D, TOK), B16), ((KV, TOK), F32)] + [((KV, TOK), B16)] * 3,
        scratch=[pltpu.VMEM((D, TOK), B16)],
        smem=(0, 1),
        count=10,
    )(own_block, per_head_scale, query, query_n, do, kv_own, *moved, positions.reshape(64, TOK))
    returned = [passed_along(piece, -(j + 1)) for j, piece in enumerate((back1, back2, back3))]
    early_ring = exchange(early, RING)
    late = call(
        tokens_body,
        [((8, 176, TOK), B16)],
        scratch=[pltpu.VMEM((KV, TOK), B16)],
        count=11,
    )(own, *returned, key, d_q, w_qkv, tokens, gain, grad_out, by_member)[0]
    late_ring = exchange(late, RING)
    core = lax.axis_index("c").astype(jnp.int32).reshape(1)
    stem_terms, row_terms = call(
        terms_body,
        [((256, 1024), B16), ((D, 256), B16)],
        scratch=[
            pltpu.VMEM((8, 192, TOK), B16),
            pltpu.VMEM((8, 256, 256), B16),
            pltpu.VMEM((256, 1024), B16),
        ],
        smem=(0,),
        count=8,
    )(core, early_ring, late_ring, tiles_mine, tiles_other, ring_mine, ring_other, place)
    row_total = jnp.sum(exchange(row_terms.reshape(32, 24, 256), REST).astype(F32), axis=0)
    rows = exchange(row_total.reshape(8, 3, 256), RING)
    stem_total = jnp.sum(exchange(stem_terms.reshape(32, 8, 1024), REST).astype(F32), axis=0)
    d_stem_weight = stem_total[:6].reshape(2, 3, 1024).transpose(0, 2, 1)
    own_column = (lax.axis_index(BLK) * 4 + lax.axis_index(BAND)) * 3
    d_norm_gain = lax.dynamic_slice_in_dim(stem_total[6], own_column, 3)
    d_w_qkv = jnp.concatenate(
        [
            rows[:, :, first:last].transpose(1, 0, 2).reshape(3, -1)
            for first, last in ((0, 96), (96, 128), (224, 256))
        ],
        axis=1,
    )
    d_w_out = rows[:, :, 128:224].transpose(0, 2, 1).reshape(D, 3)
    return (d_stem_weight, d_norm_gain, d_w_qkv, d_w_out)


def solution(mesh):
    fine = Mesh(mesh.devices.reshape(2, 4, 8, 2, 2), BLK + BAND)
    placed = (P(BAND, BLK, None), P(), P(), P(), P(), P(), P(), P(BAND, BLK, None))
    every = BLK + BAND
    return jax.shard_map(
        shards,
        mesh=fine,
        in_specs=placed,
        out_specs=(P(None, None, every), P(every), P(every, None), P(None, every)),
        check_vma=False,
    )
```

```python
import jax
import jax.numpy as jnp
import numpy as np
from jax import lax
from jax.experimental import pallas as pl
from jax.experimental.pallas import tpu as pltpu
from jax.sharding import Mesh, PartitionSpec as P

QUERY_HEADS = 12
KEY_VALUE_HEADS = 4
HEAD_SIZE = 64
TC = 16
D = 768
KV = 512
TOK = 128
BLK = ("yl", "x", "z")
BAND = ("yh", "c")
RING = ("yl", "yh", "c")
REST = ("x", "z")
F32 = jnp.float32
B16 = jnp.bfloat16
NN = (((1,), (0,)), ((), ()))
NT = (((1,), (1,)), ((), ()))
TN = (((0,), (0,)), ((), ()))


def dot(a, b, dims=NN):
    return lax.dot_general(a, b, dims, preferred_element_type=F32)


def passed_along(x, by):
    peers = lax.axis_size(BLK)
    return lax.ppermute(x, BLK, [(i, (i + by) % peers) for i in range(peers)])


def exchange(x, axes):
    return lax.all_to_all(x, axes, split_axis=0, concat_axis=0, tiled=True)


def orders():
    column = np.arange(D).reshape(2, 32, 4, 3)
    by_rest = column.transpose(1, 0, 2, 3).reshape(32, 24)
    by_rest = np.concatenate([by_rest[:, :16].reshape(-1), by_rest[:, 16:].reshape(-1)])
    by_member = column.transpose(0, 2, 1, 3).reshape(-1)
    eye = np.eye(D, dtype=np.float32)
    place = np.zeros((2, 512, 192), np.float32)
    fold = np.zeros((2, 512, 256), np.float32)
    for half in range(2):
        for r in range(32):
            for j in range(2):
                for k in range(3):
                    place[half, r * 16 + half * 6 + j * 3 + k, j * 96 + r * 3 + k] = 1
            for i in range(8):
                fold[half, r * 16 + half * 8 + i, r * 8 + i] = 1
    tables = (eye[by_rest], eye[by_member], place, fold)
    return [jnp.asarray(table, B16) for table in tables]


def call(body, outs, scratch=(), smem=(), count=0, limit=60, flops=10**9):
    specs = [
        pl.BlockSpec(memory_space=pltpu.SMEM if i in smem else pltpu.VMEM) for i in range(count)
    ]
    shapes = [jax.ShapeDtypeStruct(shape, kind) for shape, kind in outs]
    return pl.pallas_call(
        body,
        out_shape=shapes,
        in_specs=specs,
        out_specs=[pl.BlockSpec(memory_space=pltpu.VMEM)] * len(shapes),
        scratch_shapes=list(scratch),
        compiler_params=pltpu.CompilerParams(vmem_limit_bytes=limit * 2**20),
        cost_estimate=pl.CostEstimate(flops=flops, bytes_accessed=4 * 2**20, transcendentals=0),
    )


def stem_body(tiles, arrived, stem_w, gain, w_qkv, tokens_o, hidden_o, key_o, kv_o):
    own = tiles[...]
    below = jnp.concatenate([tiles[TC:, :], arrived[...]], axis=0)
    stem = dot(own, stem_w[0]) + dot(below, stem_w[1])
    low = stem.astype(B16)
    tokens_o[...] = low
    tok = low.astype(F32)
    factor = lax.rsqrt(jnp.mean(tok * tok, axis=1, keepdims=True) + 1e-05)
    hidden = (tok * factor * gain[...].astype(F32)).astype(B16)
    hidden_o[...] = hidden
    kv = dot(hidden, w_qkv[:, D:]).T
    key_o[...] = kv[:256]
    for h in range(KEY_VALUE_HEADS):
        k = kv[h * 64 : h * 64 + 64]
        scale = lax.rsqrt(jnp.mean(k * k, axis=0, keepdims=True) + 1e-06)
        kv_o[h * 64 : h * 64 + 64, :] = (k * scale).astype(B16)
    kv_o[256:, :] = kv[256:].astype(B16)


def query_body(hidden, d_out, w_qkv, w_out, by_rest, query_o, query_n_o, do_o, ring_o):
    h = hidden[...]
    q = dot(h, w_qkv[:, :D]).T
    query_o[...] = q
    for i in range(QUERY_HEADS):
        part = q[i * 64 : i * 64 + 64]
        scale = lax.rsqrt(jnp.mean(part * part, axis=0, keepdims=True) + 1e-06)
        query_n_o[i * 64 : i * 64 + 64, :] = (part * scale).astype(B16)
    g = d_out[...]
    do_o[...] = dot(w_out[...], g, NT).astype(B16)
    ring_o[:, :TOK] = dot(by_rest[...], h, NT).astype(B16)
    ring_o[:, TOK:] = dot(by_rest[...], g, NT).astype(B16)


def attend_body(
    own_block, scales, query, query_n, do, kv0, kv1, kv2, kv3, positions,
    early_o, dq_o, own_o, back1_o, back2_o, back3_o, attn_s,
):
    own = own_block[0]
    blocks = (kv0, kv1, kv2, kv3)
    q_pos = positions[pl.ds(own, 1), :]
    columns = []
    for j in range(4):
        row = positions[pl.ds(lax.rem(own - j + 64, 64), 1), :].astype(F32)
        columns.append(jnp.broadcast_to(row, (TOK, TOK)).T)
    key_pos = jnp.concatenate(columns, axis=0)
    bias = jnp.where(key_pos <= q_pos.astype(F32), 0.0, -1e30)
    bias = jnp.concatenate([bias] * 3, axis=1)
    for g in range(KEY_VALUE_HEADS):
        k = jnp.concatenate([b[g * 64 : g * 64 + 64, :] for b in blocks], axis=1)
        v = jnp.concatenate([b[256 + g * 64 : 320 + g * 64, :] for b in blocks], axis=1)
        heads = [3 * g + i for i in range(3)]
        q = jnp.concatenate([query_n[h * 64 : h * 64 + 64, :] for h in heads], axis=1)
        dy = jnp.concatenate([do[h * 64 : h * 64 + 64, :] for h in heads], axis=1)
        scale = jnp.concatenate([jnp.full((1, TOK), scales[h], F32) for h in heads], axis=1)
        scores = dot(k, q, TN) * scale
        scores = jnp.where(bias < 0.0, -1e30, scores)
        top = jnp.max(scores, axis=0, keepdims=True)
        weights = jnp.exp(scores - top)
        probs = weights * (1.0 / jnp.sum(weights, axis=0, keepdims=True))
        low = probs.astype(B16)
        attn = dot(v, low)
        delta = jnp.sum(dy.astype(F32) * attn, axis=0, keepdims=True)
        dprobs = dot(v, dy, TN)
        dscores = (scale * probs * (dprobs - delta)).astype(B16)
        dq = dot(k, dscores)
        dk = dot(q, dscores, NT)
        dv = dot(dy, low, NT)
        for i, h in enumerate(heads):
            rows = slice(h * 64, h * 64 + 64)
            lanes = slice(i * TOK, i * TOK + TOK)
            attn_s[rows, :] = attn[:, lanes].astype(B16)
            x = query[rows, :]
            dx = dq[:, lanes]
            r = lax.rsqrt(jnp.mean(x * x, axis=0, keepdims=True) + 1e-06)
            inner = jnp.mean(x * dx, axis=0, keepdims=True)
            dq_o[rows, :] = (r * dx - x * (r * r * r * inner)).astype(B16)
        own_o[g * 64 : g * 64 + 64, :] = dk[:, :TOK]
        own_o[256 + g * 64 : 320 + g * 64, :] = dv[:, :TOK]
        for j, back in enumerate((back1_o, back2_o, back3_o)):
            lanes = slice((j + 1) * TOK, (j + 2) * TOK)
            back[g * 64 : g * 64 + 64, :] = dk[:, lanes].astype(B16)
            back[256 + g * 64 : 320 + g * 64, :] = dv[:, lanes].astype(B16)
    for m in range(8):
        early_o[m, :96, :] = attn_s[m * 96 : m * 96 + 96, :]
        early_o[m, 96:, :] = dq_o[m * 96 : m * 96 + 96, :]


def tokens_body(
    own, back1, back2, back3, key, dq, w_qkv, tokens, gain, d_out, by_member, late_o, dkv_s
):
    total = own[...] + back1[...].astype(F32) + back2[...].astype(F32) + back3[...].astype(F32)
    for h in range(KEY_VALUE_HEADS):
        rows = slice(h * 64, h * 64 + 64)
        x = key[rows, :]
        dx = total[rows]
        r = lax.rsqrt(jnp.mean(x * x, axis=0, keepdims=True) + 1e-06)
        inner = jnp.mean(x * dx, axis=0, keepdims=True)
        dkv_s[rows, :] = (r * dx - x * (r * r * r * inner)).astype(B16)
    dkv_s[256:, :] = total[256:].astype(B16)
    d_hidden = (dot(w_qkv[:, :D], dq[...]) + dot(w_qkv[:, D:], dkv_s[...])).T
    tok = tokens[...].astype(F32)
    r = lax.rsqrt(jnp.mean(tok * tok, axis=1, keepdims=True) + 1e-05)
    gain_term = jnp.sum(d_hidden * (tok * r), axis=0, keepdims=True)
    dx = d_hidden * gain[...].astype(F32)
    inner = jnp.mean(tok * dx, axis=1, keepdims=True)
    d_tokens = (d_out[...].astype(F32) + (r * dx - tok * (r * r * r * inner))).astype(B16)
    spread = dot(by_member[...], d_tokens, NT).astype(B16)
    gains = jnp.concatenate(
        [gain_term[:, i * TOK : i * TOK + TOK] for i in range(6)] + [jnp.zeros((10, TOK), F32)],
        axis=0,
    ).astype(B16)
    for m in range(8):
        late_o[m, :96, :] = spread[m * 96 : m * 96 + 96]
        late_o[m, 96:128, :] = dkv_s[m * 32 : m * 32 + 32, :]
        late_o[m, 128:160, :] = dkv_s[256 + m * 32 : 288 + m * 32, :]
        late_o[m, 160:, :] = gains


def terms_body(
    core, early, late, tiles0, tiles1, ring0, ring1, place, fold, terms_o, pair_s, rhs_s, both_s
):
    lane = lax.broadcasted_iota(jnp.int32, (96, TOK), 1)
    gain = jnp.zeros((16, TOK), F32)
    zero = jnp.zeros((TOK, TOK), B16)
    for yl in range(2):
        before = jnp.zeros((96, TOK), F32)
        for band in range(4):
            m = yl * 4 + band
            block = late[m, :96, :]
            gain = gain + late[m, 160:, :].astype(F32)
            moved = pltpu.roll(block.astype(F32), TC, 1)
            pair_s[m, :96, :] = block
            pair_s[m, 96:, :] = jnp.where(lane < TC, before, moved).astype(B16)
            before = moved
            rhs_s[m, :96, :TOK] = early[m, 96:, :]
            rhs_s[m, 96:128, :TOK] = late[m, 96:128, :]
            rhs_s[m, :128, TOK:] = zero
            rhs_s[m, 128:224, :TOK] = zero[:96]
            rhs_s[m, 128:224, TOK:] = early[m, :96, :]
            rhs_s[m, 224:, :TOK] = late[m, 128:160, :]
            rhs_s[m, 224:, TOK:] = zero[:32]
    rows = jnp.zeros((D, 256), F32)
    for s, ring in enumerate((ring0, ring1)):
        side = lax.rem(core[0] + s, 2)
        for j in range(4):
            m = (j % 2) * 4 + (j // 2) * 2 + side
            at = s * 4 + j
            for half in range(2):
                both_s[half, :, at * TOK : at * TOK + TOK] = dot(place[half], pair_s[m]).astype(B16)
            rows = rows + dot(ring[j], rhs_s[m], NT)
    low = rows.astype(B16)
    terms_o[:, 512:768] = low[:512]
    terms_o[:, 768:] = (dot(fold[0], low[512:, :TOK]) + dot(fold[1], low[512:, TOK:])).astype(B16)
    stem = dot(both_s[0, :, :512], tiles0[:, :512]) + dot(both_s[0, :, 512:], tiles1[:, :512])
    stem = stem + dot(both_s[1, :, :512], tiles0[:, 512:])
    stem = stem + dot(both_s[1, :, 512:], tiles1[:, 512:])
    slot = lax.rem(lax.broadcasted_iota(jnp.int32, (512, 512), 0), 16)
    first = jnp.concatenate([gain[i : i + 1, :] for i in range(4)], axis=1)
    second = jnp.concatenate([gain[4:5, :], gain[5:6, :], jnp.zeros((1, 256), F32)], axis=1)
    stem = jnp.where(slot == 12, jnp.broadcast_to(first, (512, 512)), stem)
    stem = jnp.where(slot == 13, jnp.broadcast_to(second, (512, 512)), stem)
    terms_o[:, :512] = stem.astype(B16)


def total_body(terms, stem_o, gain_o, rows_o):
    total = terms[0].astype(F32)
    for r in range(1, 32):
        total = total + terms[r].astype(F32)
    stem_o[:, :512] = total[:6, :512]
    stem_o[:, 512:] = total[6:12, :512]
    gain_o[:, :512] = total[12:13, :512]
    gain_o[:, 512:] = total[13:14, :256]
    last = jnp.concatenate([total[:8, 768:], total[8:, 768:]], axis=1)
    rows = jnp.concatenate([total[:, 512:768], last], axis=0)
    for m in range(8):
        rows_o[m, :3, :] = rows[m * 3 : m * 3 + 3]
        rows_o[m, 3:, :] = jnp.zeros((5, 256), F32)


def final_body(rows, qkv_o, out_o):
    for first, last, to in ((0, 96, 0), (96, 128, D), (224, 256, D + 256)):
        width = last - first
        for m in range(8):
            qkv_o[:, to + m * width : to + m * width + width] = rows[m, :3, first:last]
    for m in range(8):
        out_o[:, m * 96 : m * 96 + 96] = rows[m, :3, 128:224]


def shards(patches, stem_weight, norm_gain, w_qkv, w_out, per_head_scale, positions, d_out):
    tiles = patches[0]
    grad_out = d_out[0]
    by_rest, by_member, place, fold = orders()
    bands = lax.axis_size(BAND)
    arrived = lax.ppermute(tiles[:TC], BAND, [(i, i - 1) for i in range(1, bands)])
    tiles_mine = lax.all_gather(tiles, ("yh", "yl"), axis=0, tiled=True)
    gain = norm_gain.reshape(1, D)
    tokens, hidden, key, kv_own = call(
        stem_body,
        [((TOK, D), B16), ((TOK, D), B16), ((256, TOK), F32), ((KV, TOK), B16)],
        count=5,
    )(tiles, arrived, stem_weight, gain, w_qkv)
    moved = [passed_along(kv_own, offset) for offset in range(1, 4)]
    query, query_n, do, ring_own = call(
        query_body,
        [((D, TOK), F32), ((D, TOK), B16), ((D, TOK), B16), ((D, 2 * TOK), B16)],
        count=5,
    )(hidden, grad_out, w_qkv, w_out, by_rest)
    ring_mine = lax.all_gather(ring_own, ("yh", "yl"), axis=0, tiled=False)
    own_block = lax.axis_index(BLK).astype(jnp.int32).reshape(1)
    early, d_q, own, back1, back2, back3 = call(
        attend_body,
        [((8, 192, TOK), B16), ((D, TOK), B16), ((KV, TOK), F32)] + [((KV, TOK), B16)] * 3,
        scratch=[pltpu.VMEM((D, TOK), B16)],
        smem=(0, 1),
        count=10,
    )(own_block, per_head_scale, query, query_n, do, kv_own, *moved, positions.reshape(64, TOK))
    returned = [passed_along(piece, -(j + 1)) for j, piece in enumerate((back1, back2, back3))]
    early_ring = exchange(early, RING)
    late = call(
        tokens_body,
        [((8, 176, TOK), B16)],
        scratch=[pltpu.VMEM((KV, TOK), B16)],
        count=11,
    )(own, *returned, key, d_q, w_qkv, tokens, gain, grad_out, by_member)[0]
    late_ring = exchange(late, RING)
    tiles_mine, ring_mine, late = lax.optimization_barrier((tiles_mine, ring_mine, late))
    tiles_other = lax.ppermute(tiles_mine, "c", [(0, 1), (1, 0)])
    ring_other = lax.ppermute(ring_mine, "c", [(0, 1), (1, 0)])
    core = lax.axis_index("c").astype(jnp.int32).reshape(1)
    terms = call(
        terms_body,
        [((512, 896), B16)],
        scratch=[
            pltpu.VMEM((8, 192, TOK), B16),
            pltpu.VMEM((8, 256, 256), B16),
            pltpu.VMEM((2, 512, 1024), B16),
        ],
        smem=(0,),
        count=9,
    )(core, early_ring, late_ring, tiles_mine, tiles_other, ring_mine, ring_other, place, fold)[0]
    stem_total, gain_total, row_total = call(
        total_body, [((6, 1024), F32), ((1, D), F32), ((8, 8, 256), F32)], count=1
    )(exchange(terms.reshape(32, 16, 896), REST))
    d_w_qkv, d_w_out = call(final_body, [((3, 1280), F32), ((3, D), F32)], count=1)(
        exchange(row_total, RING)
    )
    own_column = (lax.axis_index(BLK) * 4 + lax.axis_index(BAND)) * 3
    d_norm_gain = lax.dynamic_slice_in_dim(gain_total[0], own_column, 3)
    d_stem_weight = stem_total.reshape(2, 3, 1024).transpose(0, 2, 1)
    return (d_stem_weight, d_norm_gain, d_w_qkv, d_w_out.T)


def solution(mesh):
    fine = Mesh(mesh.devices.reshape(2, 4, 8, 2, 2), BLK + BAND)
    placed = (P(BAND, BLK, None), P(), P(), P(), P(), P(), P(), P(BAND, BLK, None))
    every = BLK + BAND
    return jax.shard_map(
        shards,
        mesh=fine,
        in_specs=placed,
        out_specs=(P(None, None, every), P(every), P(every, None), P(None, every)),
        check_vma=False,
    )
```

```python
import jax
import jax.numpy as jnp
import numpy as np
from jax import lax
from jax.experimental import pallas as pl
from jax.experimental.pallas import tpu as pltpu
from jax.sharding import Mesh, PartitionSpec as P

QUERY_HEADS = 12
KEY_VALUE_HEADS = 4
HEAD_SIZE = 64
TC = 16
D = 768
KV = 512
TOK = 128
BLK = ("yl", "x", "z")
BAND = ("yh", "c")
RING = ("yl", "yh", "c")
REST = ("x", "z")
F32 = jnp.float32
B16 = jnp.bfloat16
NN = (((1,), (0,)), ((), ()))
NT = (((1,), (1,)), ((), ()))
TN = (((0,), (0,)), ((), ()))


def dot(a, b, dims=NN):
    return lax.dot_general(a, b, dims, preferred_element_type=F32)


def passed_along(x, by):
    peers = lax.axis_size(BLK)
    return lax.ppermute(x, BLK, [(i, (i + by) % peers) for i in range(peers)])


def exchange(x, axes):
    return lax.all_to_all(x, axes, split_axis=0, concat_axis=0, tiled=True)


def orders():
    column = np.arange(D).reshape(2, 32, 4, 3)
    by_rest = column.transpose(1, 0, 2, 3).reshape(32, 24)
    by_rest = np.concatenate([by_rest[:, :16].reshape(-1), by_rest[:, 16:].reshape(-1)])
    by_member = column.transpose(0, 2, 1, 3).reshape(-1)
    eye = np.eye(D, dtype=np.float32)
    place = np.zeros((2, 512, 192), np.float32)
    fold = np.zeros((2, 512, 256), np.float32)
    for half in range(2):
        for r in range(32):
            for j in range(2):
                for k in range(3):
                    place[half, r * 16 + half * 6 + j * 3 + k, j * 96 + r * 3 + k] = 1
            for i in range(8):
                fold[half, r * 16 + half * 8 + i, r * 8 + i] = 1
    tables = (eye[by_rest], eye[by_member], place, fold)
    return [jnp.asarray(table, B16) for table in tables]


class Loaded:
    def __init__(self, ref, pieces):
        self.ref, self.pieces = ref, pieces

    def piece(self, i):
        copy, place = self.pieces[i]
        if copy is not None:
            copy.wait()
            self.pieces[i] = (None, place)
        return self.ref.at[place]

    def __getitem__(self, index):
        for i in range(len(self.pieces)):
            self.piece(i)
        return self.ref[index]


def split(shape, count):
    rows = shape[0] // count
    return [slice(i * rows, i * rows + rows) for i in range(count)]


def call(body, outs, scratch=(), smem=(), pieces=None, columns=None, flops=10**9):
    pieces, columns = pieces or {}, columns or {}

    def run(*operands):
        held, parts, total = [], [], 0
        for i, operand in enumerate(operands):
            if i in smem:
                continue
            shape = operand.shape
            if i in columns:
                shape = (shape[0], columns[i][1] - columns[i][0])
            held.append(pltpu.VMEM(shape, operand.dtype))
            parts.append((i, split(shape, pieces.get(i, 1))))
            total += pieces.get(i, 1)

        def kernel(*refs):
            inputs = list(refs[: len(operands)])
            others = refs[len(operands) : len(refs) - len(held) - 1]
            stores, sems = refs[len(refs) - len(held) - 1 : -1], refs[-1]
            used = 0
            for (i, places), store in zip(parts, stores):
                source = inputs[i]
                if i in columns:
                    source = source.at[:, columns[i][0] : columns[i][1]]
                made = []
                for place in places:
                    copy = pltpu.make_async_copy(
                        source.at[place], store.at[place], sems.at[used]
                    )
                    copy.start()
                    made.append((copy, place))
                    used += 1
                inputs[i] = Loaded(store, made)
            body(*inputs, *others)
            for value in inputs:
                if isinstance(value, Loaded):
                    for j in range(len(value.pieces)):
                        value.piece(j)

        shapes = [jax.ShapeDtypeStruct(shape, kind) for shape, kind in outs]
        return pl.pallas_call(
            kernel,
            out_shape=shapes,
            in_specs=[
                pl.BlockSpec(memory_space=pltpu.SMEM if i in smem else pl.ANY)
                for i in range(len(operands))
            ],
            out_specs=[pl.BlockSpec(memory_space=pltpu.VMEM)] * len(shapes),
            scratch_shapes=[*scratch, *held, pltpu.SemaphoreType.DMA((total,))],
            compiler_params=pltpu.CompilerParams(vmem_limit_bytes=64 * 2**20),
            cost_estimate=pl.CostEstimate(
                flops=flops, bytes_accessed=4 * 2**20, transcendentals=0
            ),
        )(*operands)

    return run


def stem_body(
    tiles, stem_w, arrived, w_kv, gain, d_out, by_rest, tokens_o, hidden_o, key_o, kv_o, ring_o
):
    own = tiles[...]
    deep = own.shape[1] // 4
    below = jnp.concatenate([own[TC:], arrived[...]], axis=0)
    stem = jnp.zeros((TOK, D), F32)
    for j, rows in enumerate((own, below)):
        for i in range(4):
            columns = rows[:, i * deep : i * deep + deep]
            stem = stem + dot(columns, stem_w.piece(4 * j + i)[...])
    low = stem.astype(B16)
    tokens_o[...] = low
    tok = low.astype(F32)
    factor = lax.rsqrt(jnp.mean(tok * tok, axis=1, keepdims=True) + 1e-05)
    hidden = (tok * factor * gain[...].astype(F32)).astype(B16)
    hidden_o[...] = hidden
    kv = dot(hidden, w_kv[...]).T
    key_o[...] = kv[:256]
    for h in range(KEY_VALUE_HEADS):
        k = kv[h * 64 : h * 64 + 64]
        scale = lax.rsqrt(jnp.mean(k * k, axis=0, keepdims=True) + 1e-06)
        kv_o[h * 64 : h * 64 + 64, :] = (k * scale).astype(B16)
    kv_o[256:, :] = kv[256:].astype(B16)
    ring_o[:, :TOK] = dot(by_rest[...], hidden, NT).astype(B16)
    ring_o[:, TOK:] = dot(by_rest[...], d_out[...], NT).astype(B16)


def query_body(hidden, d_out, w_q, w_out, query_o, query_n_o, do_o):
    h = hidden[...]
    g = d_out[...]
    q = dot(h, w_q[...]).T
    query_o[...] = q
    for i in range(QUERY_HEADS):
        part = q[i * 64 : i * 64 + 64]
        scale = lax.rsqrt(jnp.mean(part * part, axis=0, keepdims=True) + 1e-06)
        query_n_o[i * 64 : i * 64 + 64, :] = (part * scale).astype(B16)
    do_o[...] = dot(w_out[...], g, NT).astype(B16)


def attend_body(
    own_block, scales, positions, kv0, kv1, kv2, kv3, query_n, do, query,
    attn_o, dq_o, own_o, back1_o, back2_o, back3_o,
):
    own = own_block[0]
    blocks = (kv0, kv1, kv2, kv3)
    positions[:8]
    rows = positions.ref
    q_pos = rows[pl.ds(own, 1), :]
    columns = []
    for j in range(4):
        row = rows[pl.ds(lax.rem(own - j + 64, 64), 1), :].astype(F32)
        columns.append(jnp.broadcast_to(row, (TOK, TOK)).T)
    key_pos = jnp.concatenate(columns, axis=0)
    bias = jnp.where(key_pos <= q_pos.astype(F32), 0.0, -1e30)
    bias = jnp.concatenate([bias] * 3, axis=1)
    for g in range(KEY_VALUE_HEADS):
        k = jnp.concatenate([b[g * 64 : g * 64 + 64, :] for b in blocks], axis=1)
        v = jnp.concatenate([b[256 + g * 64 : 320 + g * 64, :] for b in blocks], axis=1)
        heads = [3 * g + i for i in range(3)]
        q = jnp.concatenate([query_n[h * 64 : h * 64 + 64, :] for h in heads], axis=1)
        dy = jnp.concatenate([do[h * 64 : h * 64 + 64, :] for h in heads], axis=1)
        scale = jnp.concatenate([jnp.full((1, TOK), scales[h], F32) for h in heads], axis=1)
        scores = dot(k, q, TN) * scale
        scores = jnp.where(bias < 0.0, -1e30, scores)
        top = jnp.max(scores, axis=0, keepdims=True)
        weights = jnp.exp(scores - top)
        probs = weights * (1.0 / jnp.sum(weights, axis=0, keepdims=True))
        low = probs.astype(B16)
        attn = dot(v, low)
        delta = jnp.sum(dy.astype(F32) * attn, axis=0, keepdims=True)
        dprobs = dot(v, dy, TN)
        dscores = (scale * probs * (dprobs - delta)).astype(B16)
        dq = dot(k, dscores)
        dk = dot(q, dscores, NT)
        dv = dot(dy, low, NT)
        for i, h in enumerate(heads):
            rows = slice(h * 64, h * 64 + 64)
            lanes = slice(i * TOK, i * TOK + TOK)
            attn_o[rows, :] = attn[:, lanes].astype(B16)
            x = query[rows, :]
            dx = dq[:, lanes]
            r = lax.rsqrt(jnp.mean(x * x, axis=0, keepdims=True) + 1e-06)
            inner = jnp.mean(x * dx, axis=0, keepdims=True)
            dq_o[rows, :] = (r * dx - x * (r * r * r * inner)).astype(B16)
        own_o[g * 64 : g * 64 + 64, :] = dk[:, :TOK]
        own_o[256 + g * 64 : 320 + g * 64, :] = dv[:, :TOK]
        for j, back in enumerate((back1_o, back2_o, back3_o)):
            lanes = slice((j + 1) * TOK, (j + 2) * TOK)
            back[g * 64 : g * 64 + 64, :] = dk[:, lanes].astype(B16)
            back[256 + g * 64 : 320 + g * 64, :] = dv[:, lanes].astype(B16)


def part_body(w_q, dq, part_o):
    part_o[...] = dot(w_q[...], dq[...]).T


def tokens_body(
    own, back1, back2, back3, key, w_kv, tokens, gain, part, d_out, by_member, attn, dq,
    late_o, dkv_s,
):
    total = own[...] + back1[...].astype(F32) + back2[...].astype(F32) + back3[...].astype(F32)
    for h in range(KEY_VALUE_HEADS):
        rows = slice(h * 64, h * 64 + 64)
        x = key[rows, :]
        dx = total[rows]
        r = lax.rsqrt(jnp.mean(x * x, axis=0, keepdims=True) + 1e-06)
        inner = jnp.mean(x * dx, axis=0, keepdims=True)
        dkv_s[rows, :] = (r * dx - x * (r * r * r * inner)).astype(B16)
    dkv_s[256:, :] = total[256:].astype(B16)
    d_hidden = part[...] + dot(w_kv[...], dkv_s[...]).T
    tok = tokens[...].astype(F32)
    r = lax.rsqrt(jnp.mean(tok * tok, axis=1, keepdims=True) + 1e-05)
    gain_term = jnp.sum(d_hidden * (tok * r), axis=0, keepdims=True)
    dx = d_hidden * gain[...].astype(F32)
    inner = jnp.mean(tok * dx, axis=1, keepdims=True)
    d_tokens = (d_out[...].astype(F32) + (r * dx - tok * (r * r * r * inner))).astype(B16)
    spread = dot(by_member[...], d_tokens, NT).astype(B16)
    gains = jnp.concatenate(
        [gain_term[:, i * TOK : i * TOK + TOK] for i in range(6)] + [jnp.zeros((10, TOK), F32)],
        axis=0,
    ).astype(B16)
    for m in range(8):
        late_o[m, :96, :] = spread[m * 96 : m * 96 + 96]
        late_o[m, 96:128, :] = dkv_s[m * 32 : m * 32 + 32, :]
        late_o[m, 128:160, :] = dkv_s[256 + m * 32 : 288 + m * 32, :]
        late_o[m, 160:176, :] = gains
        late_o[m, 176:272, :] = attn[m * 96 : m * 96 + 96, :]
        late_o[m, 272:, :] = dq[m * 96 : m * 96 + 96, :]


def terms_body(
    core, late, place, ring0, ring1, tiles0, tiles1, fold, terms_o, pair_s, rhs_s, both_s
):
    lane = lax.broadcasted_iota(jnp.int32, (96, TOK), 1)
    gain = jnp.zeros((16, TOK), F32)
    zero = jnp.zeros((TOK, TOK), B16)
    for yl in range(2):
        before = jnp.zeros((96, TOK), F32)
        for band in range(4):
            m = yl * 4 + band
            block = late[m, :96, :]
            gain = gain + late[m, 160:176, :].astype(F32)
            moved = pltpu.roll(block.astype(F32), TC, 1)
            pair_s[m, :96, :] = block
            pair_s[m, 96:, :] = jnp.where(lane < TC, before, moved).astype(B16)
            before = moved
            rhs_s[m, :96, :TOK] = late[m, 272:, :]
            rhs_s[m, 96:128, :TOK] = late[m, 96:128, :]
            rhs_s[m, :128, TOK:] = zero
            rhs_s[m, 128:224, :TOK] = zero[:96]
            rhs_s[m, 128:224, TOK:] = late[m, 176:272, :]
            rhs_s[m, 224:, :TOK] = late[m, 128:160, :]
            rhs_s[m, 224:, TOK:] = zero[:32]
    rows = jnp.zeros((D, 256), F32)
    for s, ring in enumerate((ring0, ring1)):
        side = lax.rem(core[0] + s, 2)
        for j in range(4):
            m = (j % 2) * 4 + (j // 2) * 2 + side
            at = s * 4 + j
            for half in range(2):
                both_s[half, :, at * TOK : at * TOK + TOK] = dot(place[half], pair_s[m]).astype(B16)
            rows = rows + dot(ring.piece(j)[0], rhs_s[m], NT)
    low = rows.astype(B16)
    terms_o[:, 512:768] = low[:512]
    terms_o[:, 768:] = (dot(fold[0], low[512:, :TOK]) + dot(fold[1], low[512:, TOK:])).astype(B16)
    stem = dot(both_s[0, :, :512], tiles0[:, :512]) + dot(both_s[1, :, :512], tiles0[:, 512:])
    stem = stem + dot(both_s[0, :, 512:], tiles1[:, :512])
    stem = stem + dot(both_s[1, :, 512:], tiles1[:, 512:])
    slot = lax.rem(lax.broadcasted_iota(jnp.int32, (512, 512), 0), 16)
    first = jnp.concatenate([gain[i : i + 1, :] for i in range(4)], axis=1)
    second = jnp.concatenate([gain[4:5, :], gain[5:6, :], jnp.zeros((1, 256), F32)], axis=1)
    stem = jnp.where(slot == 12, jnp.broadcast_to(first, (512, 512)), stem)
    stem = jnp.where(slot == 13, jnp.broadcast_to(second, (512, 512)), stem)
    terms_o[:, :512] = stem.astype(B16)


def total_body(terms, stem_o, gain_o, rows_o):
    total = jnp.zeros((16, 896), F32)
    for piece in range(4):
        block = terms.piece(piece)
        for r in range(8):
            total = total + block[r].astype(F32)
    for j in range(2):
        for k in range(3):
            at = j * 3 + k
            stem_o[k, j : j + 1, :512] = total[at : at + 1, :512]
            stem_o[k, j : j + 1, 512:] = total[at + 6 : at + 7, :512]
    gain_o[:, :512] = total[12:13, :512]
    gain_o[:, 512:] = total[13:14, :256]
    last = jnp.concatenate([total[:8, 768:], total[8:, 768:]], axis=1)
    rows = jnp.concatenate([total[:, 512:768], last], axis=0)
    for m in range(8):
        rows_o[m, :3, :] = rows[m * 3 : m * 3 + 3]
        rows_o[m, 3:, :] = jnp.zeros((5, 256), F32)


def final_body(rows, qkv_o, out_o):
    for first, last, to in ((0, 96, 0), (96, 128, D), (224, 256, D + 256)):
        width = last - first
        for m in range(8):
            qkv_o[:, to + m * width : to + m * width + width] = rows[m, :3, first:last]
    for m in range(8):
        out_o[:, m * 96 : m * 96 + 96] = rows[m, :3, 128:224]


def shards(patches, stem_weight, norm_gain, w_qkv, w_out, per_head_scale, positions, d_out):
    tiles = patches[0]
    grad_out = d_out[0]
    by_rest, by_member, place, fold = orders()
    bands = lax.axis_size(BAND)
    arrived = lax.ppermute(tiles[:TC], BAND, [(i, i - 1) for i in range(1, bands)])
    tiles_mine = lax.all_gather(tiles, ("yh", "yl"), axis=0, tiled=True)
    gain = norm_gain.reshape(1, D)
    tokens, hidden, key, kv_own, ring_own = call(
        stem_body,
        [
            ((TOK, D), B16),
            ((TOK, D), B16),
            ((256, TOK), F32),
            ((KV, TOK), B16),
            ((D, 2 * TOK), B16),
        ],
        pieces={1: 8, 3: 2, 6: 2},
        columns={3: (D, D + KV)},
    )(tiles, stem_weight.reshape(-1, D), arrived, w_qkv, gain, grad_out, by_rest)
    moved = [passed_along(kv_own, offset) for offset in range(1, 4)]
    moved[0], hidden = lax.optimization_barrier((moved[0], hidden))
    query, query_n, do = call(
        query_body,
        [((D, TOK), F32), ((D, TOK), B16), ((D, TOK), B16)],
        pieces={2: 2, 3: 2},
        columns={2: (0, D)},
    )(hidden, grad_out, w_qkv, w_out)
    ring_mine = lax.all_gather(ring_own, ("yh", "yl"), axis=0, tiled=False)
    own_block = lax.axis_index(BLK).astype(jnp.int32).reshape(1)
    attn, d_q, own, back1, back2, back3 = call(
        attend_body,
        [((D, TOK), B16), ((D, TOK), B16), ((KV, TOK), F32)] + [((KV, TOK), B16)] * 3,
        smem=(0, 1),
    )(own_block, per_head_scale, positions.reshape(64, TOK), kv_own, *moved, query_n, do, query)
    returned = [passed_along(piece, -(j + 1)) for j, piece in enumerate((back1, back2, back3))]
    returned[0], d_q = lax.optimization_barrier((returned[0], d_q))
    part = call(part_body, [((TOK, D), F32)], pieces={0: 2}, columns={0: (0, D)})(w_qkv, d_q)[0]
    late = call(
        tokens_body,
        [((8, 368, TOK), B16)],
        scratch=[pltpu.VMEM((KV, TOK), B16)],
        pieces={5: 2, 10: 2},
        columns={5: (D, D + KV)},
    )(own, *returned, key, w_qkv, tokens, gain, part, grad_out, by_member, attn, d_q)[0]
    late_ring = exchange(late, RING)
    tiles_mine, ring_mine, late = lax.optimization_barrier((tiles_mine, ring_mine, late))
    tiles_other = lax.ppermute(tiles_mine, "c", [(0, 1), (1, 0)])
    ring_other = lax.ppermute(ring_mine, "c", [(0, 1), (1, 0)])
    core = lax.axis_index("c").astype(jnp.int32).reshape(1)
    terms = call(
        terms_body,
        [((512, 896), B16)],
        scratch=[
            pltpu.VMEM((8, 192, TOK), B16),
            pltpu.VMEM((8, 256, 256), B16),
            pltpu.VMEM((2, 512, 1024), B16),
        ],
        smem=(0,),
        pieces={1: 2, 3: 4, 4: 4, 5: 2, 6: 2},
    )(core, late_ring, place, ring_mine, ring_other, tiles_mine, tiles_other, fold)[0]
    stem_total, gain_total, row_total = call(
        total_body, [((3, 2, 1024), F32), ((1, D), F32), ((8, 8, 256), F32)], pieces={0: 4}
    )(exchange(terms.reshape(32, 16, 896), REST))
    d_w_qkv, d_w_out = call(final_body, [((3, 1280), F32), ((3, D), F32)])(
        exchange(row_total, RING)
    )
    own_column = (lax.axis_index(BLK) * 4 + lax.axis_index(BAND)) * 3
    d_norm_gain = lax.dynamic_slice_in_dim(gain_total[0], own_column, 3)
    d_stem_weight = stem_total.transpose(1, 2, 0)
    return (d_stem_weight, d_norm_gain, d_w_qkv, d_w_out.T)


def solution(mesh):
    fine = Mesh(mesh.devices.reshape(2, 4, 8, 2, 2), BLK + BAND)
    placed = (P(BAND, BLK, None), P(), P(), P(), P(), P(), P(), P(BAND, BLK, None))
    every = BLK + BAND
    return jax.shard_map(
        shards,
        mesh=fine,
        in_specs=placed,
        out_specs=(P(None, None, every), P(every), P(every, None), P(None, every)),
        check_vma=False,
    )
```

```python
import jax
import jax.numpy as jnp
import numpy as np
from jax import lax
from jax.experimental import pallas as pl
from jax.experimental.pallas import tpu as pltpu
from jax.sharding import Mesh, PartitionSpec as P

QUERY_HEADS = 12
KEY_VALUE_HEADS = 4
HEAD_SIZE = 64
TC = 16
D = 768
KV = 512
TOK = 128
BLK = ("yl", "x", "z")
BAND = ("yh", "c")
RING = ("yl", "yh", "c")
REST = ("x", "z")
F32 = jnp.float32
B16 = jnp.bfloat16
NN = (((1,), (0,)), ((), ()))
NT = (((1,), (1,)), ((), ()))
TN = (((0,), (0,)), ((), ()))


def dot(a, b, dims=NN):
    return lax.dot_general(a, b, dims, preferred_element_type=F32)


def passed_along(x, by):
    peers = lax.axis_size(BLK)
    return lax.ppermute(x, BLK, [(i, (i + by) % peers) for i in range(peers)])


def exchange(x, axes):
    return lax.all_to_all(x, axes, split_axis=0, concat_axis=0, tiled=True)


def member_order():
    column = np.arange(D).reshape(2, 32, 4, 3).transpose(0, 2, 1, 3).reshape(-1)
    return jnp.asarray(np.eye(D, dtype=np.float32)[column], B16)


class Loaded:
    def __init__(self, ref, pieces):
        self.ref, self.pieces = ref, pieces

    def piece(self, i):
        copy, place = self.pieces[i]
        if copy is not None:
            copy.wait()
            self.pieces[i] = (None, place)
        return self.ref.at[place]

    def __getitem__(self, index):
        for i in range(len(self.pieces)):
            self.piece(i)
        return self.ref[index]


def split(shape, count):
    rows = shape[0] // count
    return [slice(i * rows, i * rows + rows) for i in range(count)]


def call(body, outs, scratch=(), smem=(), pieces=None, columns=None, limit=64, flops=10**9):
    pieces, columns = pieces or {}, columns or {}

    def run(*operands):
        held, parts, total = [], [], 0
        for i, operand in enumerate(operands):
            if i in smem:
                continue
            shape = operand.shape
            if i in columns:
                shape = (shape[0], columns[i][1] - columns[i][0])
            held.append(pltpu.VMEM(shape, operand.dtype))
            parts.append((i, split(shape, pieces.get(i, 1))))
            total += pieces.get(i, 1)

        def kernel(*refs):
            inputs = list(refs[: len(operands)])
            others = refs[len(operands) : len(refs) - len(held) - 1]
            stores, sems = refs[len(refs) - len(held) - 1 : -1], refs[-1]
            used = 0
            for (i, places), store in zip(parts, stores):
                source = inputs[i]
                if i in columns:
                    source = source.at[:, columns[i][0] : columns[i][1]]
                made = []
                for place in places:
                    copy = pltpu.make_async_copy(
                        source.at[place], store.at[place], sems.at[used]
                    )
                    copy.start()
                    made.append((copy, place))
                    used += 1
                inputs[i] = Loaded(store, made)
            body(*inputs, *others)
            for value in inputs:
                if isinstance(value, Loaded):
                    for j in range(len(value.pieces)):
                        value.piece(j)

        shapes = [jax.ShapeDtypeStruct(shape, kind) for shape, kind in outs]
        return pl.pallas_call(
            kernel,
            out_shape=shapes,
            in_specs=[
                pl.BlockSpec(memory_space=pltpu.SMEM if i in smem else pl.ANY)
                for i in range(len(operands))
            ],
            out_specs=[pl.BlockSpec(memory_space=pltpu.VMEM)] * len(shapes),
            scratch_shapes=[*scratch, *held, pltpu.SemaphoreType.DMA((total,))],
            compiler_params=pltpu.CompilerParams(vmem_limit_bytes=limit * 2**20),
            cost_estimate=pl.CostEstimate(
                flops=flops, bytes_accessed=4 * 2**20, transcendentals=0
            ),
        )(*operands)

    return run


def stem_body(
    tiles, stem_w, arrived, w_kv, gain, d_out, tokens_o, hidden_o, key_o, kv_o, ring_o
):
    own = tiles[...]
    deep = own.shape[1] // 4
    below = jnp.concatenate([own[TC:], arrived[...]], axis=0)
    stem = jnp.zeros((TOK, D), F32)
    for j, rows in enumerate((own, below)):
        for i in range(4):
            columns = rows[:, i * deep : i * deep + deep]
            stem = stem + dot(columns, stem_w.piece(4 * j + i)[...])
    low = stem.astype(B16)
    tokens_o[...] = low
    tok = low.astype(F32)
    factor = lax.rsqrt(jnp.mean(tok * tok, axis=1, keepdims=True) + 1e-05)
    hidden = (tok * factor * gain[...].astype(F32)).astype(B16)
    hidden_o[...] = hidden
    kv = dot(hidden, w_kv[...]).T
    key_o[...] = kv[:256]
    for h in range(KEY_VALUE_HEADS):
        k = kv[h * 64 : h * 64 + 64]
        scale = lax.rsqrt(jnp.mean(k * k, axis=0, keepdims=True) + 1e-06)
        kv_o[h * 64 : h * 64 + 64, :] = (k * scale).astype(B16)
    kv_o[256:, :] = kv[256:].astype(B16)
    ring_o[:, :TOK] = hidden.astype(F32).T.astype(B16)
    ring_o[:, TOK:] = d_out[...].astype(F32).T.astype(B16)


def query_body(hidden, d_out, w_q, w_out, query_o, query_n_o, do_o):
    h = hidden[...]
    g = d_out[...]
    q = dot(h, w_q[...]).T
    query_o[...] = q
    for i in range(QUERY_HEADS):
        part = q[i * 64 : i * 64 + 64]
        scale = lax.rsqrt(jnp.mean(part * part, axis=0, keepdims=True) + 1e-06)
        query_n_o[i * 64 : i * 64 + 64, :] = (part * scale).astype(B16)
    do_o[...] = dot(w_out[...], g, NT).astype(B16)


def attend_body(
    own_block, scales, positions, kv0, kv1, kv2, kv3, query_n, do, query,
    attn_o, dq_o, own_o, back1_o, back2_o, back3_o,
):
    own = own_block[0]
    blocks = (kv0, kv1, kv2, kv3)
    positions[:8]
    rows = positions.ref
    q_pos = rows[pl.ds(own, 1), :]
    columns = []
    for j in range(4):
        row = rows[pl.ds(lax.rem(own - j + 64, 64), 1), :].astype(F32)
        columns.append(jnp.broadcast_to(row, (TOK, TOK)).T)
    key_pos = jnp.concatenate(columns, axis=0)
    bias = jnp.where(key_pos <= q_pos.astype(F32), 0.0, -1e30)
    bias = jnp.concatenate([bias] * 3, axis=1)
    for g in range(KEY_VALUE_HEADS):
        k = jnp.concatenate([b[g * 64 : g * 64 + 64, :] for b in blocks], axis=1)
        v = jnp.concatenate([b[256 + g * 64 : 320 + g * 64, :] for b in blocks], axis=1)
        heads = [3 * g + i for i in range(3)]
        q = jnp.concatenate([query_n[h * 64 : h * 64 + 64, :] for h in heads], axis=1)
        dy = jnp.concatenate([do[h * 64 : h * 64 + 64, :] for h in heads], axis=1)
        scale = jnp.concatenate([jnp.full((1, TOK), scales[h], F32) for h in heads], axis=1)
        scores = dot(k, q, TN) * scale
        scores = jnp.where(bias < 0.0, -1e30, scores)
        top = jnp.max(scores, axis=0, keepdims=True)
        weights = jnp.exp(scores - top)
        probs = weights * (1.0 / jnp.sum(weights, axis=0, keepdims=True))
        low = probs.astype(B16)
        attn = dot(v, low)
        delta = jnp.sum(dy.astype(F32) * attn, axis=0, keepdims=True)
        dprobs = dot(v, dy, TN)
        dscores = (scale * probs * (dprobs - delta)).astype(B16)
        dq = dot(k, dscores)
        dk = dot(q, dscores, NT)
        dv = dot(dy, low, NT)
        for i, h in enumerate(heads):
            rows = slice(h * 64, h * 64 + 64)
            lanes = slice(i * TOK, i * TOK + TOK)
            attn_o[rows, :] = attn[:, lanes].astype(B16)
            x = query[rows, :]
            dx = dq[:, lanes]
            r = lax.rsqrt(jnp.mean(x * x, axis=0, keepdims=True) + 1e-06)
            inner = jnp.mean(x * dx, axis=0, keepdims=True)
            dq_o[rows, :] = (r * dx - x * (r * r * r * inner)).astype(B16)
        own_o[g * 64 : g * 64 + 64, :] = dk[:, :TOK]
        own_o[256 + g * 64 : 320 + g * 64, :] = dv[:, :TOK]
        for j, back in enumerate((back1_o, back2_o, back3_o)):
            lanes = slice((j + 1) * TOK, (j + 2) * TOK)
            back[g * 64 : g * 64 + 64, :] = dk[:, lanes].astype(B16)
            back[256 + g * 64 : 320 + g * 64, :] = dv[:, lanes].astype(B16)


def part_body(w_q, dq, part_o):
    part_o[...] = dot(w_q[...], dq[...]).T


def tokens_body(
    own, back1, back2, back3, key, w_kv, tokens, gain, part, d_out, by_member, attn, dq,
    late_o, dkv_s,
):
    total = own[...] + back1[...].astype(F32) + back2[...].astype(F32) + back3[...].astype(F32)
    for h in range(KEY_VALUE_HEADS):
        rows = slice(h * 64, h * 64 + 64)
        x = key[rows, :]
        dx = total[rows]
        r = lax.rsqrt(jnp.mean(x * x, axis=0, keepdims=True) + 1e-06)
        inner = jnp.mean(x * dx, axis=0, keepdims=True)
        dkv_s[rows, :] = (r * dx - x * (r * r * r * inner)).astype(B16)
    dkv_s[256:, :] = total[256:].astype(B16)
    d_hidden = part[...] + dot(w_kv[...], dkv_s[...]).T
    tok = tokens[...].astype(F32)
    r = lax.rsqrt(jnp.mean(tok * tok, axis=1, keepdims=True) + 1e-05)
    gain_term = jnp.sum(d_hidden * (tok * r), axis=0, keepdims=True)
    dx = d_hidden * gain[...].astype(F32)
    inner = jnp.mean(tok * dx, axis=1, keepdims=True)
    d_tokens = (d_out[...].astype(F32) + (r * dx - tok * (r * r * r * inner))).astype(B16)
    spread = dot(by_member[...], d_tokens, NT).astype(B16)
    gains = jnp.concatenate(
        [gain_term[:, i * TOK : i * TOK + TOK] for i in range(6)] + [jnp.zeros((10, TOK), F32)],
        axis=0,
    ).astype(B16)
    for m in range(8):
        late_o[m, :96, :] = spread[m * 96 : m * 96 + 96]
        late_o[m, 96:128, :] = dkv_s[m * 32 : m * 32 + 32, :]
        late_o[m, 128:160, :] = dkv_s[256 + m * 32 : 288 + m * 32, :]
        late_o[m, 160:176, :] = gains
        late_o[m, 176:272, :] = attn[m * 96 : m * 96 + 96, :]
        late_o[m, 272:, :] = dq[m * 96 : m * 96 + 96, :]


def terms_body(
    core, late, ring0, ring1, tiles0, tiles1, terms_o, pair_s, rhs_s, both_s, sums_s, all_s
):
    lane = lax.broadcasted_iota(jnp.int32, (96, TOK), 1)
    gain = jnp.zeros((16, TOK), F32)
    zero = jnp.zeros((TOK, TOK), B16)
    for yl in range(2):
        before = jnp.zeros((96, TOK), F32)
        for band in range(4):
            m = yl * 4 + band
            block = late[m, :96, :]
            gain = gain + late[m, 160:176, :].astype(F32)
            moved = pltpu.roll(block.astype(F32), TC, 1)
            pair_s[m, :96, :] = block
            pair_s[m, 96:, :] = jnp.where(lane < TC, before, moved).astype(B16)
            before = moved
            rhs_s[m, :96, :TOK] = late[m, 272:, :]
            rhs_s[m, 96:128, :TOK] = late[m, 96:128, :]
            rhs_s[m, :128, TOK:] = zero
            rhs_s[m, 128:224, :TOK] = zero[:96]
            rhs_s[m, 128:224, TOK:] = late[m, 176:272, :]
            rhs_s[m, 224:, :TOK] = late[m, 128:160, :]
            rhs_s[m, 224:, TOK:] = zero[:32]
    rows = jnp.zeros((D, 256), F32)
    for s, ring in enumerate((ring0, ring1)):
        side = lax.rem(core[0] + s, 2)
        for j in range(4):
            m = (j % 2) * 4 + (j // 2) * 2 + side
            at = s * 4 + j
            both_s[:, at * TOK : at * TOK + TOK] = pair_s[m]
            rows = rows + dot(ring.piece(j)[0], rhs_s[m], NT)
    for half in range(2):
        sums_s[half] = rows[:, half * TOK : half * TOK + TOK]
        for i in range(24):
            picked = sums_s[half, pl.ds(i // 12 * 384 + i % 12, 32, stride=12), :]
            all_s[pl.ds(48 + half * 24 + i, 32, stride=104), :] = picked
    for i in range(8):
        row = gain[i : i + 1, :]
        all_s[pl.ds(96 + i, 32, stride=104), :] = jnp.broadcast_to(row, (32, TOK))
    stem = dot(both_s[:, :512], tiles0[...]) + dot(both_s[:, 512:], tiles1[...])
    for c in range(8):
        sums_s[0, :192, :] = stem[:, c * TOK : c * TOK + TOK]
        for i in range(6):
            picked = sums_s[0, pl.ds(i // 3 * 96 + i % 3, 32, stride=3), :]
            all_s[pl.ds(i * 8 + c, 32, stride=104), :] = picked
    terms_o[...] = all_s[...].astype(B16)


def total_body(terms, stem_o, gain_o, rows_o):
    total = jnp.zeros((104, TOK), F32)
    for piece in range(4):
        block = terms.piece(piece)
        for r in range(8):
            total = total + block[r].astype(F32)
    for j in range(2):
        for k in range(3):
            for c in range(8):
                at = (j * 3 + k) * 8 + c
                stem_o[k, j : j + 1, c * TOK : c * TOK + TOK] = total[at : at + 1]
    for c in range(6):
        gain_o[:, c * TOK : c * TOK + TOK] = total[96 + c : 97 + c]
    for half in range(2):
        lanes = slice(half * TOK, half * TOK + TOK)
        for m in range(8):
            at = 48 + half * 24 + m * 3
            rows_o[m, :3, lanes] = total[at : at + 3]
            rows_o[m, 3:, lanes] = jnp.zeros((5, TOK), F32)


def final_body(rows, qkv_o, out_o):
    for first, last, to in ((0, 96, 0), (96, 128, D), (224, 256, D + 256)):
        width = last - first
        for m in range(8):
            qkv_o[:, to + m * width : to + m * width + width] = rows[m, :3, first:last]
    for m in range(8):
        out_o[:, m * 96 : m * 96 + 96] = rows[m, :3, 128:224]


def shards(patches, stem_weight, norm_gain, w_qkv, w_out, per_head_scale, positions, d_out):
    tiles = patches[0]
    grad_out = d_out[0]
    by_member = member_order()
    bands = lax.axis_size(BAND)
    arrived = lax.ppermute(tiles[:TC], BAND, [(i, i - 1) for i in range(1, bands)])
    tiles_mine = lax.all_gather(tiles, ("yh", "yl"), axis=0, tiled=True)
    gain = norm_gain.reshape(1, D)
    tokens, hidden, key, kv_own, ring_own = call(
        stem_body,
        [
            ((TOK, D), B16),
            ((TOK, D), B16),
            ((256, TOK), F32),
            ((KV, TOK), B16),
            ((D, 2 * TOK), B16),
        ],
        pieces={1: 8, 3: 2},
        columns={3: (D, D + KV)},
    )(tiles, stem_weight.reshape(-1, D), arrived, w_qkv, gain, grad_out)
    moved = [passed_along(kv_own, offset) for offset in range(1, 4)]
    moved[0], hidden = lax.optimization_barrier((moved[0], hidden))
    query, query_n, do = call(
        query_body,
        [((D, TOK), F32), ((D, TOK), B16), ((D, TOK), B16)],
        pieces={2: 2, 3: 2},
        columns={2: (0, D)},
    )(hidden, grad_out, w_qkv, w_out)
    ring_mine = lax.all_gather(ring_own, ("yh", "yl"), axis=0, tiled=False)
    own_block = lax.axis_index(BLK).astype(jnp.int32).reshape(1)
    attn, d_q, own, back1, back2, back3 = call(
        attend_body,
        [((D, TOK), B16), ((D, TOK), B16), ((KV, TOK), F32)] + [((KV, TOK), B16)] * 3,
        smem=(0, 1),
    )(own_block, per_head_scale, positions.reshape(64, TOK), kv_own, *moved, query_n, do, query)
    returned = [passed_along(piece, -(j + 1)) for j, piece in enumerate((back1, back2, back3))]
    returned[0], d_q = lax.optimization_barrier((returned[0], d_q))
    part = call(part_body, [((TOK, D), F32)], pieces={0: 2}, columns={0: (0, D)})(w_qkv, d_q)[0]
    late = call(
        tokens_body,
        [((8, 368, TOK), B16)],
        scratch=[pltpu.VMEM((KV, TOK), B16)],
        pieces={5: 2, 10: 2},
        columns={5: (D, D + KV)},
    )(own, *returned, key, w_qkv, tokens, gain, part, grad_out, by_member, attn, d_q)[0]
    late_ring = exchange(late, RING)
    tiles_mine, ring_mine, late = lax.optimization_barrier((tiles_mine, ring_mine, late))
    tiles_other = lax.ppermute(tiles_mine, "c", [(0, 1), (1, 0)])
    ring_other = lax.ppermute(ring_mine, "c", [(0, 1), (1, 0)])
    core = lax.axis_index("c").astype(jnp.int32).reshape(1)
    terms = call(
        terms_body,
        [((32 * 104, TOK), B16)],
        scratch=[
            pltpu.VMEM((8, 192, TOK), B16),
            pltpu.VMEM((8, 256, 256), B16),
            pltpu.VMEM((192, 1024), B16),
            pltpu.VMEM((2, D, TOK), F32),
            pltpu.VMEM((32 * 104, TOK), F32),
        ],
        smem=(0,),
        pieces={2: 4, 3: 4, 4: 2, 5: 2},
    )(core, late_ring, ring_mine, ring_other, tiles_mine, tiles_other)[0]
    stem_total, gain_total, row_total = call(
        total_body,
        [((3, 2, 1024), F32), ((1, D), F32), ((8, 8, 256), F32)],
        pieces={0: 4},
        limit=16,
    )(exchange(terms.reshape(32, 104, TOK), REST))
    d_w_qkv, d_w_out = call(final_body, [((3, 1280), F32), ((3, D), F32)], limit=16)(
        exchange(row_total, RING)
    )
    own_column = (lax.axis_index(BLK) * 4 + lax.axis_index(BAND)) * 3
    d_norm_gain = lax.dynamic_slice_in_dim(gain_total[0], own_column, 3)
    d_stem_weight = stem_total.transpose(1, 2, 0)
    return (d_stem_weight, d_norm_gain, d_w_qkv, d_w_out.T)


def solution(mesh):
    fine = Mesh(mesh.devices.reshape(2, 4, 8, 2, 2), BLK + BAND)
    placed = (P(BAND, BLK, None), P(), P(), P(), P(), P(), P(), P(BAND, BLK, None))
    every = BLK + BAND
    return jax.shard_map(
        shards,
        mesh=fine,
        in_specs=placed,
        out_specs=(P(None, None, every), P(every), P(every, None), P(None, every)),
        check_vma=False,
    )
```

```python
import jax
import jax.numpy as jnp
import numpy as np
from jax import lax
from jax.experimental import pallas as pl
from jax.experimental.pallas import tpu as pltpu
from jax.sharding import Mesh, PartitionSpec as P

QUERY_HEADS = 12
KEY_VALUE_HEADS = 4
HEAD_SIZE = 64
TC = 16
D = 768
KV = 512
TOK = 128
BLK = ("yl", "x", "z")
BAND = ("yh", "c")
RING = ("yl", "yh", "c")
CHIPS = ("yl", "yh")
REST = ("x", "z")
F32 = jnp.float32
B16 = jnp.bfloat16
NN = (((1,), (0,)), ((), ()))
NT = (((1,), (1,)), ((), ()))
TN = (((0,), (0,)), ((), ()))


def dot(a, b, dims=NN):
    return lax.dot_general(a, b, dims, preferred_element_type=F32)


def passed_along(x, by):
    peers = lax.axis_size(BLK)
    return lax.ppermute(x, BLK, [(i, (i + by) % peers) for i in range(peers)])


def from_chips(x):
    order = [0, 2, 1, 3]
    return [
        lax.ppermute(x, CHIPS, [(order[i], order[(i + by) % 4]) for i in range(4)])
        for by in range(1, 4)
    ]


def other_core(x):
    return lax.ppermute(x, "c", [(0, 1), (1, 0)])


def exchange(x, axes):
    return lax.all_to_all(x, axes, split_axis=0, concat_axis=0, tiled=True)


def member_order():
    column = np.arange(D).reshape(2, 32, 4, 3).transpose(0, 2, 1, 3).reshape(-1)
    return jnp.asarray(np.eye(D, dtype=np.float32)[column], B16)


class Loaded:
    def __init__(self, ref, pieces):
        self.ref, self.pieces = ref, pieces

    def piece(self, i):
        copy, place = self.pieces[i]
        if copy is not None:
            copy.wait()
            self.pieces[i] = (None, place)
        return self.ref.at[place]

    def __getitem__(self, index):
        for i in range(len(self.pieces)):
            self.piece(i)
        return self.ref[index]


def split(shape, count):
    rows = shape[0] // count
    return [slice(i * rows, i * rows + rows) for i in range(count)]


def call(body, outs, scratch=(), smem=(), pieces=None, columns=None, limit=64, flops=10**9):
    pieces, columns = pieces or {}, columns or {}

    def run(*operands):
        held, parts, total = [], [], 0
        for i, operand in enumerate(operands):
            if i in smem:
                continue
            shape = operand.shape
            if i in columns:
                shape = (shape[0], columns[i][1] - columns[i][0])
            held.append(pltpu.VMEM(shape, operand.dtype))
            parts.append((i, split(shape, pieces.get(i, 1))))
            total += pieces.get(i, 1)

        def kernel(*refs):
            inputs = list(refs[: len(operands)])
            others = refs[len(operands) : len(refs) - len(held) - 1]
            stores, sems = refs[len(refs) - len(held) - 1 : -1], refs[-1]
            used = 0
            for (i, places), store in zip(parts, stores):
                source = inputs[i]
                if i in columns:
                    source = source.at[:, columns[i][0] : columns[i][1]]
                made = []
                for place in places:
                    copy = pltpu.make_async_copy(
                        source.at[place], store.at[place], sems.at[used]
                    )
                    copy.start()
                    made.append((copy, place))
                    used += 1
                inputs[i] = Loaded(store, made)
            body(*inputs, *others)
            for value in inputs:
                if isinstance(value, Loaded):
                    for j in range(len(value.pieces)):
                        value.piece(j)

        shapes = [jax.ShapeDtypeStruct(shape, kind) for shape, kind in outs]
        return pl.pallas_call(
            kernel,
            out_shape=shapes,
            in_specs=[
                pl.BlockSpec(memory_space=pltpu.SMEM if i in smem else pl.ANY)
                for i in range(len(operands))
            ],
            out_specs=[pl.BlockSpec(memory_space=pltpu.VMEM)] * len(shapes),
            scratch_shapes=[*scratch, *held, pltpu.SemaphoreType.DMA((total,))],
            compiler_params=pltpu.CompilerParams(vmem_limit_bytes=limit * 2**20),
            cost_estimate=pl.CostEstimate(
                flops=flops, bytes_accessed=4 * 2**20, transcendentals=0
            ),
        )(*operands)

    return run


def stem_body(
    tiles, stem_w, arrived, w_kv, gain, d_out, tokens_o, hidden_o, key_o, kv_o, ring_o
):
    own = tiles[...]
    deep = own.shape[1] // 4
    below = jnp.concatenate([own[TC:], arrived[...]], axis=0)
    stem = jnp.zeros((TOK, D), F32)
    for j, rows in enumerate((own, below)):
        for i in range(4):
            columns = rows[:, i * deep : i * deep + deep]
            stem = stem + dot(columns, stem_w.piece(4 * j + i)[...])
    low = stem.astype(B16)
    tokens_o[...] = low
    tok = low.astype(F32)
    factor = lax.rsqrt(jnp.mean(tok * tok, axis=1, keepdims=True) + 1e-05)
    hidden = (tok * factor * gain[...].astype(F32)).astype(B16)
    hidden_o[...] = hidden
    kv = dot(hidden, w_kv[...]).T
    key_o[...] = kv[:256]
    for h in range(KEY_VALUE_HEADS):
        k = kv[h * 64 : h * 64 + 64]
        scale = lax.rsqrt(jnp.mean(k * k, axis=0, keepdims=True) + 1e-06)
        kv_o[h * 64 : h * 64 + 64, :] = (k * scale).astype(B16)
    kv_o[256:, :] = kv[256:].astype(B16)
    ring_o[:, :TOK] = hidden.astype(F32).T.astype(B16)
    ring_o[:, TOK:] = d_out[...].astype(F32).T.astype(B16)


def query_body(hidden, d_out, w_q, w_out, query_o, query_n_o, do_o):
    h = hidden[...]
    g = d_out[...]
    q = dot(h, w_q[...]).T
    query_o[...] = q
    for i in range(QUERY_HEADS):
        part = q[i * 64 : i * 64 + 64]
        scale = lax.rsqrt(jnp.mean(part * part, axis=0, keepdims=True) + 1e-06)
        query_n_o[i * 64 : i * 64 + 64, :] = (part * scale).astype(B16)
    do_o[...] = dot(w_out[...], g, NT).astype(B16)


def attend_body(
    own_block, scales, positions, kv0, kv1, kv2, kv3, query_n, do, query,
    attn_o, dq_o, own_o, back1_o, back2_o, back3_o,
):
    own = own_block[0]
    blocks = (kv0, kv1, kv2, kv3)
    positions[:8]
    rows = positions.ref
    q_pos = rows[pl.ds(own, 1), :]
    columns = []
    for j in range(4):
        row = rows[pl.ds(lax.rem(own - j + 64, 64), 1), :].astype(F32)
        columns.append(jnp.broadcast_to(row, (TOK, TOK)).T)
    key_pos = jnp.concatenate(columns, axis=0)
    bias = jnp.where(key_pos <= q_pos.astype(F32), 0.0, -1e30)
    bias = jnp.concatenate([bias] * 3, axis=1)
    for g in range(KEY_VALUE_HEADS):
        k = jnp.concatenate([b[g * 64 : g * 64 + 64, :] for b in blocks], axis=1)
        v = jnp.concatenate([b[256 + g * 64 : 320 + g * 64, :] for b in blocks], axis=1)
        heads = [3 * g + i for i in range(3)]
        q = jnp.concatenate([query_n[h * 64 : h * 64 + 64, :] for h in heads], axis=1)
        dy = jnp.concatenate([do[h * 64 : h * 64 + 64, :] for h in heads], axis=1)
        scale = jnp.concatenate([jnp.full((1, TOK), scales[h], F32) for h in heads], axis=1)
        scores = dot(k, q, TN) * scale
        scores = jnp.where(bias < 0.0, -1e30, scores)
        top = jnp.max(scores, axis=0, keepdims=True)
        weights = jnp.exp(scores - top)
        probs = weights * (1.0 / jnp.sum(weights, axis=0, keepdims=True))
        low = probs.astype(B16)
        attn = dot(v, low)
        delta = jnp.sum(dy.astype(F32) * attn, axis=0, keepdims=True)
        dprobs = dot(v, dy, TN)
        dscores = (scale * probs * (dprobs - delta)).astype(B16)
        dq = dot(k, dscores)
        dk = dot(q, dscores, NT)
        dv = dot(dy, low, NT)
        for i, h in enumerate(heads):
            rows = slice(h * 64, h * 64 + 64)
            lanes = slice(i * TOK, i * TOK + TOK)
            attn_o[rows, :] = attn[:, lanes].astype(B16)
            x = query[rows, :]
            dx = dq[:, lanes]
            r = lax.rsqrt(jnp.mean(x * x, axis=0, keepdims=True) + 1e-06)
            inner = jnp.mean(x * dx, axis=0, keepdims=True)
            dq_o[rows, :] = (r * dx - x * (r * r * r * inner)).astype(B16)
        own_o[g * 64 : g * 64 + 64, :] = dk[:, :TOK]
        own_o[256 + g * 64 : 320 + g * 64, :] = dv[:, :TOK]
        for j, back in enumerate((back1_o, back2_o, back3_o)):
            lanes = slice((j + 1) * TOK, (j + 2) * TOK)
            back[g * 64 : g * 64 + 64, :] = dk[:, lanes].astype(B16)
            back[256 + g * 64 : 320 + g * 64, :] = dv[:, lanes].astype(B16)


def part_body(w_q, dq, part_o):
    part_o[...] = dot(w_q[...], dq[...]).T


def tokens_body(
    own, back1, back2, back3, key, w_kv, tokens, gain, part, d_out, by_member, attn, dq,
    late_o, dkv_s,
):
    total = own[...] + back1[...].astype(F32) + back2[...].astype(F32) + back3[...].astype(F32)
    for h in range(KEY_VALUE_HEADS):
        rows = slice(h * 64, h * 64 + 64)
        x = key[rows, :]
        dx = total[rows]
        r = lax.rsqrt(jnp.mean(x * x, axis=0, keepdims=True) + 1e-06)
        inner = jnp.mean(x * dx, axis=0, keepdims=True)
        dkv_s[rows, :] = (r * dx - x * (r * r * r * inner)).astype(B16)
    dkv_s[256:, :] = total[256:].astype(B16)
    d_hidden = part[...] + dot(w_kv[...], dkv_s[...]).T
    tok = tokens[...].astype(F32)
    r = lax.rsqrt(jnp.mean(tok * tok, axis=1, keepdims=True) + 1e-05)
    gain_term = jnp.sum(d_hidden * (tok * r), axis=0, keepdims=True)
    dx = d_hidden * gain[...].astype(F32)
    inner = jnp.mean(tok * dx, axis=1, keepdims=True)
    d_tokens = (d_out[...].astype(F32) + (r * dx - tok * (r * r * r * inner))).astype(B16)
    spread = dot(by_member[...], d_tokens, NT).astype(B16)
    gains = jnp.concatenate(
        [gain_term[:, i * TOK : i * TOK + TOK] for i in range(6)] + [jnp.zeros((10, TOK), F32)],
        axis=0,
    ).astype(B16)
    for m in range(8):
        late_o[m, :96, :] = spread[m * 96 : m * 96 + 96]
        late_o[m, 96:128, :] = dkv_s[m * 32 : m * 32 + 32, :]
        late_o[m, 128:160, :] = dkv_s[256 + m * 32 : 288 + m * 32, :]
        late_o[m, 160:176, :] = gains
        late_o[m, 176:272, :] = attn[m * 96 : m * 96 + 96, :]
        late_o[m, 272:, :] = dq[m * 96 : m * 96 + 96, :]


def terms_body(
    place, late, *rest
):
    rings, tiles = rest[:8], rest[8:16]
    terms_o, pair_s, rhs_s, sums_s, all_s = rest[16:]
    lane = lax.broadcasted_iota(jnp.int32, (96, TOK), 1)
    gain = jnp.zeros((16, TOK), F32)
    zero = jnp.zeros((TOK, TOK), B16)
    for yl in range(2):
        before = jnp.zeros((96, TOK), F32)
        for band in range(4):
            m = yl * 4 + band
            block = late[m, :96, :]
            gain = gain + late[m, 160:176, :].astype(F32)
            moved = pltpu.roll(block.astype(F32), TC, 1)
            pair_s[m, :96, :] = block
            pair_s[m, 96:, :] = jnp.where(lane < TC, before, moved).astype(B16)
            before = moved
            rhs_s[m, :96, :TOK] = late[m, 272:, :]
            rhs_s[m, 96:128, :TOK] = late[m, 96:128, :]
            rhs_s[m, :128, TOK:] = zero
            rhs_s[m, 128:224, :TOK] = zero[:96]
            rhs_s[m, 128:224, TOK:] = late[m, 176:272, :]
            rhs_s[m, 224:, :TOK] = late[m, 128:160, :]
            rhs_s[m, 224:, TOK:] = zero[:32]
    rows = jnp.zeros((D, 256), F32)
    members = []
    for side in range(2):
        for back in range(4):
            chip = lax.rem(place[0] + 4 - back, 4)
            core = lax.rem(place[1] + side, 2)
            members.append(lax.rem(chip, 2) * 4 + lax.div(chip, 2) * 2 + core)
    for ring, m in zip(rings, members):
        rows = rows + dot(ring[...], rhs_s[m], NT)
    for half in range(2):
        sums_s[half] = rows[:, half * TOK : half * TOK + TOK]
        for i in range(24):
            picked = sums_s[half, pl.ds(i // 12 * 384 + i % 12, 32, stride=12), :]
            all_s[pl.ds(48 + half * 24 + i, 32, stride=104), :] = picked
    for i in range(8):
        row = gain[i : i + 1, :]
        all_s[pl.ds(96 + i, 32, stride=104), :] = jnp.broadcast_to(row, (32, TOK))
    stem = jnp.zeros((192, 1024), F32)
    for tile, m in zip(tiles, members):
        stem = stem + dot(pair_s[m], tile[...])
    for c in range(8):
        sums_s[0, :192, :] = stem[:, c * TOK : c * TOK + TOK]
        for i in range(6):
            picked = sums_s[0, pl.ds(i // 3 * 96 + i % 3, 32, stride=3), :]
            all_s[pl.ds(i * 8 + c, 32, stride=104), :] = picked
    terms_o[...] = all_s[...].astype(B16)


def total_body(terms, stem_o, gain_o, rows_o):
    total = jnp.zeros((104, TOK), F32)
    for piece in range(4):
        block = terms.piece(piece)
        for r in range(8):
            total = total + block[r].astype(F32)
    for j in range(2):
        for k in range(3):
            for c in range(8):
                at = (j * 3 + k) * 8 + c
                stem_o[k, j : j + 1, c * TOK : c * TOK + TOK] = total[at : at + 1]
    for c in range(6):
        gain_o[:, c * TOK : c * TOK + TOK] = total[96 + c : 97 + c]
    for half in range(2):
        lanes = slice(half * TOK, half * TOK + TOK)
        for m in range(8):
            at = 48 + half * 24 + m * 3
            rows_o[m, :3, lanes] = total[at : at + 3]
            rows_o[m, 3:, lanes] = jnp.zeros((5, TOK), F32)


def final_body(rows, qkv_o, out_o):
    for first, last, to in ((0, 96, 0), (96, 128, D), (224, 256, D + 256)):
        width = last - first
        for m in range(8):
            qkv_o[:, to + m * width : to + m * width + width] = rows[m, :3, first:last]
    for m in range(8):
        out_o[:, m * 96 : m * 96 + 96] = rows[m, :3, 128:224]


def shards(patches, stem_weight, norm_gain, w_qkv, w_out, per_head_scale, positions, d_out):
    tiles = patches[0]
    grad_out = d_out[0]
    by_member = member_order()
    bands = lax.axis_size(BAND)
    arrived = lax.ppermute(tiles[:TC], BAND, [(i, i - 1) for i in range(1, bands)])
    tiles_mine = from_chips(tiles)
    gain = norm_gain.reshape(1, D)
    tokens, hidden, key, kv_own, ring_own = call(
        stem_body,
        [
            ((TOK, D), B16),
            ((TOK, D), B16),
            ((256, TOK), F32),
            ((KV, TOK), B16),
            ((D, 2 * TOK), B16),
        ],
        pieces={1: 8, 3: 2},
        columns={3: (D, D + KV)},
    )(tiles, stem_weight.reshape(-1, D), arrived, w_qkv, gain, grad_out)
    moved = [passed_along(kv_own, offset) for offset in range(1, 4)]
    moved[0], hidden = lax.optimization_barrier((moved[0], hidden))
    query, query_n, do = call(
        query_body,
        [((D, TOK), F32), ((D, TOK), B16), ((D, TOK), B16)],
        pieces={2: 2, 3: 2},
        columns={2: (0, D)},
    )(hidden, grad_out, w_qkv, w_out)
    query_n, tiles_mine = lax.optimization_barrier((query_n, tiles_mine))
    own_block = lax.axis_index(BLK).astype(jnp.int32).reshape(1)
    attn, d_q, own, back1, back2, back3 = call(
        attend_body,
        [((D, TOK), B16), ((D, TOK), B16), ((KV, TOK), F32)] + [((KV, TOK), B16)] * 3,
        smem=(0, 1),
    )(own_block, per_head_scale, positions.reshape(64, TOK), kv_own, *moved, query_n, do, query)
    returned = [passed_along(piece, -(j + 1)) for j, piece in enumerate((back1, back2, back3))]
    returned[0], d_q = lax.optimization_barrier((returned[0], d_q))
    part = call(part_body, [((TOK, D), F32)], pieces={0: 2}, columns={0: (0, D)})(w_qkv, d_q)[0]
    ring_mine = from_chips(ring_own)
    ring_mine, part = lax.optimization_barrier((ring_mine, part))
    late = call(
        tokens_body,
        [((8, 368, TOK), B16)],
        scratch=[pltpu.VMEM((KV, TOK), B16)],
        pieces={5: 2, 10: 2},
        columns={5: (D, D + KV)},
    )(own, *returned, key, w_qkv, tokens, gain, part, grad_out, by_member, attn, d_q)[0]
    late_ring = exchange(late, RING)
    rings = [ring_own, *ring_mine]
    blocks = [tiles, *tiles_mine]
    rings = rings + [other_core(x) for x in rings]
    blocks = blocks + [other_core(x) for x in blocks]
    chip = lax.axis_index("yh") * 2 + lax.axis_index("yl")
    place = jnp.stack([chip, lax.axis_index("c")]).astype(jnp.int32)
    terms = call(
        terms_body,
        [((32 * 104, TOK), B16)],
        scratch=[
            pltpu.VMEM((8, 192, TOK), B16),
            pltpu.VMEM((8, 256, 256), B16),
            pltpu.VMEM((2, D, TOK), F32),
            pltpu.VMEM((32 * 104, TOK), F32),
        ],
        smem=(0,),
    )(place, late_ring, *rings, *blocks)[0]
    stem_total, gain_total, row_total = call(
        total_body,
        [((3, 2, 1024), F32), ((1, D), F32), ((8, 8, 256), F32)],
        pieces={0: 4},
        limit=16,
    )(exchange(terms.reshape(32, 104, TOK), REST))
    d_w_qkv, d_w_out = call(final_body, [((3, 1280), F32), ((3, D), F32)], limit=16)(
        exchange(row_total, RING)
    )
    own_column = (lax.axis_index(BLK) * 4 + lax.axis_index(BAND)) * 3
    d_norm_gain = lax.dynamic_slice_in_dim(gain_total[0], own_column, 3)
    d_stem_weight = stem_total.transpose(1, 2, 0)
    return (d_stem_weight, d_norm_gain, d_w_qkv, d_w_out.T)


def solution(mesh):
    fine = Mesh(mesh.devices.reshape(2, 4, 8, 2, 2), BLK + BAND)
    placed = (P(BAND, BLK, None), P(), P(), P(), P(), P(), P(), P(BAND, BLK, None))
    every = BLK + BAND
    return jax.shard_map(
        shards,
        mesh=fine,
        in_specs=placed,
        out_specs=(P(None, None, every), P(every), P(every, None), P(None, every)),
        check_vma=False,
    )
```

```python
import jax
import jax.numpy as jnp
from jax import lax
from jax.experimental import pallas as pl
from jax.experimental.pallas import tpu as pltpu
from jax.sharding import Mesh, PartitionSpec as P

QUERY_HEADS = 12
KEY_VALUE_HEADS = 4
HEAD_SIZE = 64
TC = 16
D = 768
KV = 512
TOK = 128
BLK = ("yl", "x", "z")
BAND = ("yh", "c")
RING = ("yl", "yh", "c")
CHIPS = ("yl", "yh")
REST = ("x", "z")
F32 = jnp.float32
B16 = jnp.bfloat16
NN = (((1,), (0,)), ((), ()))
NT = (((1,), (1,)), ((), ()))
TN = (((0,), (0,)), ((), ()))


def dot(a, b, dims=NN):
    return lax.dot_general(a, b, dims, preferred_element_type=F32)


def passed_along(x, by):
    peers = lax.axis_size(BLK)
    return lax.ppermute(x, BLK, [(i, (i + by) % peers) for i in range(peers)])


def from_chips(x):
    order = [0, 2, 1, 3]
    return [
        lax.ppermute(x, CHIPS, [(order[i], order[(i + by) % 4]) for i in range(4)])
        for by in range(1, 4)
    ]


def other_core(x):
    return lax.ppermute(x, "c", [(0, 1), (1, 0)])


def exchange(x, axes):
    return lax.all_to_all(x, axes, split_axis=0, concat_axis=0, tiled=True)


class Loaded:
    def __init__(self, ref, pieces):
        self.ref, self.pieces = ref, pieces

    def piece(self, i):
        copy, place = self.pieces[i]
        if copy is not None:
            copy.wait()
            self.pieces[i] = (None, place)
        return self.ref.at[place]

    def __getitem__(self, index):
        for i in range(len(self.pieces)):
            self.piece(i)
        return self.ref[index]


def split(shape, count):
    rows = shape[0] // count
    return [slice(i * rows, i * rows + rows) for i in range(count)]


def call(
    body, outs, scratch=(), smem=(), pieces=None, columns=None, joined=None, limit=64, flops=10**9
):
    pieces, columns = pieces or {}, columns or {}

    def run(*operands):
        held, parts, total = [], [], 0
        count = len(operands) if joined is None else joined
        if joined is not None:
            rows, width = operands[joined].shape
            held.append(pltpu.VMEM(((len(operands) - joined) * rows, width), operands[joined].dtype))
            total += len(operands) - joined
        for i, operand in enumerate(operands[:count]):
            if i in smem:
                continue
            shape = operand.shape
            if i in columns:
                shape = (shape[0], columns[i][1] - columns[i][0])
            held.append(pltpu.VMEM(shape, operand.dtype))
            parts.append((i, split(shape, pieces.get(i, 1))))
            total += pieces.get(i, 1)

        def kernel(*refs):
            inputs = list(refs[: len(operands)])
            others = refs[len(operands) : len(refs) - len(held) - 1]
            stores, sems = refs[len(refs) - len(held) - 1 : -1], refs[-1]
            used = 0
            if joined is not None:
                used, made = len(operands) - joined, []
                for i, place in enumerate(split(stores[0].shape, used)):
                    made.append(
                        (pltpu.make_async_copy(inputs[joined + i], stores[0].at[place], sems.at[i]), place)
                    )
                inputs[joined:] = [Loaded(stores[0], made)]
                stores = stores[1:]
            for (i, places), store in zip(parts, stores):
                source = inputs[i]
                if i in columns:
                    source = source.at[:, columns[i][0] : columns[i][1]]
                made = []
                for place in places:
                    copy = pltpu.make_async_copy(
                        source.at[place], store.at[place], sems.at[used]
                    )
                    copy.start()
                    made.append((copy, place))
                    used += 1
                inputs[i] = Loaded(store, made)
            if joined is not None:
                for copy, _ in inputs[joined].pieces:
                    copy.start()
            body(*inputs, *others)
            for value in inputs:
                if isinstance(value, Loaded):
                    for j in range(len(value.pieces)):
                        value.piece(j)

        shapes = [jax.ShapeDtypeStruct(shape, kind) for shape, kind in outs]
        return pl.pallas_call(
            kernel,
            out_shape=shapes,
            in_specs=[
                pl.BlockSpec(memory_space=pltpu.SMEM if i in smem else pl.ANY)
                for i in range(len(operands))
            ],
            out_specs=[pl.BlockSpec(memory_space=pltpu.VMEM)] * len(shapes),
            scratch_shapes=[*scratch, *held, pltpu.SemaphoreType.DMA((total,))],
            compiler_params=pltpu.CompilerParams(vmem_limit_bytes=limit * 2**20),
            cost_estimate=pl.CostEstimate(
                flops=flops, bytes_accessed=4 * 2**20, transcendentals=0
            ),
        )(*operands)

    return run


def stem_body(
    tiles, stem_w, arrived, w_kv, gain, d_out, tokens_o, hidden_o, key_o, kv_o, ring_o
):
    own = tiles[...]
    deep = own.shape[1] // 4
    below = jnp.concatenate([own[TC:], arrived[...]], axis=0)
    stem = jnp.zeros((TOK, D), F32)
    for j, rows in enumerate((own, below)):
        for i in range(4):
            columns = rows[:, i * deep : i * deep + deep]
            stem = stem + dot(columns, stem_w.piece(4 * j + i)[...])
    low = stem.astype(B16)
    tokens_o[...] = low
    tok = low.astype(F32)
    factor = lax.rsqrt(jnp.mean(tok * tok, axis=1, keepdims=True) + 1e-05)
    hidden = (tok * factor * gain[...].astype(F32)).astype(B16)
    hidden_o[...] = hidden
    kv = dot(hidden, w_kv[...]).T
    key_o[...] = kv[:256]
    for h in range(KEY_VALUE_HEADS):
        k = kv[h * 64 : h * 64 + 64]
        scale = lax.rsqrt(jnp.mean(k * k, axis=0, keepdims=True) + 1e-06)
        kv_o[h * 64 : h * 64 + 64, :] = (k * scale).astype(B16)
    kv_o[256:, :] = kv[256:].astype(B16)
    ring_o[:, :TOK] = hidden.astype(F32).T.astype(B16)
    ring_o[:, TOK:] = d_out[...].astype(F32).T.astype(B16)


def query_body(hidden, d_out, w_q, w_out, query_o, query_n_o, do_o):
    h = hidden[...]
    g = d_out[...]
    q = dot(h, w_q[...]).T
    query_o[...] = q
    for i in range(QUERY_HEADS):
        part = q[i * 64 : i * 64 + 64]
        scale = lax.rsqrt(jnp.mean(part * part, axis=0, keepdims=True) + 1e-06)
        query_n_o[i * 64 : i * 64 + 64, :] = (part * scale).astype(B16)
    do_o[...] = dot(w_out[...], g, NT).astype(B16)


def attend_body(
    own_block, scales, positions, kv0, kv1, kv2, kv3, query_n, do, query,
    attn_o, dq_o, own_o, back1_o, back2_o, back3_o,
):
    own = own_block[0]
    blocks = (kv0, kv1, kv2, kv3)
    positions[:8]
    rows = positions.ref
    q_pos = rows[pl.ds(own, 1), :]
    columns = []
    for j in range(4):
        row = rows[pl.ds(lax.rem(own - j + 64, 64), 1), :].astype(F32)
        columns.append(jnp.broadcast_to(row, (TOK, TOK)).T)
    key_pos = jnp.concatenate(columns, axis=0)
    bias = jnp.where(key_pos <= q_pos.astype(F32), 0.0, -1e30)
    bias = jnp.concatenate([bias] * 3, axis=1)
    for g in range(KEY_VALUE_HEADS):
        k = jnp.concatenate([b[g * 64 : g * 64 + 64, :] for b in blocks], axis=1)
        v = jnp.concatenate([b[256 + g * 64 : 320 + g * 64, :] for b in blocks], axis=1)
        heads = [3 * g + i for i in range(3)]
        q = jnp.concatenate([query_n[h * 64 : h * 64 + 64, :] for h in heads], axis=1)
        dy = jnp.concatenate([do[h * 64 : h * 64 + 64, :] for h in heads], axis=1)
        scale = jnp.concatenate([jnp.full((1, TOK), scales[h], F32) for h in heads], axis=1)
        scores = dot(k, q, TN) * scale
        scores = jnp.where(bias < 0.0, -1e30, scores)
        top = jnp.max(scores, axis=0, keepdims=True)
        weights = jnp.exp(scores - top)
        probs = weights * (1.0 / jnp.sum(weights, axis=0, keepdims=True))
        low = probs.astype(B16)
        attn = dot(v, low)
        delta = jnp.sum(dy.astype(F32) * attn, axis=0, keepdims=True)
        dprobs = dot(v, dy, TN)
        dscores = (scale * probs * (dprobs - delta)).astype(B16)
        dq = dot(k, dscores)
        dk = dot(q, dscores, NT)
        dv = dot(dy, low, NT)
        for i, h in enumerate(heads):
            rows = slice(h * 64, h * 64 + 64)
            lanes = slice(i * TOK, i * TOK + TOK)
            attn_o[rows, :] = attn[:, lanes].astype(B16)
            x = query[rows, :]
            dx = dq[:, lanes]
            r = lax.rsqrt(jnp.mean(x * x, axis=0, keepdims=True) + 1e-06)
            inner = jnp.mean(x * dx, axis=0, keepdims=True)
            dq_o[rows, :] = (r * dx - x * (r * r * r * inner)).astype(B16)
        own_o[g * 64 : g * 64 + 64, :] = dk[:, :TOK]
        own_o[256 + g * 64 : 320 + g * 64, :] = dv[:, :TOK]
        for j, back in enumerate((back1_o, back2_o, back3_o)):
            lanes = slice((j + 1) * TOK, (j + 2) * TOK)
            back[g * 64 : g * 64 + 64, :] = dk[:, lanes].astype(B16)
            back[256 + g * 64 : 320 + g * 64, :] = dv[:, lanes].astype(B16)


def part_body(w_q, dq, part_o):
    part_o[...] = dot(w_q[...], dq[...]).T


def tokens_body(
    own, back1, back2, back3, key, w_kv, tokens, gain, part, d_out, attn, dq,
    late_o, dkv_s, tokens_s,
):
    total = own[...] + back1[...].astype(F32) + back2[...].astype(F32) + back3[...].astype(F32)
    for h in range(KEY_VALUE_HEADS):
        rows = slice(h * 64, h * 64 + 64)
        x = key[rows, :]
        dx = total[rows]
        r = lax.rsqrt(jnp.mean(x * x, axis=0, keepdims=True) + 1e-06)
        inner = jnp.mean(x * dx, axis=0, keepdims=True)
        dkv_s[rows, :] = (r * dx - x * (r * r * r * inner)).astype(B16)
    dkv_s[256:, :] = total[256:].astype(B16)
    d_hidden = part[...] + dot(w_kv[...], dkv_s[...]).T
    tok = tokens[...].astype(F32)
    r = lax.rsqrt(jnp.mean(tok * tok, axis=1, keepdims=True) + 1e-05)
    gain_term = jnp.sum(d_hidden * (tok * r), axis=0, keepdims=True)
    dx = d_hidden * gain[...].astype(F32)
    inner = jnp.mean(tok * dx, axis=1, keepdims=True)
    tokens_s[...] = (d_out[...].astype(F32) + (r * dx - tok * (r * r * r * inner))).T
    gains = jnp.concatenate(
        [gain_term[:, i * TOK : i * TOK + TOK] for i in range(6)] + [jnp.zeros((10, TOK), F32)],
        axis=0,
    ).astype(B16)
    for m in range(8):
        for k in range(3):
            picked = tokens_s[pl.ds(m // 4 * 384 + m % 4 * 3 + k, 32, stride=12), :]
            late_o[m, k * 32 : k * 32 + 32, :] = picked.astype(B16)
        late_o[m, 96:128, :] = dkv_s[m * 32 : m * 32 + 32, :]
        late_o[m, 128:160, :] = dkv_s[256 + m * 32 : 288 + m * 32, :]
        late_o[m, 160:176, :] = gains
        late_o[m, 176:272, :] = attn[m * 96 : m * 96 + 96, :]
        late_o[m, 272:, :] = dq[m * 96 : m * 96 + 96, :]


def terms_body(
    place, late, *rest
):
    rings, tiles = rest[:8], rest[8]
    terms_o, both_s, pair_s, rhs_s, sums_s, all_s = rest[9:]
    lane = lax.broadcasted_iota(jnp.int32, (96, TOK), 1)
    gain = jnp.zeros((16, TOK), F32)
    zero = jnp.zeros((TOK, TOK), B16)
    for yl in range(2):
        before = jnp.zeros((96, TOK), F32)
        for band in range(4):
            m = yl * 4 + band
            block = late[m, :96, :]
            gain = gain + late[m, 160:176, :].astype(F32)
            moved = pltpu.roll(block.astype(F32), TC, 1)
            pair_s[m, :96, :] = block
            pair_s[m, 96:, :] = jnp.where(lane < TC, before, moved).astype(B16)
            before = moved
            rhs_s[m, :96, :TOK] = late[m, 272:, :]
            rhs_s[m, 96:128, :TOK] = late[m, 96:128, :]
            rhs_s[m, :128, TOK:] = zero
            rhs_s[m, 128:224, :TOK] = zero[:96]
            rhs_s[m, 128:224, TOK:] = late[m, 176:272, :]
            rhs_s[m, 224:, :TOK] = late[m, 128:160, :]
            rhs_s[m, 224:, TOK:] = zero[:32]
    rows = jnp.zeros((D, 256), F32)
    members = []
    for side in range(2):
        for back in range(4):
            chip = lax.rem(place[0] + 4 - back, 4)
            core = lax.rem(place[1] + side, 2)
            members.append(lax.rem(chip, 2) * 4 + lax.div(chip, 2) * 2 + core)
    for ring, m in zip(rings, members):
        rows = rows + dot(ring[...], rhs_s[m], NT)
    for half in range(2):
        sums_s[half] = rows[:, half * TOK : half * TOK + TOK]
        for i in range(24):
            picked = sums_s[half, pl.ds(i // 12 * 384 + i % 12, 32, stride=12), :]
            all_s[pl.ds(48 + half * 24 + i, 32, stride=104), :] = picked
    for i in range(8):
        row = gain[i : i + 1, :]
        all_s[pl.ds(96 + i, 32, stride=104), :] = jnp.broadcast_to(row, (32, TOK))
    for i, m in enumerate(members):
        both_s[:, i * TOK : i * TOK + TOK] = pair_s[m]
        tiles.piece(i)
    stem = dot(both_s[...], tiles[...])
    for c in range(8):
        for i in range(6):
            picked = stem[i * 32 : i * 32 + 32, c * TOK : c * TOK + TOK]
            all_s[pl.ds(i * 8 + c, 32, stride=104), :] = picked
    terms_o[...] = all_s[...].astype(B16)


def total_body(terms, stem_o, gain_o, rows_o):
    total = jnp.zeros((104, TOK), F32)
    for piece in range(4):
        block = terms.piece(piece)
        for r in range(8):
            total = total + block[r].astype(F32)
    for j in range(2):
        for k in range(3):
            for c in range(8):
                at = (j * 3 + k) * 8 + c
                stem_o[k, j : j + 1, c * TOK : c * TOK + TOK] = total[at : at + 1]
    for c in range(6):
        gain_o[:, c * TOK : c * TOK + TOK] = total[96 + c : 97 + c]
    for half in range(2):
        lanes = slice(half * TOK, half * TOK + TOK)
        for m in range(8):
            at = 48 + half * 24 + m * 3
            rows_o[m, :3, lanes] = total[at : at + 3]
            rows_o[m, 3:, lanes] = jnp.zeros((5, TOK), F32)


def final_body(rows, qkv_o, out_o):
    for first, last, to in ((0, 96, 0), (96, 128, D), (224, 256, D + 256)):
        width = last - first
        for m in range(8):
            qkv_o[:, to + m * width : to + m * width + width] = rows[m, :3, first:last]
    for m in range(8):
        out_o[:, m * 96 : m * 96 + 96] = rows[m, :3, 128:224]


def shards(patches, stem_weight, norm_gain, w_qkv, w_out, per_head_scale, positions, d_out):
    tiles = patches[0]
    grad_out = d_out[0]
    bands = lax.axis_size(BAND)
    arrived = lax.ppermute(tiles[:TC], BAND, [(i, i - 1) for i in range(1, bands)])
    tiles_mine = from_chips(tiles)
    gain = norm_gain.reshape(1, D)
    tokens, hidden, key, kv_own, ring_own = call(
        stem_body,
        [
            ((TOK, D), B16),
            ((TOK, D), B16),
            ((256, TOK), F32),
            ((KV, TOK), B16),
            ((D, 2 * TOK), B16),
        ],
        pieces={1: 8, 3: 2},
        columns={3: (D, D + KV)},
    )(tiles, stem_weight.reshape(-1, D), arrived, w_qkv, gain, grad_out)
    moved = [passed_along(kv_own, offset) for offset in range(1, 4)]
    moved[0], hidden = lax.optimization_barrier((moved[0], hidden))
    query, query_n, do = call(
        query_body,
        [((D, TOK), F32), ((D, TOK), B16), ((D, TOK), B16)],
        pieces={2: 2, 3: 2},
        columns={2: (0, D)},
    )(hidden, grad_out, w_qkv, w_out)
    query_n, tiles_mine = lax.optimization_barrier((query_n, tiles_mine))
    own_block = lax.axis_index(BLK).astype(jnp.int32).reshape(1)
    attn, d_q, own, back1, back2, back3 = call(
        attend_body,
        [((D, TOK), B16), ((D, TOK), B16), ((KV, TOK), F32)] + [((KV, TOK), B16)] * 3,
        smem=(0, 1),
    )(own_block, per_head_scale, positions.reshape(64, TOK), kv_own, *moved, query_n, do, query)
    returned = [passed_along(piece, -(j + 1)) for j, piece in enumerate((back1, back2, back3))]
    returned[0], d_q = lax.optimization_barrier((returned[0], d_q))
    part = call(part_body, [((TOK, D), F32)], pieces={0: 2}, columns={0: (0, D)})(w_qkv, d_q)[0]
    ring_mine = from_chips(ring_own)
    ring_mine, part = lax.optimization_barrier((ring_mine, part))
    late = call(
        tokens_body,
        [((8, 368, TOK), B16)],
        scratch=[pltpu.VMEM((KV, TOK), B16), pltpu.VMEM((D, TOK), F32)],
        pieces={5: 2},
        columns={5: (D, D + KV)},
    )(own, *returned, key, w_qkv, tokens, gain, part, grad_out, attn, d_q)[0]
    late_ring = exchange(late, RING)
    rings = [ring_own, *ring_mine]
    blocks = [tiles, *tiles_mine]
    rings = rings + [other_core(x) for x in rings]
    blocks = blocks + [other_core(x) for x in blocks]
    chip = lax.axis_index("yh") * 2 + lax.axis_index("yl")
    place = jnp.stack([chip, lax.axis_index("c")]).astype(jnp.int32)
    terms = call(
        terms_body,
        [((32 * 104, TOK), B16)],
        scratch=[
            pltpu.VMEM((192, 1024), B16),
            pltpu.VMEM((8, 192, TOK), B16),
            pltpu.VMEM((8, 256, 256), B16),
            pltpu.VMEM((2, D, TOK), F32),
            pltpu.VMEM((32 * 104, TOK), F32),
        ],
        smem=(0,),
        joined=10,
    )(place, late_ring, *rings, *blocks)[0]
    stem_total, gain_total, row_total = call(
        total_body,
        [((3, 2, 1024), F32), ((1, D), F32), ((8, 8, 256), F32)],
        pieces={0: 4},
        limit=16,
    )(exchange(terms.reshape(32, 104, TOK), REST))
    d_w_qkv, d_w_out = call(final_body, [((3, 1280), F32), ((3, D), F32)], limit=16)(
        exchange(row_total, RING)
    )
    own_column = (lax.axis_index(BLK) * 4 + lax.axis_index(BAND)) * 3
    d_norm_gain = lax.dynamic_slice_in_dim(gain_total[0], own_column, 3)
    d_stem_weight = stem_total.transpose(1, 2, 0)
    return (d_stem_weight, d_norm_gain, d_w_qkv, d_w_out.T)


def solution(mesh):
    fine = Mesh(mesh.devices.reshape(2, 4, 8, 2, 2), BLK + BAND)
    placed = (P(BAND, BLK, None), P(), P(), P(), P(), P(), P(), P(BAND, BLK, None))
    every = BLK + BAND
    return jax.shard_map(
        shards,
        mesh=fine,
        in_specs=placed,
        out_specs=(P(None, None, every), P(every), P(every, None), P(None, every)),
        check_vma=False,
    )
```

```python
import jax
import jax.numpy as jnp
from jax import lax
from jax.experimental import pallas as pl
from jax.experimental.pallas import tpu as pltpu
from jax.sharding import Mesh, PartitionSpec as P

QUERY_HEADS = 12
KEY_VALUE_HEADS = 4
HEAD_SIZE = 64
TC = 16
D = 768
KV = 512
TOK = 128
BLK = ("yl", "x", "z")
BAND = ("yh", "c")
RING = ("yl", "yh", "c")
CHIPS = ("yl", "yh")
REST = ("x", "z")
F32 = jnp.float32
B16 = jnp.bfloat16
NN = (((1,), (0,)), ((), ()))
NT = (((1,), (1,)), ((), ()))
TN = (((0,), (0,)), ((), ()))


def dot(a, b, dims=NN):
    return lax.dot_general(a, b, dims, preferred_element_type=F32)


def passed_along(x, by):
    peers = lax.axis_size(BLK)
    return lax.ppermute(x, BLK, [(i, (i + by) % peers) for i in range(peers)])


def along_ring(x, by):
    order = [0, 2, 1, 3]
    return lax.ppermute(x, CHIPS, [(order[i], order[(i + by) % 4]) for i in range(4)])


def other_core(x):
    return lax.ppermute(x, "c", [(0, 1), (1, 0)])


def exchange(x, axes):
    return lax.all_to_all(x, axes, split_axis=0, concat_axis=0, tiled=True)


class Loaded:
    def __init__(self, ref, pieces):
        self.ref, self.pieces = ref, pieces

    def piece(self, i):
        copy, place = self.pieces[i]
        if copy is not None:
            copy.wait()
            self.pieces[i] = (None, place)
        return self.ref.at[place]

    def __getitem__(self, index):
        for i in range(len(self.pieces)):
            self.piece(i)
        return self.ref[index]


def split(shape, count):
    rows = shape[0] // count
    return [slice(i * rows, i * rows + rows) for i in range(count)]


def call(
    body, outs, scratch=(), smem=(), pieces=None, columns=None, joined=None, limit=64, flops=10**9
):
    pieces, columns = pieces or {}, columns or {}

    def run(*operands):
        held, parts, total = [], [], 0
        count = len(operands) if joined is None else joined
        if joined is not None:
            rows, width = operands[joined].shape
            held.append(pltpu.VMEM(((len(operands) - joined) * rows, width), operands[joined].dtype))
            total += len(operands) - joined
        for i, operand in enumerate(operands[:count]):
            if i in smem:
                continue
            shape = operand.shape
            if i in columns:
                shape = (shape[0], columns[i][1] - columns[i][0])
            held.append(pltpu.VMEM(shape, operand.dtype))
            parts.append((i, split(shape, pieces.get(i, 1))))
            total += pieces.get(i, 1)

        def kernel(*refs):
            inputs = list(refs[: len(operands)])
            others = refs[len(operands) : len(refs) - len(held) - 1]
            stores, sems = refs[len(refs) - len(held) - 1 : -1], refs[-1]
            used = 0
            if joined is not None:
                used, made = len(operands) - joined, []
                for i, place in enumerate(split(stores[0].shape, used)):
                    made.append(
                        (pltpu.make_async_copy(inputs[joined + i], stores[0].at[place], sems.at[i]), place)
                    )
                inputs[joined:] = [Loaded(stores[0], made)]
                stores = stores[1:]
            for (i, places), store in zip(parts, stores):
                source = inputs[i]
                if i in columns:
                    source = source.at[:, columns[i][0] : columns[i][1]]
                made = []
                for place in places:
                    copy = pltpu.make_async_copy(
                        source.at[place], store.at[place], sems.at[used]
                    )
                    copy.start()
                    made.append((copy, place))
                    used += 1
                inputs[i] = Loaded(store, made)
            if joined is not None:
                for copy, _ in inputs[joined].pieces:
                    copy.start()
            body(*inputs, *others)
            for value in inputs:
                if isinstance(value, Loaded):
                    for j in range(len(value.pieces)):
                        value.piece(j)

        shapes = [jax.ShapeDtypeStruct(shape, kind) for shape, kind in outs]
        return pl.pallas_call(
            kernel,
            out_shape=shapes,
            in_specs=[
                pl.BlockSpec(memory_space=pltpu.SMEM if i in smem else pl.ANY)
                for i in range(len(operands))
            ],
            out_specs=[pl.BlockSpec(memory_space=pltpu.VMEM)] * len(shapes),
            scratch_shapes=[*scratch, *held, pltpu.SemaphoreType.DMA((total,))],
            compiler_params=pltpu.CompilerParams(vmem_limit_bytes=limit * 2**20),
            cost_estimate=pl.CostEstimate(
                flops=flops, bytes_accessed=4 * 2**20, transcendentals=0
            ),
        )(*operands)

    return run


def stem_body(
    tiles, stem_w, arrived, w_kv, gain, d_out, tokens_o, hidden_o, key_o, kv_o, ring_o
):
    own = tiles[...]
    deep = own.shape[1] // 4
    below = jnp.concatenate([own[TC:], arrived[...]], axis=0)
    stem = jnp.zeros((TOK, D), F32)
    for j, rows in enumerate((own, below)):
        for i in range(4):
            columns = rows[:, i * deep : i * deep + deep]
            stem = stem + dot(columns, stem_w.piece(4 * j + i)[...])
    low = stem.astype(B16)
    tokens_o[...] = low
    tok = low.astype(F32)
    factor = lax.rsqrt(jnp.mean(tok * tok, axis=1, keepdims=True) + 1e-05)
    hidden = (tok * factor * gain[...].astype(F32)).astype(B16)
    hidden_o[...] = hidden
    kv = dot(hidden, w_kv[...]).T
    key_o[...] = kv[:256]
    for h in range(KEY_VALUE_HEADS):
        k = kv[h * 64 : h * 64 + 64]
        scale = lax.rsqrt(jnp.mean(k * k, axis=0, keepdims=True) + 1e-06)
        kv_o[h * 64 : h * 64 + 64, :] = (k * scale).astype(B16)
    kv_o[256:, :] = kv[256:].astype(B16)
    ring_o[:, :TOK] = hidden.astype(F32).T.astype(B16)
    ring_o[:, TOK:] = d_out[...].astype(F32).T.astype(B16)


def query_body(hidden, d_out, w_q, w_out, query_o, query_n_o, do_o):
    h = hidden[...]
    g = d_out[...]
    q = dot(h, w_q[...]).T
    query_o[...] = q
    for i in range(QUERY_HEADS):
        part = q[i * 64 : i * 64 + 64]
        scale = lax.rsqrt(jnp.mean(part * part, axis=0, keepdims=True) + 1e-06)
        query_n_o[i * 64 : i * 64 + 64, :] = (part * scale).astype(B16)
    do_o[...] = dot(w_out[...], g, NT).astype(B16)


def attend_body(
    own_block, scales, positions, kv0, kv1, kv2, kv3, query_n, do, query,
    attn_o, dq_o, own_o, back1_o, back2_o, back3_o,
):
    own = own_block[0]
    blocks = (kv0, kv1, kv2, kv3)
    positions[:8]
    rows = positions.ref
    q_pos = rows[pl.ds(own, 1), :]
    columns = []
    for j in range(4):
        row = rows[pl.ds(lax.rem(own - j + 64, 64), 1), :].astype(F32)
        columns.append(jnp.broadcast_to(row, (TOK, TOK)).T)
    key_pos = jnp.concatenate(columns, axis=0)
    bias = jnp.where(key_pos <= q_pos.astype(F32), 0.0, -1e30)
    bias = jnp.concatenate([bias] * 3, axis=1)
    for g in range(KEY_VALUE_HEADS):
        k = jnp.concatenate([b[g * 64 : g * 64 + 64, :] for b in blocks], axis=1)
        v = jnp.concatenate([b[256 + g * 64 : 320 + g * 64, :] for b in blocks], axis=1)
        heads = [3 * g + i for i in range(3)]
        q = jnp.concatenate([query_n[h * 64 : h * 64 + 64, :] for h in heads], axis=1)
        dy = jnp.concatenate([do[h * 64 : h * 64 + 64, :] for h in heads], axis=1)
        scale = jnp.concatenate([jnp.full((1, TOK), scales[h], F32) for h in heads], axis=1)
        scores = dot(k, q, TN) * scale + bias
        top = jnp.max(scores, axis=0, keepdims=True)
        weights = jnp.exp(scores - top)
        probs = weights * (1.0 / jnp.sum(weights, axis=0, keepdims=True))
        low = probs.astype(B16)
        attn = dot(v, low)
        delta = jnp.sum(dy.astype(F32) * attn, axis=0, keepdims=True)
        dprobs = dot(v, dy, TN)
        dscores = (scale * probs * (dprobs - delta)).astype(B16)
        dq = dot(k, dscores)
        dk = dot(q, dscores, NT)
        dv = dot(dy, low, NT)
        for i, h in enumerate(heads):
            rows = slice(h * 64, h * 64 + 64)
            lanes = slice(i * TOK, i * TOK + TOK)
            attn_o[rows, :] = attn[:, lanes].astype(B16)
            x = query[rows, :]
            dx = dq[:, lanes]
            r = lax.rsqrt(jnp.mean(x * x, axis=0, keepdims=True) + 1e-06)
            inner = jnp.mean(x * dx, axis=0, keepdims=True)
            dq_o[rows, :] = (r * dx - x * (r * r * r * inner)).astype(B16)
        own_o[g * 64 : g * 64 + 64, :] = dk[:, :TOK]
        own_o[256 + g * 64 : 320 + g * 64, :] = dv[:, :TOK]
        for j, back in enumerate((back1_o, back2_o, back3_o)):
            lanes = slice((j + 1) * TOK, (j + 2) * TOK)
            back[g * 64 : g * 64 + 64, :] = dk[:, lanes].astype(B16)
            back[256 + g * 64 : 320 + g * 64, :] = dv[:, lanes].astype(B16)


def part_body(w_q, dq, part_o):
    part_o[...] = dot(w_q[...], dq[...]).T


def tokens_body(
    own, back1, back2, back3, key, w_kv, tokens, gain, part, d_out, attn, dq,
    late_o, dkv_s, tokens_s,
):
    total = own[...] + back1[...].astype(F32) + back2[...].astype(F32) + back3[...].astype(F32)
    for h in range(KEY_VALUE_HEADS):
        rows = slice(h * 64, h * 64 + 64)
        x = key[rows, :]
        dx = total[rows]
        r = lax.rsqrt(jnp.mean(x * x, axis=0, keepdims=True) + 1e-06)
        inner = jnp.mean(x * dx, axis=0, keepdims=True)
        dkv_s[rows, :] = (r * dx - x * (r * r * r * inner)).astype(B16)
    dkv_s[256:, :] = total[256:].astype(B16)
    d_hidden = part[...] + dot(w_kv[...], dkv_s[...]).T
    tok = tokens[...].astype(F32)
    r = lax.rsqrt(jnp.mean(tok * tok, axis=1, keepdims=True) + 1e-05)
    gain_term = jnp.sum(d_hidden * (tok * r), axis=0, keepdims=True)
    dx = d_hidden * gain[...].astype(F32)
    inner = jnp.mean(tok * dx, axis=1, keepdims=True)
    tokens_s[...] = (d_out[...].astype(F32) + (r * dx - tok * (r * r * r * inner))).T
    gains = jnp.concatenate(
        [gain_term[:, i * TOK : i * TOK + TOK] for i in range(6)] + [jnp.zeros((10, TOK), F32)],
        axis=0,
    ).astype(B16)
    for m in range(8):
        for k in range(3):
            picked = tokens_s[pl.ds(m // 4 * 384 + m % 4 * 3 + k, 32, stride=12), :]
            late_o[m, k * 32 : k * 32 + 32, :] = picked.astype(B16)
        late_o[m, 96:128, :] = dkv_s[m * 32 : m * 32 + 32, :]
        late_o[m, 128:160, :] = dkv_s[256 + m * 32 : 288 + m * 32, :]
        late_o[m, 160:176, :] = gains
        late_o[m, 176:272, :] = attn[m * 96 : m * 96 + 96, :]
        late_o[m, 272:, :] = dq[m * 96 : m * 96 + 96, :]


def terms_body(
    place, late, *rest
):
    rings, tiles = rest[:8], rest[8]
    terms_o, both_s, pair_s, rhs_s, sums_s, all_s = rest[9:]
    lane = lax.broadcasted_iota(jnp.int32, (96, TOK), 1)
    gain = jnp.zeros((16, TOK), F32)
    zero = jnp.zeros((TOK, TOK), B16)
    for yl in range(2):
        before = jnp.zeros((96, TOK), F32)
        for band in range(4):
            m = yl * 4 + band
            block = late[m, :96, :]
            gain = gain + late[m, 160:176, :].astype(F32)
            moved = pltpu.roll(block.astype(F32), TC, 1)
            pair_s[m, :96, :] = block
            pair_s[m, 96:, :] = jnp.where(lane < TC, before, moved).astype(B16)
            before = moved
            rhs_s[m, :96, :TOK] = late[m, 272:, :]
            rhs_s[m, 96:128, :TOK] = late[m, 96:128, :]
            rhs_s[m, :128, TOK:] = zero
            rhs_s[m, 128:224, :TOK] = zero[:96]
            rhs_s[m, 128:224, TOK:] = late[m, 176:272, :]
            rhs_s[m, 224:, :TOK] = late[m, 128:160, :]
            rhs_s[m, 224:, TOK:] = zero[:32]
    rows = jnp.zeros((D, 256), F32)
    members = []
    for side in range(2):
        for back in range(4):
            chip = lax.rem(place[0] + 4 - back, 4)
            core = lax.rem(place[1] + side, 2)
            members.append(lax.rem(chip, 2) * 4 + lax.div(chip, 2) * 2 + core)
    for ring, m in zip(rings, members):
        rows = rows + dot(ring[...], rhs_s[m], NT)
    for half in range(2):
        sums_s[half] = rows[:, half * TOK : half * TOK + TOK]
        for i in range(24):
            picked = sums_s[half, pl.ds(i // 12 * 384 + i % 12, 32, stride=12), :]
            all_s[pl.ds(48 + half * 24 + i, 32, stride=104), :] = picked
    for i in range(8):
        row = gain[i : i + 1, :]
        all_s[pl.ds(96 + i, 32, stride=104), :] = jnp.broadcast_to(row, (32, TOK))
    for i, m in enumerate(members):
        both_s[:, i * TOK : i * TOK + TOK] = pair_s[m]
        tiles.piece(i)
    stem = dot(both_s[...], tiles[...])
    for c in range(8):
        for i in range(6):
            picked = stem[i * 32 : i * 32 + 32, c * TOK : c * TOK + TOK]
            all_s[pl.ds(i * 8 + c, 32, stride=104), :] = picked
    terms_o[...] = all_s[...].astype(B16)


def total_body(terms, stem_o, gain_o, rows_o):
    total = jnp.zeros((104, TOK), F32)
    for piece in range(8):
        block = terms.piece(piece)
        for r in range(4):
            total = total + block[r].astype(F32)
    for j in range(2):
        for k in range(3):
            for c in range(8):
                at = (j * 3 + k) * 8 + c
                stem_o[k, j : j + 1, c * TOK : c * TOK + TOK] = total[at : at + 1]
    for c in range(6):
        gain_o[:, c * TOK : c * TOK + TOK] = total[96 + c : 97 + c]
    for half in range(2):
        lanes = slice(half * TOK, half * TOK + TOK)
        for m in range(8):
            at = 48 + half * 24 + m * 3
            rows_o[m, :3, lanes] = total[at : at + 3]
            rows_o[m, 3:, lanes] = jnp.zeros((5, TOK), F32)


def final_body(rows, qkv_o, out_o):
    for first, last, to in ((0, 96, 0), (96, 128, D), (224, 256, D + 256)):
        width = last - first
        for m in range(8):
            qkv_o[:, to + m * width : to + m * width + width] = rows[m, :3, first:last]
    for m in range(8):
        out_o[:, m * 96 : m * 96 + 96] = rows[m, :3, 128:224]


def shards(patches, stem_weight, norm_gain, w_qkv, w_out, per_head_scale, positions, d_out):
    tiles = patches[0]
    grad_out = d_out[0]
    bands = lax.axis_size(BAND)
    arrived = lax.ppermute(tiles[:TC], BAND, [(i, i - 1) for i in range(1, bands)])
    tiles_mine = [along_ring(tiles, 1), None, along_ring(tiles, 3)]
    gain = norm_gain.reshape(1, D)
    tokens, hidden, key, kv_own, ring_own = call(
        stem_body,
        [
            ((TOK, D), B16),
            ((TOK, D), B16),
            ((256, TOK), F32),
            ((KV, TOK), B16),
            ((D, 2 * TOK), B16),
        ],
        pieces={1: 8, 3: 2},
        columns={3: (D, D + KV)},
    )(tiles, stem_weight.reshape(-1, D), arrived, w_qkv, gain, grad_out)
    moved = [passed_along(kv_own, offset) for offset in range(1, 4)]
    moved[0], hidden = lax.optimization_barrier((moved[0], hidden))
    query, query_n, do = call(
        query_body,
        [((D, TOK), F32), ((D, TOK), B16), ((D, TOK), B16)],
        pieces={2: 2, 3: 2},
        columns={2: (0, D)},
    )(hidden, grad_out, w_qkv, w_out)
    query_n, tiles_late = lax.optimization_barrier((query_n, tiles_mine[0]))
    tiles_mine[1] = along_ring(tiles_late, 1)
    query_n, tiles_mine[0], tiles_mine[2] = lax.optimization_barrier(
        (query_n, tiles_mine[0], tiles_mine[2])
    )
    own_block = lax.axis_index(BLK).astype(jnp.int32).reshape(1)
    attn, d_q, own, back1, back2, back3 = call(
        attend_body,
        [((D, TOK), B16), ((D, TOK), B16), ((KV, TOK), F32)] + [((KV, TOK), B16)] * 3,
        smem=(0, 1),
    )(own_block, per_head_scale, positions.reshape(64, TOK), kv_own, *moved, query_n, do, query)
    returned = [passed_along(piece, -(j + 1)) for j, piece in enumerate((back1, back2, back3))]
    returned[0], d_q = lax.optimization_barrier((returned[0], d_q))
    part = call(part_body, [((TOK, D), F32)], pieces={0: 2}, columns={0: (0, D)})(w_qkv, d_q)[0]
    ring_mine = [along_ring(ring_own, by) for by in (1, 2, 3)]
    ring_mine[0], ring_mine[2], tiles_mine[1], part = lax.optimization_barrier(
        (ring_mine[0], ring_mine[2], tiles_mine[1], part)
    )
    late = call(
        tokens_body,
        [((8, 368, TOK), B16)],
        scratch=[pltpu.VMEM((KV, TOK), B16), pltpu.VMEM((D, TOK), F32)],
        pieces={5: 2},
        columns={5: (D, D + KV)},
    )(own, *returned, key, w_qkv, tokens, gain, part, grad_out, attn, d_q)[0]
    late_ring = exchange(late, RING)
    rings = [ring_own, *ring_mine]
    blocks = [tiles, *tiles_mine]
    rings = rings + [other_core(x) for x in rings]
    blocks = blocks + [other_core(x) for x in blocks]
    chip = lax.axis_index("yh") * 2 + lax.axis_index("yl")
    place = jnp.stack([chip, lax.axis_index("c")]).astype(jnp.int32)
    terms = call(
        terms_body,
        [((32 * 104, TOK), B16)],
        scratch=[
            pltpu.VMEM((192, 1024), B16),
            pltpu.VMEM((8, 192, TOK), B16),
            pltpu.VMEM((8, 256, 256), B16),
            pltpu.VMEM((2, D, TOK), F32),
            pltpu.VMEM((32 * 104, TOK), F32),
        ],
        smem=(0,),
        joined=10,
    )(place, late_ring, *rings, *blocks)[0]
    stem_total, gain_total, row_total = call(
        total_body,
        [((3, 2, 1024), F32), ((1, D), F32), ((8, 8, 256), F32)],
        pieces={0: 8},
        limit=16,
    )(exchange(terms.reshape(32, 104, TOK), REST))
    d_w_qkv, d_w_out = call(final_body, [((3, 1280), F32), ((3, D), F32)], limit=16)(
        exchange(row_total, RING)
    )
    own_column = (lax.axis_index(BLK) * 4 + lax.axis_index(BAND)) * 3
    d_norm_gain = lax.dynamic_slice_in_dim(gain_total[0], own_column, 3)
    d_stem_weight = stem_total.transpose(1, 2, 0)
    return (d_stem_weight, d_norm_gain, d_w_qkv, d_w_out.T)


def solution(mesh):
    fine = Mesh(mesh.devices.reshape(2, 4, 8, 2, 2), BLK + BAND)
    placed = (P(BAND, BLK, None), P(), P(), P(), P(), P(), P(), P(BAND, BLK, None))
    every = BLK + BAND
    return jax.shard_map(
        shards,
        mesh=fine,
        in_specs=placed,
        out_specs=(P(None, None, every), P(every), P(every, None), P(None, every)),
        check_vma=False,
    )
```

```python
import jax
import jax.numpy as jnp
from jax import lax
from jax.experimental import pallas as pl
from jax.experimental.pallas import tpu as pltpu
from jax.sharding import Mesh, PartitionSpec as P

QUERY_HEADS = 12
KEY_VALUE_HEADS = 4
HEAD_SIZE = 64
TC = 16
D = 768
KV = 512
TOK = 128
BLK = ("yl", "x", "z")
BAND = ("yh", "c")
RING = ("yl", "yh", "c")
CHIPS = ("yl", "yh")
REST = ("x", "z")
F32 = jnp.float32
B16 = jnp.bfloat16
NN = (((1,), (0,)), ((), ()))
NT = (((1,), (1,)), ((), ()))
TN = (((0,), (0,)), ((), ()))


def dot(a, b, dims=NN):
    return lax.dot_general(a, b, dims, preferred_element_type=F32)


def passed_along(x, by):
    peers = lax.axis_size(BLK)
    return lax.ppermute(x, BLK, [(i, (i + by) % peers) for i in range(peers)])


def along_ring(x, by):
    order = [0, 2, 1, 3]
    return lax.ppermute(x, CHIPS, [(order[i], order[(i + by) % 4]) for i in range(4)])


def other_core(x):
    return lax.ppermute(x, "c", [(0, 1), (1, 0)])


def exchange(x, axes):
    return lax.all_to_all(x, axes, split_axis=0, concat_axis=0, tiled=True)


class Loaded:
    def __init__(self, ref, pieces):
        self.ref, self.pieces = ref, pieces

    def piece(self, i):
        copy, place = self.pieces[i]
        if copy is not None:
            copy.wait()
            self.pieces[i] = (None, place)
        return self.ref.at[place]

    def __getitem__(self, index):
        for i in range(len(self.pieces)):
            self.piece(i)
        return self.ref[index]


def split(shape, count):
    rows = shape[0] // count
    return [slice(i * rows, i * rows + rows) for i in range(count)]


def call(
    body, outs, scratch=(), smem=(), pieces=None, columns=None, joined=None, limit=64, flops=10**9
):
    pieces, columns = pieces or {}, columns or {}

    def run(*operands):
        held, parts, total = [], [], 0
        count = len(operands) if joined is None else joined
        if joined is not None:
            rows, width = operands[joined].shape
            held.append(pltpu.VMEM(((len(operands) - joined) * rows, width), operands[joined].dtype))
            total += len(operands) - joined
        for i, operand in enumerate(operands[:count]):
            if i in smem:
                continue
            shape = operand.shape
            if i in columns:
                shape = (shape[0], columns[i][1] - columns[i][0])
            held.append(pltpu.VMEM(shape, operand.dtype))
            parts.append((i, split(shape, pieces.get(i, 1))))
            total += pieces.get(i, 1)

        def kernel(*refs):
            inputs = list(refs[: len(operands)])
            others = refs[len(operands) : len(refs) - len(held) - 1]
            stores, sems = refs[len(refs) - len(held) - 1 : -1], refs[-1]
            used = 0
            if joined is not None:
                used, made = len(operands) - joined, []
                for i, place in enumerate(split(stores[0].shape, used)):
                    made.append(
                        (pltpu.make_async_copy(inputs[joined + i], stores[0].at[place], sems.at[i]), place)
                    )
                inputs[joined:] = [Loaded(stores[0], made)]
                stores = stores[1:]
            for (i, places), store in zip(parts, stores):
                source = inputs[i]
                if i in columns:
                    source = source.at[:, columns[i][0] : columns[i][1]]
                made = []
                for place in places:
                    copy = pltpu.make_async_copy(
                        source.at[place], store.at[place], sems.at[used]
                    )
                    copy.start()
                    made.append((copy, place))
                    used += 1
                inputs[i] = Loaded(store, made)
            if joined is not None:
                for copy, _ in inputs[joined].pieces:
                    copy.start()
            body(*inputs, *others)
            for value in inputs:
                if isinstance(value, Loaded):
                    for j in range(len(value.pieces)):
                        value.piece(j)

        shapes = [jax.ShapeDtypeStruct(shape, kind) for shape, kind in outs]
        return pl.pallas_call(
            kernel,
            out_shape=shapes,
            in_specs=[
                pl.BlockSpec(memory_space=pltpu.SMEM if i in smem else pl.ANY)
                for i in range(len(operands))
            ],
            out_specs=[pl.BlockSpec(memory_space=pltpu.VMEM)] * len(shapes),
            scratch_shapes=[*scratch, *held, pltpu.SemaphoreType.DMA((total,))],
            compiler_params=pltpu.CompilerParams(vmem_limit_bytes=limit * 2**20),
            cost_estimate=pl.CostEstimate(
                flops=flops, bytes_accessed=4 * 2**20, transcendentals=0
            ),
        )(*operands)

    return run


def stem_body(
    tiles, stem_w, arrived, w_kv, gain, tokens_o, hidden_o, key_o, kv_o
):
    own = tiles[...]
    deep = own.shape[1] // 4
    below = jnp.concatenate([own[TC:], arrived[...]], axis=0)
    stem = jnp.zeros((TOK, D), F32)
    for j, rows in enumerate((own, below)):
        for i in range(4):
            columns = rows[:, i * deep : i * deep + deep]
            stem = stem + dot(columns, stem_w.piece(4 * j + i)[...])
    low = stem.astype(B16)
    tokens_o[...] = low
    tok = low.astype(F32)
    factor = lax.rsqrt(jnp.mean(tok * tok, axis=1, keepdims=True) + 1e-05)
    hidden = (tok * factor * gain[...].astype(F32)).astype(B16)
    hidden_o[...] = hidden
    kv = dot(hidden, w_kv[...]).T
    key_o[...] = kv[:256]
    for h in range(KEY_VALUE_HEADS):
        k = kv[h * 64 : h * 64 + 64]
        scale = lax.rsqrt(jnp.mean(k * k, axis=0, keepdims=True) + 1e-06)
        kv_o[h * 64 : h * 64 + 64, :] = (k * scale).astype(B16)
    kv_o[256:, :] = kv[256:].astype(B16)


def query_body(hidden, d_out, w_q, w_out, query_o, query_n_o, do_o, ring_o):
    h = hidden[...]
    g = d_out[...]
    q = dot(h, w_q[...]).T
    query_o[...] = q
    for i in range(QUERY_HEADS):
        part = q[i * 64 : i * 64 + 64]
        scale = lax.rsqrt(jnp.mean(part * part, axis=0, keepdims=True) + 1e-06)
        query_n_o[i * 64 : i * 64 + 64, :] = (part * scale).astype(B16)
    do_o[...] = dot(w_out[...], g, NT).astype(B16)
    ring_o[:, :TOK] = h.astype(F32).T.astype(B16)
    ring_o[:, TOK:] = g.astype(F32).T.astype(B16)


def attend_body(
    own_block, scales, positions, kv0, kv1, kv2, kv3, query_n, do,
    attn_o, dq_o, own_o, back1_o, back2_o, back3_o,
):
    own = own_block[0]
    blocks = (kv0, kv1, kv2, kv3)
    positions[:8]
    rows = positions.ref
    q_pos = rows[pl.ds(own, 1), :]
    columns = []
    for j in range(4):
        row = rows[pl.ds(lax.rem(own - j + 64, 64), 1), :].astype(F32)
        columns.append(jnp.broadcast_to(row, (TOK, TOK)).T)
    key_pos = jnp.concatenate(columns, axis=0)
    bias = jnp.where(key_pos <= q_pos.astype(F32), 0.0, -1e30)
    bias = jnp.concatenate([bias] * 3, axis=1)
    for g in range(KEY_VALUE_HEADS):
        k = jnp.concatenate([b[g * 64 : g * 64 + 64, :] for b in blocks], axis=1)
        v = jnp.concatenate([b[256 + g * 64 : 320 + g * 64, :] for b in blocks], axis=1)
        heads = [3 * g + i for i in range(3)]
        q = jnp.concatenate([query_n[h * 64 : h * 64 + 64, :] for h in heads], axis=1)
        dy = jnp.concatenate([do[h * 64 : h * 64 + 64, :] for h in heads], axis=1)
        scale = jnp.concatenate([jnp.full((1, TOK), scales[h], F32) for h in heads], axis=1)
        scores = dot(k, q, TN) * scale + bias
        top = jnp.max(scores, axis=0, keepdims=True)
        weights = jnp.exp(scores - top)
        probs = weights * (1.0 / jnp.sum(weights, axis=0, keepdims=True))
        low = probs.astype(B16)
        attn = dot(v, low)
        delta = jnp.sum(dy.astype(F32) * attn, axis=0, keepdims=True)
        dprobs = dot(v, dy, TN)
        dscores = (scale * probs * (dprobs - delta)).astype(B16)
        dq = dot(k, dscores)
        dk = dot(q, dscores, NT)
        dv = dot(dy, low, NT)
        for i, h in enumerate(heads):
            rows = slice(h * 64, h * 64 + 64)
            lanes = slice(i * TOK, i * TOK + TOK)
            attn_o[rows, :] = attn[:, lanes].astype(B16)
            dq_o[rows, :] = dq[:, lanes]
        own_o[g * 64 : g * 64 + 64, :] = dk[:, :TOK]
        own_o[256 + g * 64 : 320 + g * 64, :] = dv[:, :TOK]
        for j, back in enumerate((back1_o, back2_o, back3_o)):
            lanes = slice((j + 1) * TOK, (j + 2) * TOK)
            back[g * 64 : g * 64 + 64, :] = dk[:, lanes].astype(B16)
            back[256 + g * 64 : 320 + g * 64, :] = dv[:, lanes].astype(B16)


def part_body(dq_n, query, w_q, dq_o, part_o):
    for h in range(QUERY_HEADS):
        rows = slice(h * 64, h * 64 + 64)
        x = query[rows, :]
        dx = dq_n[rows, :]
        r = lax.rsqrt(jnp.mean(x * x, axis=0, keepdims=True) + 1e-06)
        inner = jnp.mean(x * dx, axis=0, keepdims=True)
        dq_o[rows, :] = (r * dx - x * (r * r * r * inner)).astype(B16)
    part_o[...] = dot(w_q[...], dq_o[...]).T


def tokens_body(
    own, back1, back2, back3, key, w_kv, tokens, gain, part, d_out, attn, dq,
    late_o, dkv_s, tokens_s,
):
    total = own[...] + back1[...].astype(F32) + back2[...].astype(F32) + back3[...].astype(F32)
    for h in range(KEY_VALUE_HEADS):
        rows = slice(h * 64, h * 64 + 64)
        x = key[rows, :]
        dx = total[rows]
        r = lax.rsqrt(jnp.mean(x * x, axis=0, keepdims=True) + 1e-06)
        inner = jnp.mean(x * dx, axis=0, keepdims=True)
        dkv_s[rows, :] = (r * dx - x * (r * r * r * inner)).astype(B16)
    dkv_s[256:, :] = total[256:].astype(B16)
    d_hidden = part[...] + dot(w_kv[...], dkv_s[...]).T
    tok = tokens[...].astype(F32)
    r = lax.rsqrt(jnp.mean(tok * tok, axis=1, keepdims=True) + 1e-05)
    gain_term = jnp.sum(d_hidden * (tok * r), axis=0, keepdims=True)
    dx = d_hidden * gain[...].astype(F32)
    inner = jnp.mean(tok * dx, axis=1, keepdims=True)
    tokens_s[...] = (d_out[...].astype(F32) + (r * dx - tok * (r * r * r * inner))).T
    gains = jnp.concatenate(
        [gain_term[:, i * TOK : i * TOK + TOK] for i in range(6)] + [jnp.zeros((10, TOK), F32)],
        axis=0,
    ).astype(B16)
    for m in range(8):
        for k in range(3):
            picked = tokens_s[pl.ds(m // 4 * 384 + m % 4 * 3 + k, 32, stride=12), :]
            late_o[m, k * 32 : k * 32 + 32, :] = picked.astype(B16)
        late_o[m, 96:128, :] = dkv_s[m * 32 : m * 32 + 32, :]
        late_o[m, 128:160, :] = dkv_s[256 + m * 32 : 288 + m * 32, :]
        late_o[m, 160:176, :] = gains
        late_o[m, 176:272, :] = attn[m * 96 : m * 96 + 96, :]
        late_o[m, 272:, :] = dq[m * 96 : m * 96 + 96, :]


def terms_body(
    place, late, *rest
):
    rings, tiles = rest[:8], rest[8]
    terms_o, both_s, pair_s, rhs_s, sums_s, all_s = rest[9:]
    lane = lax.broadcasted_iota(jnp.int32, (96, TOK), 1)
    gain = jnp.zeros((16, TOK), F32)
    zero = jnp.zeros((TOK, TOK), B16)
    for yl in range(2):
        before = jnp.zeros((96, TOK), F32)
        for band in range(4):
            m = yl * 4 + band
            block = late[m, :96, :]
            gain = gain + late[m, 160:176, :].astype(F32)
            moved = pltpu.roll(block.astype(F32), TC, 1)
            pair_s[m, :96, :] = block
            pair_s[m, 96:, :] = jnp.where(lane < TC, before, moved).astype(B16)
            before = moved
            rhs_s[m, :96, :TOK] = late[m, 272:, :]
            rhs_s[m, 96:128, :TOK] = late[m, 96:128, :]
            rhs_s[m, :128, TOK:] = zero
            rhs_s[m, 128:224, :TOK] = zero[:96]
            rhs_s[m, 128:224, TOK:] = late[m, 176:272, :]
            rhs_s[m, 224:, :TOK] = late[m, 128:160, :]
            rhs_s[m, 224:, TOK:] = zero[:32]
    rows = jnp.zeros((D, 256), F32)
    members = []
    for side in range(2):
        for back in range(4):
            chip = lax.rem(place[0] + 4 - back, 4)
            core = lax.rem(place[1] + side, 2)
            members.append(lax.rem(chip, 2) * 4 + lax.div(chip, 2) * 2 + core)
    for ring, m in zip(rings, members):
        rows = rows + dot(ring[...], rhs_s[m], NT)
    for half in range(2):
        sums_s[half] = rows[:, half * TOK : half * TOK + TOK]
        for i in range(24):
            picked = sums_s[half, pl.ds(i // 12 * 384 + i % 12, 32, stride=12), :]
            all_s[pl.ds(48 + half * 24 + i, 32, stride=104), :] = picked
    for i in range(8):
        row = gain[i : i + 1, :]
        all_s[pl.ds(96 + i, 32, stride=104), :] = jnp.broadcast_to(row, (32, TOK))
    for i, m in enumerate(members):
        both_s[:, i * TOK : i * TOK + TOK] = pair_s[m]
        tiles.piece(i)
    stem = dot(both_s[...], tiles[...])
    for c in range(8):
        for i in range(6):
            picked = stem[i * 32 : i * 32 + 32, c * TOK : c * TOK + TOK]
            all_s[pl.ds(i * 8 + c, 32, stride=104), :] = picked
    terms_o[...] = all_s[...].astype(B16)


def total_body(terms, stem_o, gain_o, rows_o):
    total = jnp.zeros((104, TOK), F32)
    for piece in range(8):
        block = terms.piece(piece)
        for r in range(4):
            total = total + block[r].astype(F32)
    for j in range(2):
        for k in range(3):
            for c in range(8):
                at = (j * 3 + k) * 8 + c
                stem_o[k, j : j + 1, c * TOK : c * TOK + TOK] = total[at : at + 1]
    for c in range(6):
        gain_o[:, c * TOK : c * TOK + TOK] = total[96 + c : 97 + c]
    for half in range(2):
        lanes = slice(half * TOK, half * TOK + TOK)
        for m in range(8):
            at = 48 + half * 24 + m * 3
            rows_o[m, :3, lanes] = total[at : at + 3]
            rows_o[m, 3:, lanes] = jnp.zeros((5, TOK), F32)


def final_body(rows, qkv_o, out_o):
    for first, last, to in ((0, 96, 0), (96, 128, D), (224, 256, D + 256)):
        width = last - first
        for m in range(8):
            qkv_o[:, to + m * width : to + m * width + width] = rows[m, :3, first:last]
    for m in range(8):
        out_o[:, m * 96 : m * 96 + 96] = rows[m, :3, 128:224]


def shards(patches, stem_weight, norm_gain, w_qkv, w_out, per_head_scale, positions, d_out):
    tiles = patches[0]
    grad_out = d_out[0]
    bands = lax.axis_size(BAND)
    arrived = lax.ppermute(tiles[:TC], BAND, [(i, i - 1) for i in range(1, bands)])
    tiles_mine = [along_ring(tiles, 1), None, along_ring(tiles, 3)]
    gain = norm_gain.reshape(1, D)
    tokens, hidden, key, kv_own = call(
        stem_body,
        [
            ((TOK, D), B16),
            ((TOK, D), B16),
            ((256, TOK), F32),
            ((KV, TOK), B16),
        ],
        pieces={1: 8, 3: 2},
        columns={3: (D, D + KV)},
    )(tiles, stem_weight.reshape(-1, D), arrived, w_qkv, gain)
    moved = [passed_along(kv_own, offset) for offset in range(1, 4)]
    moved[0], hidden = lax.optimization_barrier((moved[0], hidden))
    query, query_n, do, ring_own = call(
        query_body,
        [((D, TOK), F32), ((D, TOK), B16), ((D, TOK), B16), ((D, 2 * TOK), B16)],
        pieces={2: 2, 3: 2},
        columns={2: (0, D)},
    )(hidden, grad_out, w_qkv, w_out)
    query_n, tiles_late = lax.optimization_barrier((query_n, tiles_mine[0]))
    tiles_mine[1] = along_ring(tiles_late, 1)
    query_n, tiles_mine[0], tiles_mine[2] = lax.optimization_barrier(
        (query_n, tiles_mine[0], tiles_mine[2])
    )
    own_block = lax.axis_index(BLK).astype(jnp.int32).reshape(1)
    attn, d_q, own, back1, back2, back3 = call(
        attend_body,
        [((D, TOK), B16), ((D, TOK), F32), ((KV, TOK), F32)] + [((KV, TOK), B16)] * 3,
        smem=(0, 1),
    )(own_block, per_head_scale, positions.reshape(64, TOK), kv_own, *moved, query_n, do)
    returned = [passed_along(piece, -(j + 1)) for j, piece in enumerate((back1, back2, back3))]
    returned[0], d_q = lax.optimization_barrier((returned[0], d_q))
    d_q, part = call(
        part_body, [((D, TOK), B16), ((TOK, D), F32)], pieces={2: 2}, columns={2: (0, D)}
    )(d_q, query, w_qkv)
    ring_mine = [along_ring(ring_own, by) for by in (1, 2, 3)]
    ring_mine[0], ring_mine[2], tiles_mine[1], part = lax.optimization_barrier(
        (ring_mine[0], ring_mine[2], tiles_mine[1], part)
    )
    late = call(
        tokens_body,
        [((8, 368, TOK), B16)],
        scratch=[pltpu.VMEM((KV, TOK), B16), pltpu.VMEM((D, TOK), F32)],
        pieces={5: 2},
        columns={5: (D, D + KV)},
    )(own, *returned, key, w_qkv, tokens, gain, part, grad_out, attn, d_q)[0]
    late_ring = exchange(late, RING)
    rings = [ring_own, *ring_mine]
    blocks = [tiles, *tiles_mine]
    rings = rings + [other_core(x) for x in rings]
    blocks = blocks + [other_core(x) for x in blocks]
    chip = lax.axis_index("yh") * 2 + lax.axis_index("yl")
    place = jnp.stack([chip, lax.axis_index("c")]).astype(jnp.int32)
    terms = call(
        terms_body,
        [((32 * 104, TOK), B16)],
        scratch=[
            pltpu.VMEM((192, 1024), B16),
            pltpu.VMEM((8, 192, TOK), B16),
            pltpu.VMEM((8, 256, 256), B16),
            pltpu.VMEM((2, D, TOK), F32),
            pltpu.VMEM((32 * 104, TOK), F32),
        ],
        smem=(0,),
        joined=10,
    )(place, late_ring, *rings, *blocks)[0]
    stem_total, gain_total, row_total = call(
        total_body,
        [((3, 2, 1024), F32), ((1, D), F32), ((8, 8, 256), F32)],
        pieces={0: 8},
        limit=16,
    )(exchange(terms.reshape(32, 104, TOK), REST))
    d_w_qkv, d_w_out = call(final_body, [((3, 1280), F32), ((3, D), F32)], limit=16)(
        exchange(row_total, RING)
    )
    own_column = (lax.axis_index(BLK) * 4 + lax.axis_index(BAND)) * 3
    d_norm_gain = lax.dynamic_slice_in_dim(gain_total[0], own_column, 3)
    d_stem_weight = stem_total.transpose(1, 2, 0)
    return (d_stem_weight, d_norm_gain, d_w_qkv, d_w_out.T)


def solution(mesh):
    fine = Mesh(mesh.devices.reshape(2, 4, 8, 2, 2), BLK + BAND)
    placed = (P(BAND, BLK, None), P(), P(), P(), P(), P(), P(), P(BAND, BLK, None))
    every = BLK + BAND
    return jax.shard_map(
        shards,
        mesh=fine,
        in_specs=placed,
        out_specs=(P(None, None, every), P(every), P(every, None), P(None, every)),
        check_vma=False,
    )
```

```python
import jax
import jax.numpy as jnp
from jax import lax
from jax.experimental import pallas as pl
from jax.experimental.pallas import tpu as pltpu
from jax.sharding import Mesh, PartitionSpec as P

QUERY_HEADS = 12
KEY_VALUE_HEADS = 4
HEAD_SIZE = 64
TC = 16
D = 768
KV = 512
TOK = 128
BLK = ("yl", "x", "z")
BAND = ("yh", "c")
RING = ("yl", "yh", "c")
CHIPS = ("yl", "yh")
REST = ("x", "z")
F32 = jnp.float32
B16 = jnp.bfloat16
NN = (((1,), (0,)), ((), ()))
NT = (((1,), (1,)), ((), ()))
TN = (((0,), (0,)), ((), ()))


def dot(a, b, dims=NN):
    return lax.dot_general(a, b, dims, preferred_element_type=F32)


def passed_along(x, by):
    peers = lax.axis_size(BLK)
    return lax.ppermute(x, BLK, [(i, (i + by) % peers) for i in range(peers)])


def along_ring(x, by):
    order = [0, 2, 1, 3]
    return lax.ppermute(x, CHIPS, [(order[i], order[(i + by) % 4]) for i in range(4)])


def other_core(x):
    return lax.ppermute(x, "c", [(0, 1), (1, 0)])


def exchange(x, axes):
    return lax.all_to_all(x, axes, split_axis=0, concat_axis=0, tiled=True)


class Loaded:
    def __init__(self, ref, pieces):
        self.ref, self.pieces = ref, pieces

    def piece(self, i):
        copy, place = self.pieces[i]
        if copy is not None:
            copy.wait()
            self.pieces[i] = (None, place)
        return self.ref.at[place]

    def __getitem__(self, index):
        for i in range(len(self.pieces)):
            self.piece(i)
        return self.ref[index]


def split(shape, count):
    rows = shape[0] // count
    return [slice(i * rows, i * rows + rows) for i in range(count)]


def call(
    body, outs, scratch=(), smem=(), pieces=None, columns=None, joined=None, limit=64, flops=10**9
):
    pieces, columns = pieces or {}, columns or {}

    def run(*operands):
        held, parts, total = [], [], 0
        count = len(operands) if joined is None else joined
        if joined is not None:
            rows, width = operands[joined].shape
            held.append(pltpu.VMEM(((len(operands) - joined) * rows, width), operands[joined].dtype))
            total += len(operands) - joined
        for i, operand in enumerate(operands[:count]):
            if i in smem:
                continue
            shape = operand.shape
            if i in columns:
                shape = (shape[0], columns[i][1] - columns[i][0])
            held.append(pltpu.VMEM(shape, operand.dtype))
            parts.append((i, split(shape, pieces.get(i, 1))))
            total += pieces.get(i, 1)

        def kernel(*refs):
            inputs = list(refs[: len(operands)])
            others = refs[len(operands) : len(refs) - len(held) - 1]
            stores, sems = refs[len(refs) - len(held) - 1 : -1], refs[-1]
            used = 0
            if joined is not None:
                used, made = len(operands) - joined, []
                for i, place in enumerate(split(stores[0].shape, used)):
                    made.append(
                        (pltpu.make_async_copy(inputs[joined + i], stores[0].at[place], sems.at[i]), place)
                    )
                inputs[joined:] = [Loaded(stores[0], made)]
                stores = stores[1:]
            for (i, places), store in zip(parts, stores):
                source = inputs[i]
                if i in columns:
                    source = source.at[:, columns[i][0] : columns[i][1]]
                made = []
                for place in places:
                    copy = pltpu.make_async_copy(
                        source.at[place], store.at[place], sems.at[used]
                    )
                    copy.start()
                    made.append((copy, place))
                    used += 1
                inputs[i] = Loaded(store, made)
            if joined is not None:
                for copy, _ in inputs[joined].pieces:
                    copy.start()
            body(*inputs, *others)
            for value in inputs:
                if isinstance(value, Loaded):
                    for j in range(len(value.pieces)):
                        value.piece(j)

        shapes = [jax.ShapeDtypeStruct(shape, kind) for shape, kind in outs]
        return pl.pallas_call(
            kernel,
            out_shape=shapes,
            in_specs=[
                pl.BlockSpec(memory_space=pltpu.SMEM if i in smem else pl.ANY)
                for i in range(len(operands))
            ],
            out_specs=[pl.BlockSpec(memory_space=pltpu.VMEM)] * len(shapes),
            scratch_shapes=[*scratch, *held, pltpu.SemaphoreType.DMA((total,))],
            compiler_params=pltpu.CompilerParams(vmem_limit_bytes=limit * 2**20),
            cost_estimate=pl.CostEstimate(
                flops=flops, bytes_accessed=4 * 2**20, transcendentals=0
            ),
        )(*operands)

    return run


def stem_body(
    tiles, stem_w, arrived, w_kv, gain, tokens_o, hidden_o, key_o, kv_o
):
    own = tiles[...]
    deep = own.shape[1] // 4
    below = jnp.concatenate([own[TC:], arrived[...]], axis=0)
    stem = jnp.zeros((TOK, D), F32)
    for j, rows in enumerate((own, below)):
        for i in range(4):
            columns = rows[:, i * deep : i * deep + deep]
            stem = stem + dot(columns, stem_w.piece(4 * j + i)[...])
    low = stem.astype(B16)
    tokens_o[...] = low
    tok = low.astype(F32)
    factor = lax.rsqrt(jnp.mean(tok * tok, axis=1, keepdims=True) + 1e-05)
    hidden = (tok * factor * gain[...].astype(F32)).astype(B16)
    hidden_o[...] = hidden
    kv = dot(hidden, w_kv[...]).T
    key_o[...] = kv[:256]
    for h in range(KEY_VALUE_HEADS):
        k = kv[h * 64 : h * 64 + 64]
        scale = lax.rsqrt(jnp.mean(k * k, axis=0, keepdims=True) + 1e-06)
        kv_o[h * 64 : h * 64 + 64, :] = (k * scale).astype(B16)
    kv_o[256:, :] = kv[256:].astype(B16)


def query_body(hidden, d_out, w_q, w_out, query_o, query_n_o, do_o, ring_o):
    h = hidden[...]
    g = d_out[...]
    q = dot(h, w_q[...]).T
    query_o[...] = q
    for i in range(QUERY_HEADS):
        part = q[i * 64 : i * 64 + 64]
        scale = lax.rsqrt(jnp.mean(part * part, axis=0, keepdims=True) + 1e-06)
        query_n_o[i * 64 : i * 64 + 64, :] = (part * scale).astype(B16)
    do_o[...] = dot(w_out[...], g, NT).astype(B16)
    ring_o[:, :TOK] = h.astype(F32).T.astype(B16)
    ring_o[:, TOK:] = g.astype(F32).T.astype(B16)


def attend_body(
    own_block, scales, positions, kv0, kv1, kv2, kv3, query_n, do,
    attn_o, dq_o, own_o, back1_o, back2_o, back3_o,
):
    own = own_block[0]
    blocks = (kv0, kv1, kv2, kv3)
    positions[:8]
    rows = positions.ref
    q_pos = rows[pl.ds(own, 1), :]
    columns = []
    for j in range(4):
        row = rows[pl.ds(lax.rem(own - j + 64, 64), 1), :].astype(F32)
        columns.append(jnp.broadcast_to(row, (TOK, TOK)).T)
    key_pos = jnp.concatenate(columns, axis=0)
    bias = jnp.where(key_pos <= q_pos.astype(F32), 0.0, -1e30)
    bias = jnp.concatenate([bias] * 3, axis=1)
    for g in range(KEY_VALUE_HEADS):
        k = jnp.concatenate([b[g * 64 : g * 64 + 64, :] for b in blocks], axis=1)
        v = jnp.concatenate([b[256 + g * 64 : 320 + g * 64, :] for b in blocks], axis=1)
        heads = [3 * g + i for i in range(3)]
        q = jnp.concatenate([query_n[h * 64 : h * 64 + 64, :] for h in heads], axis=1)
        dy = jnp.concatenate([do[h * 64 : h * 64 + 64, :] for h in heads], axis=1)
        scale = jnp.concatenate([jnp.full((1, TOK), scales[h], F32) for h in heads], axis=1)
        scores = dot(k, q, TN) * scale + bias
        top = jnp.max(scores, axis=0, keepdims=True)
        weights = jnp.exp(scores - top)
        probs = weights * (1.0 / jnp.sum(weights, axis=0, keepdims=True))
        low = probs.astype(B16)
        attn = dot(v, low)
        delta = jnp.sum(dy.astype(F32) * attn, axis=0, keepdims=True)
        dprobs = dot(v, dy, TN)
        dscores = (scale * probs * (dprobs - delta)).astype(B16)
        dq = dot(k, dscores)
        dk = dot(q, dscores, NT)
        dv = dot(dy, low, NT)
        for i, h in enumerate(heads):
            rows = slice(h * 64, h * 64 + 64)
            lanes = slice(i * TOK, i * TOK + TOK)
            attn_o[rows, :] = attn[:, lanes].astype(B16)
            dq_o[rows, :] = dq[:, lanes]
        own_o[g * 64 : g * 64 + 64, :] = dk[:, :TOK]
        own_o[256 + g * 64 : 320 + g * 64, :] = dv[:, :TOK]
        for j, back in enumerate((back1_o, back2_o, back3_o)):
            lanes = slice((j + 1) * TOK, (j + 2) * TOK)
            back[g * 64 : g * 64 + 64, :] = dk[:, lanes].astype(B16)
            back[256 + g * 64 : 320 + g * 64, :] = dv[:, lanes].astype(B16)


def part_body(dq_n, query, w_q, dq_o, part_o):
    for h in range(QUERY_HEADS):
        rows = slice(h * 64, h * 64 + 64)
        x = query[rows, :]
        dx = dq_n[rows, :]
        r = lax.rsqrt(jnp.mean(x * x, axis=0, keepdims=True) + 1e-06)
        inner = jnp.mean(x * dx, axis=0, keepdims=True)
        dq_o[rows, :] = (r * dx - x * (r * r * r * inner)).astype(B16)
    part_o[...] = dot(w_q[...], dq_o[...]).T


def tokens_body(
    own, back1, back2, back3, key, w_kv, tokens, gain, part, d_out, attn, dq,
    late_o, dkv_s, tokens_s,
):
    total = own[...] + back1[...].astype(F32) + back2[...].astype(F32) + back3[...].astype(F32)
    for h in range(KEY_VALUE_HEADS):
        rows = slice(h * 64, h * 64 + 64)
        x = key[rows, :]
        dx = total[rows]
        r = lax.rsqrt(jnp.mean(x * x, axis=0, keepdims=True) + 1e-06)
        inner = jnp.mean(x * dx, axis=0, keepdims=True)
        dkv_s[rows, :] = (r * dx - x * (r * r * r * inner)).astype(B16)
    dkv_s[256:, :] = total[256:].astype(B16)
    d_hidden = part[...] + dot(w_kv[...], dkv_s[...]).T
    tok = tokens[...].astype(F32)
    r = lax.rsqrt(jnp.mean(tok * tok, axis=1, keepdims=True) + 1e-05)
    gain_term = jnp.sum(d_hidden * (tok * r), axis=0, keepdims=True)
    dx = d_hidden * gain[...].astype(F32)
    inner = jnp.mean(tok * dx, axis=1, keepdims=True)
    tokens_s[...] = (d_out[...].astype(F32) + (r * dx - tok * (r * r * r * inner))).T
    gains = jnp.concatenate(
        [gain_term[:, i * TOK : i * TOK + TOK] for i in range(6)] + [jnp.zeros((10, TOK), F32)],
        axis=0,
    ).astype(B16)
    for m in range(8):
        for k in range(3):
            picked = tokens_s[pl.ds(m // 4 * 384 + m % 4 * 3 + k, 32, stride=12), :]
            late_o[m, k * 32 : k * 32 + 32, :] = picked.astype(B16)
        late_o[m, 96:128, :] = dkv_s[m * 32 : m * 32 + 32, :]
        late_o[m, 128:160, :] = dkv_s[256 + m * 32 : 288 + m * 32, :]
        late_o[m, 160:176, :] = gains
        late_o[m, 176:272, :] = attn[m * 96 : m * 96 + 96, :]
        late_o[m, 272:, :] = dq[m * 96 : m * 96 + 96, :]


def terms_body(
    place, late, *rest
):
    rings, tiles = rest[:8], rest[8]
    terms_o, both_s, pair_s, rhs_s, sums_s, all_s = rest[9:]
    lane = lax.broadcasted_iota(jnp.int32, (96, TOK), 1)
    gain = jnp.zeros((16, TOK), F32)
    zero = jnp.zeros((TOK, TOK), B16)
    for yl in range(2):
        before = jnp.zeros((96, TOK), F32)
        for band in range(4):
            m = yl * 4 + band
            block = late[m, :96, :]
            gain = gain + late[m, 160:176, :].astype(F32)
            moved = pltpu.roll(block.astype(F32), TC, 1)
            pair_s[m, :96, :] = block
            pair_s[m, 96:, :] = jnp.where(lane < TC, before, moved).astype(B16)
            before = moved
            rhs_s[m, :96, :TOK] = late[m, 272:, :]
            rhs_s[m, 96:128, :TOK] = late[m, 96:128, :]
            rhs_s[m, :128, TOK:] = zero
            rhs_s[m, 128:224, :TOK] = zero[:96]
            rhs_s[m, 128:224, TOK:] = late[m, 176:272, :]
            rhs_s[m, 224:, :TOK] = late[m, 128:160, :]
            rhs_s[m, 224:, TOK:] = zero[:32]
    rows = jnp.zeros((D, 256), F32)
    members = []
    for side in range(2):
        for back in range(4):
            chip = lax.rem(place[0] + 4 - back, 4)
            core = lax.rem(place[1] + side, 2)
            members.append(lax.rem(chip, 2) * 4 + lax.div(chip, 2) * 2 + core)
    for ring, m in zip(rings, members):
        rows = rows + dot(ring[...], rhs_s[m], NT)
    for half in range(2):
        sums_s[half] = rows[:, half * TOK : half * TOK + TOK]
        for i in range(24):
            picked = sums_s[half, pl.ds(i // 12 * 384 + i % 12, 32, stride=12), :]
            all_s[pl.ds(48 + half * 24 + i, 32, stride=104), :] = picked
    for i in range(8):
        row = gain[i : i + 1, :]
        all_s[pl.ds(96 + i, 32, stride=104), :] = jnp.broadcast_to(row, (32, TOK))
    for i, m in enumerate(members):
        both_s[:, i * TOK : i * TOK + TOK] = pair_s[m]
        tiles.piece(i)
    stem = dot(both_s[...], tiles[...])
    for c in range(8):
        for i in range(6):
            picked = stem[i * 32 : i * 32 + 32, c * TOK : c * TOK + TOK]
            all_s[pl.ds(i * 8 + c, 32, stride=104), :] = picked
    terms_o[...] = all_s[...].astype(B16)


def total_body(terms, stem_o, gain_o, rows_o):
    total = jnp.zeros((104, TOK), F32)
    for piece in range(8):
        block = terms.piece(piece)
        for r in range(4):
            total = total + block[r].astype(F32)
    for j in range(2):
        for k in range(3):
            for c in range(8):
                at = (j * 3 + k) * 8 + c
                stem_o[k, j : j + 1, c * TOK : c * TOK + TOK] = total[at : at + 1]
    for c in range(6):
        gain_o[:, c * TOK : c * TOK + TOK] = total[96 + c : 97 + c]
    for half in range(2):
        lanes = slice(half * TOK, half * TOK + TOK)
        for m in range(8):
            at = 48 + half * 24 + m * 3
            rows_o[m, :3, lanes] = total[at : at + 3]
            rows_o[m, 3:, lanes] = jnp.zeros((5, TOK), F32)


def final_body(rows, qkv_o, out_o):
    for first, last, to in ((0, 96, 0), (96, 128, D), (224, 256, D + 256)):
        width = last - first
        for m in range(8):
            qkv_o[:, to + m * width : to + m * width + width] = rows[m, :3, first:last]
    for m in range(8):
        out_o[:, m * 96 : m * 96 + 96] = rows[m, :3, 128:224]


def shards(patches, stem_weight, norm_gain, w_qkv, w_out, per_head_scale, positions, d_out):
    tiles = patches[0]
    grad_out = d_out[0]
    bands = lax.axis_size(BAND)
    arrived = lax.ppermute(tiles[:TC], BAND, [(i, i - 1) for i in range(1, bands)])
    tiles_mine = [along_ring(tiles, 1), None, along_ring(tiles, 3)]
    gain = norm_gain.reshape(1, D)
    tokens, hidden, key, kv_own = call(
        stem_body,
        [
            ((TOK, D), B16),
            ((TOK, D), B16),
            ((256, TOK), F32),
            ((KV, TOK), B16),
        ],
        pieces={1: 8, 3: 2},
        columns={3: (D, D + KV)},
    )(tiles, stem_weight.reshape(-1, D), arrived, w_qkv, gain)
    moved = [passed_along(kv_own, offset) for offset in range(1, 4)]
    moved[0], hidden = lax.optimization_barrier((moved[0], hidden))
    query, query_n, do, ring_own = call(
        query_body,
        [((D, TOK), F32), ((D, TOK), B16), ((D, TOK), B16), ((D, 2 * TOK), B16)],
        pieces={2: 2, 3: 2},
        columns={2: (0, D)},
    )(hidden, grad_out, w_qkv, w_out)
    query_n, tiles_late = lax.optimization_barrier((query_n, tiles_mine[0]))
    tiles_mine[1] = along_ring(tiles_late, 1)
    query_n, tiles_mine[0], tiles_mine[2] = lax.optimization_barrier(
        (query_n, tiles_mine[0], tiles_mine[2])
    )
    own_block = lax.axis_index(BLK).astype(jnp.int32).reshape(1)
    attn, d_q, own, back1, back2, back3 = call(
        attend_body,
        [((D, TOK), B16), ((D, TOK), F32), ((KV, TOK), F32)] + [((KV, TOK), B16)] * 3,
        smem=(0, 1),
    )(own_block, per_head_scale, positions.reshape(64, TOK), kv_own, *moved, query_n, do)
    returned = [passed_along(piece, -(j + 1)) for j, piece in enumerate((back1, back2, back3))]
    returned[0], d_q = lax.optimization_barrier((returned[0], d_q))
    d_q, part = call(
        part_body, [((D, TOK), B16), ((TOK, D), F32)], pieces={2: 2}, columns={2: (0, D)}
    )(d_q, query, w_qkv)
    ring_mine = [along_ring(ring_own, by) for by in (1, 2, 3)]
    ring_mine[0], ring_mine[2], tiles_mine[1], part = lax.optimization_barrier(
        (ring_mine[0], ring_mine[2], tiles_mine[1], part)
    )
    late = call(
        tokens_body,
        [((8, 368, TOK), B16)],
        scratch=[pltpu.VMEM((KV, TOK), B16), pltpu.VMEM((D, TOK), F32)],
        pieces={5: 2},
        columns={5: (D, D + KV)},
    )(own, *returned, key, w_qkv, tokens, gain, part, grad_out, attn, d_q)[0]
    late_ring = exchange(late, RING)
    rings = [ring_own, *ring_mine]
    blocks = [tiles, *tiles_mine]
    rings = rings + [other_core(x) for x in rings]
    blocks = blocks + [other_core(x) for x in blocks]
    chip = lax.axis_index("yh") * 2 + lax.axis_index("yl")
    place = jnp.stack([chip, lax.axis_index("c")]).astype(jnp.int32)
    terms = call(
        terms_body,
        [((32 * 104, TOK), B16)],
        scratch=[
            pltpu.VMEM((192, 1024), B16),
            pltpu.VMEM((8, 192, TOK), B16),
            pltpu.VMEM((8, 256, 256), B16),
            pltpu.VMEM((2, D, TOK), F32),
            pltpu.VMEM((32 * 104, TOK), F32),
        ],
        smem=(0,),
        joined=10,
        pieces={1: 4},
    )(place, late_ring, *rings, *blocks)[0]
    stem_total, gain_total, row_total = call(
        total_body,
        [((3, 2, 1024), F32), ((1, D), F32), ((8, 8, 256), F32)],
        pieces={0: 8},
        limit=16,
    )(exchange(terms.reshape(32, 104, TOK), REST))
    d_w_qkv, d_w_out = call(final_body, [((3, 1280), F32), ((3, D), F32)], limit=16)(
        exchange(row_total, RING)
    )
    own_column = (lax.axis_index(BLK) * 4 + lax.axis_index(BAND)) * 3
    d_norm_gain = lax.dynamic_slice_in_dim(gain_total[0], own_column, 3)
    d_stem_weight = stem_total.transpose(1, 2, 0)
    return (d_stem_weight, d_norm_gain, d_w_qkv, d_w_out.T)


def solution(mesh):
    fine = Mesh(mesh.devices.reshape(2, 4, 8, 2, 2), BLK + BAND)
    placed = (P(BAND, BLK, None), P(), P(), P(), P(), P(), P(), P(BAND, BLK, None))
    every = BLK + BAND
    return jax.shard_map(
        shards,
        mesh=fine,
        in_specs=placed,
        out_specs=(P(None, None, every), P(every), P(every, None), P(None, every)),
        check_vma=False,
    )
```
